32 devices in a mesh: grp: 4 (over z), sp: 8 (over y, x, core).
Axes of the slice: x: 2, y: 2, z: 4, core: 2. Of those that a mesh axis runs over, the one named last changes fastest.
Arguments:
- q_src: bfloat16 [128, 4, 8, 4096], P(None, 'grp', 'sp'), may hold values from -4.5 to 4.5
- k_src: bfloat16 [128, 4, 8, 1024], P(None, 'grp', 'sp'), may hold values from -4.5 to 4.5
- v_src: bfloat16 [128, 4, 8, 1024], P(None, 'grp', 'sp'), may hold values from -4.5 to 4.5
- grad_src: bfloat16 [128, 4, 8, 4096], P(None, 'grp', 'sp'), may hold values from -4.5 to 4.5
- doc_lengths: int32 [192], replicated, may hold values from 0 to 5, as said below
- doc_groups: int32 [192], replicated, may hold values from 0 to 3, as said below
- doc_offsets: int32 [192], replicated, may hold values from 0 to 47, as said below
Outputs:
- dq_grp: bfloat16 [4, 192, 8, 4096], P('grp', None, 'sp')
- dk_grp: bfloat16 [4, 192, 8, 1024], P('grp', None, 'sp')
- dv_grp: bfloat16 [4, 192, 8, 1024], P('grp', None, 'sp')
The draws below stay inside these ranges and needn't reach their ends.
Inputs may be any that keep to these rules, and one draw needn't show every extreme that they name: `doc_lengths`: documents of positive length come first, absent ones (length 0) last; the lengths sum to 128 and one document has exactly 5 blocks. `doc_groups`: placed at their offsets, the documents of a group cover its blocks 0 up to its total without gaps or intersection; every group receives at least one block, none more than 48, and one group exactly 48. Absent documents name group 0. `doc_offsets`: absent documents have offset 0.
All inputs are finite; a program needn't handle non-finite values.
Results may differ from the reference program's by a relative error of at most 0.0091.
Values may be sent and summed in bfloat16 or wider, within the bound.
A program may use at most 64 MiB of HBM per device.

```python
import jax
import jax.numpy as jnp
from jax import lax

HEADS = 32
KV_HEADS = 8
HEAD_DIM = 128
TOK_DEV = 128
MAXDOC = 5
CAP = 48
UNIT = 32
GROUP_ROWS = 192
GROUP_TOK = 1536
N_GRP = 4
N_SP = 8


def draw_q_src(key, part):
    key = jax.random.fold_in(key, 12)
    full_shape = (TOK_DEV, N_GRP, N_SP, KV_HEADS, HEADS // KV_HEADS, HEAD_DIM)
    values = jnp.clip(jax.random.normal(key, full_shape, jnp.float32), -4.5, 4.5)
    return values.reshape(TOK_DEV, N_GRP, N_SP, HEADS * HEAD_DIM).astype(jnp.bfloat16)


def draw_k_src(key, part):
    key = jax.random.fold_in(key, 11)
    full_shape = (TOK_DEV, N_GRP, N_SP, KV_HEADS, HEAD_DIM)
    values = jnp.clip(jax.random.normal(key, full_shape, jnp.float32), -4.5, 4.5)
    return values.reshape(TOK_DEV, N_GRP, N_SP, KV_HEADS * HEAD_DIM).astype(jnp.bfloat16)


def plan_tables(key):
    key_move, key_amount, key_full, key_split, key_order = jax.random.split(key, 5)
    groups_idx = jnp.arange(N_GRP, dtype=jnp.int32)
    group_load = jnp.full((N_GRP,), TOK_DEV // N_GRP, jnp.int32) + (groups_idx < TOK_DEV % N_GRP).astype(jnp.int32)
    move_count = 4 * N_GRP
    move_pairs = jax.random.randint(key_move, (move_count, 2), 0, N_GRP)
    move_sizes = jax.random.randint(key_amount, (move_count,), 1, MAXDOC + 2)

    def shuffle_step(step_idx, group_load):
        to_group = move_pairs[step_idx, 0]
        from_group = move_pairs[step_idx, 1]
        amount = jnp.minimum(jnp.minimum(move_sizes[step_idx], CAP - group_load[to_group]), group_load[from_group] - 1)
        amount = jnp.where(to_group == from_group, 0, jnp.maximum(amount, 0))
        return group_load.at[to_group].add(amount).at[from_group].add(-amount)
    group_load = lax.fori_loop(0, move_count, shuffle_step, group_load)
    full_group = jax.random.randint(key_full, (), 0, N_GRP)

    def fill_step(group_id, carried):
        group_load, still_need = carried
        taken = jnp.where(group_id == full_group, 0, jnp.minimum(group_load[group_id] - 1, still_need))
        return (group_load.at[group_id].add(-taken), still_need - taken)
    group_load, still_need = lax.fori_loop(0, N_GRP, fill_step, (group_load, CAP - group_load[full_group]))
    group_load = group_load.at[full_group].set(CAP)
    unit_idx = jnp.arange(CAP, dtype=jnp.int32)
    new_flags = jax.random.randint(key_split, (N_GRP, CAP), 0, 2)
    is_full = (groups_idx == full_group)[:, None]
    new_flags = jnp.where(is_full & (unit_idx[None, :] >= 1) & (unit_idx[None, :] < MAXDOC), 0, new_flags)
    new_flags = jnp.where(is_full & (unit_idx[None, :] == CAP - 1), 1, new_flags)
    new_flags = new_flags.at[:, 0].set(1)

    def run_step(run_len, flag_col):
        begins = (flag_col == 1) | (run_len >= MAXDOC)
        return (jnp.where(begins, 1, run_len + 1), begins)
    unused, starts = lax.scan(run_step, jnp.full((N_GRP,), MAXDOC, jnp.int32), new_flags.T)
    starts = starts.T
    after_mask = (unit_idx[None, None, :] > unit_idx[None, :, None]) & starts[:, None, :]
    next_start = jnp.min(jnp.where(after_mask, unit_idx[None, None, :], CAP), axis=2)
    doc_ends = jnp.minimum(next_start, group_load[:, None])
    doc_real = starts & (unit_idx[None, :] < group_load[:, None])
    lengths = jnp.where(doc_real, doc_ends - unit_idx[None, :], 0).reshape(-1)
    sort_keys = jax.random.permutation(key_order, N_GRP * CAP).astype(jnp.int32) + N_GRP * CAP * (1 - doc_real.reshape(-1).astype(jnp.int32))
    pack_order = jnp.argsort(sort_keys)
    flat_len = lengths[pack_order].astype(jnp.int32)
    flat_grp = jnp.where(flat_len > 0, jnp.repeat(groups_idx, CAP)[pack_order], 0).astype(jnp.int32)
    flat_off = jnp.where(flat_len > 0, jnp.tile(unit_idx, N_GRP)[pack_order], 0).astype(jnp.int32)
    return (flat_len, flat_grp, flat_off)


def draw_doc_lengths(key, part):
    tables = plan_tables(key)
    return tables[0]


def draw_doc_groups(key, part):
    tables = plan_tables(key)
    return tables[1]


def draw_doc_offsets(key, part):
    tables = plan_tables(key)
    return tables[2]


def levels(rng, dims, shards, smallest, high):
    def one(dim, blocks):
        steps = jax.random.uniform(jax.random.fold_in(jax.random.fold_in(rng, 6), dim), (blocks,), jnp.float32, smallest / len(shards), high / len(shards))
        return jnp.repeat(jnp.exp(steps), dims[dim] // blocks).reshape((-1,) + (1,) * (len(dims) - dim - 1))

    gain = one(*shards[0])
    for cut in shards[1:]:
        gain = gain * one(*cut)
    return gain


def gaussian(key, dims, spread, bound, pieces=(), kind=jnp.bfloat16):
    values = spread * jax.random.normal(key, dims, jnp.float32)
    if pieces:
        values = values * levels(key, dims, pieces, -0.22, 0.18)
    return jnp.clip(values, -bound, bound).astype(kind)


def setup_inputs(seed: int = 0) -> dict:
    key_of = jax.random.split(jax.random.key(seed), 8)
    q_src = draw_q_src(jax.random.fold_in(key_of[7], 71), 0)
    k_src = draw_k_src(jax.random.fold_in(key_of[7], 71), 0)
    v_src = gaussian(key_of[2], (TOK_DEV, N_GRP, N_SP, KV_HEADS * HEAD_DIM), 1.0, 4.5, ((1, 4), (2, 8)))
    grad_src = gaussian(key_of[3], (TOK_DEV, N_GRP, N_SP, HEADS * HEAD_DIM), 1.0, 4.5, ((1, 4), (2, 8)))
    doc_lengths = draw_doc_lengths(jax.random.fold_in(key_of[7], 71), 0)
    doc_groups = draw_doc_groups(jax.random.fold_in(key_of[7], 71), 0)
    doc_offsets = draw_doc_offsets(jax.random.fold_in(key_of[7], 71), 0)
    return {"q_src": q_src, "k_src": k_src, "v_src": v_src, "grad_src": grad_src, "doc_lengths": doc_lengths, "doc_groups": doc_groups, "doc_offsets": doc_offsets}


NEG_FILL = -1.0e30


def unchanged(passed):
    return passed


def source_units(doc_lengths, doc_groups, doc_offsets):
    unit_ids = jnp.arange(TOK_DEV, dtype=jnp.int32)
    starts = (jnp.cumsum(doc_lengths) - doc_lengths).astype(jnp.int32)
    inside = ((unit_ids[:, None] >= starts[None, :]) & (unit_ids[:, None] < (starts + doc_lengths)[None, :])).astype(jnp.int32)
    group_of = jnp.sum(inside * doc_groups[None, :], axis=1).astype(jnp.int32)
    place_of = jnp.sum(inside * (doc_offsets[None, :] + unit_ids[:, None] - starts[None, :]), axis=1).astype(jnp.int32)
    slot_ids = jnp.arange(N_GRP * CAP, dtype=jnp.int32)
    matches = ((group_of * CAP + place_of)[None, :] == slot_ids[:, None]).astype(jnp.int32)
    source = jnp.sum(matches * unit_ids[None, :], axis=1).astype(jnp.int32).reshape(N_GRP, CAP)
    filled = (jnp.sum(matches, axis=1) > 0).reshape(N_GRP, CAP)
    return source, filled


def first_tokens(group_id, doc_lengths, doc_groups, doc_offsets):
    unit_place = jnp.arange(CAP, dtype=jnp.int32)
    member = ((doc_groups[None, :] == group_id) & (doc_lengths[None, :] > 0)
              & (doc_offsets[None, :] <= unit_place[:, None])
              & (unit_place[:, None] < (doc_offsets + doc_lengths)[None, :])).astype(jnp.int32)
    first_unit = jnp.sum(member * doc_offsets[None, :], axis=1).astype(jnp.int32)
    occupied = jnp.sum(member, axis=1) > 0
    token_ids = jnp.arange(GROUP_TOK, dtype=jnp.int32)
    return jnp.where(jnp.repeat(occupied, UNIT), jnp.repeat(first_unit * UNIT, UNIT), token_ids)


def attend_all(q_grp, k_grp, v_grp, g_grp, first_tok):
    span_len = UNIT
    blocks = CAP
    q_per_kv = HEADS // KV_HEADS
    factor = HEAD_DIM ** -0.5
    lane_pos = jnp.arange(span_len, dtype=jnp.int32)
    block_low = jnp.min(first_tok.reshape(blocks, span_len), axis=1)
    heads_shape = (KV_HEADS, q_per_kv, span_len)

    def cut_block(array, index):
        return lax.dynamic_slice_in_dim(array, (index * span_len).astype(jnp.int32), span_len, 0)

    def pair_logits(q_block, first_q, q_index, k_index):
        k_block = cut_block(k_grp, k_index).astype(jnp.float32)
        logits = jnp.einsum("qjih,kjh->jiqk", q_block, k_block) * factor
        q_pos = q_index * span_len + lane_pos
        k_pos = k_index * span_len + lane_pos
        allowed = (k_pos[None, :] <= q_pos[:, None]) & (k_pos[None, :] >= first_q[:, None])
        return logits, allowed

    def is_live(q_index, k_index):
        return block_low[q_index] <= k_index * span_len + span_len - 1

    def row_norm(q_index):
        q_block = cut_block(q_grp, q_index).astype(jnp.float32)
        first_q = cut_block(first_tok, q_index)

        def visit_key(k_index, running):
            def update(running):
                row_high, row_mass = running
                logits, allowed = pair_logits(q_block, first_q, q_index, k_index)
                logits = jnp.where(allowed, logits, NEG_FILL)
                new_high = jnp.maximum(row_high, jnp.max(logits, axis=-1))
                row_mass = row_mass * jnp.exp(row_high - new_high) + jnp.sum(
                    jnp.where(allowed, jnp.exp(logits - new_high[..., None]), 0.0), axis=-1)
                return new_high, row_mass
            return lax.cond(is_live(q_index, k_index), update, unchanged, running)

        initial = (jnp.full(heads_shape, NEG_FILL, jnp.float32), jnp.zeros(heads_shape, jnp.float32))
        row_high, row_mass = lax.fori_loop(0, q_index + 1, visit_key, initial)
        return row_high + jnp.log(row_mass)

    log_norm = lax.map(row_norm, jnp.arange(blocks, dtype=jnp.int32))

    def row_delta(q_index):
        q_block = cut_block(q_grp, q_index).astype(jnp.float32)
        first_q = cut_block(first_tok, q_index)
        norm_row = log_norm[q_index]

        def visit_key(k_index, acc_out):
            def update(acc_out):
                logits, allowed = pair_logits(q_block, first_q, q_index, k_index)
                weights = jnp.where(allowed, jnp.exp(logits - norm_row[..., None]), 0.0)
                weights = lax.optimization_barrier(weights.astype(jnp.bfloat16)).astype(jnp.float32)
                v_block = cut_block(v_grp, k_index).astype(jnp.float32)
                return acc_out + jnp.einsum("jiqk,kjh->jiqh", weights, v_block)
            return lax.cond(is_live(q_index, k_index), update, unchanged, acc_out)

        acc_out = lax.fori_loop(0, q_index + 1, visit_key, jnp.zeros(heads_shape + (HEAD_DIM,), jnp.float32))
        g_block = cut_block(g_grp, q_index).astype(jnp.float32)
        return jnp.einsum("jiqh,qjih->jiq", acc_out, g_block)

    delta_all = lax.map(row_delta, jnp.arange(blocks, dtype=jnp.int32))

    def back_row(q_index, carried):
        grad_q, grad_k, grad_v = carried
        q_block = cut_block(q_grp, q_index).astype(jnp.float32)
        g_block = cut_block(g_grp, q_index).astype(jnp.float32)
        first_q = cut_block(first_tok, q_index)
        norm_row = log_norm[q_index]
        delta_row = delta_all[q_index]

        def visit_key(k_index, inner):
            def update(inner):
                q_acc, grad_k, grad_v = inner
                logits, allowed = pair_logits(q_block, first_q, q_index, k_index)
                probs = jnp.where(allowed, jnp.exp(logits - norm_row[..., None]), 0.0)
                probs_low = lax.optimization_barrier(probs.astype(jnp.bfloat16)).astype(jnp.float32)
                k_block = cut_block(k_grp, k_index).astype(jnp.float32)
                v_block = cut_block(v_grp, k_index).astype(jnp.float32)
                d_probs = jnp.einsum("qjih,kjh->jiqk", g_block, v_block)
                d_logits = probs * (d_probs - delta_row[..., None])
                d_logits = lax.optimization_barrier(d_logits.astype(jnp.bfloat16)).astype(jnp.float32)
                q_acc = q_acc + jnp.einsum("jiqk,kjh->qjih", d_logits, k_block)
                k_part = jnp.einsum("jiqk,qjih->kjih", d_logits, q_block)
                v_part = jnp.einsum("jiqk,qjih->kjih", probs_low, g_block)
                at_row = (k_index * span_len).astype(jnp.int32)
                grad_k = lax.dynamic_update_slice_in_dim(grad_k, cut_block(grad_k, k_index) + k_part, at_row, 0)
                grad_v = lax.dynamic_update_slice_in_dim(grad_v, cut_block(grad_v, k_index) + v_part, at_row, 0)
                return q_acc, grad_k, grad_v
            return lax.cond(is_live(q_index, k_index), update, unchanged, inner)

        q_start = jnp.zeros((span_len, KV_HEADS, q_per_kv, HEAD_DIM), jnp.float32)
        q_acc, grad_k, grad_v = lax.fori_loop(0, q_index + 1, visit_key, (q_start, grad_k, grad_v))
        grad_q = lax.dynamic_update_slice_in_dim(grad_q, q_acc, (q_index * span_len).astype(jnp.int32), 0)
        return grad_q, grad_k, grad_v

    empty = jnp.zeros((GROUP_TOK, KV_HEADS, q_per_kv, HEAD_DIM), jnp.float32)
    grad_q, grad_k, grad_v = lax.fori_loop(0, blocks, back_row, (empty, empty, empty))
    return grad_q * factor, grad_k * factor, grad_v


def paired_total(grad_head):
    head_low = lax.optimization_barrier(grad_head.astype(jnp.bfloat16)).astype(jnp.float32)
    half = head_low.shape[2] // 2
    paired = head_low[:, :, :half] + head_low[:, :, half:]
    paired = lax.optimization_barrier(paired.astype(jnp.bfloat16)).astype(jnp.float32)
    return jnp.sum(paired, axis=2).astype(jnp.bfloat16)


def reference(q_src, k_src, v_src, grad_src, doc_lengths, doc_groups, doc_offsets):
    source, filled = source_units(doc_lengths, doc_groups, doc_offsets)
    q_per_kv = HEADS // KV_HEADS

    def one_group(group_id):
        picked = source[group_id]
        keep_mask = filled[group_id]

        def to_group(array, head_count):
            rows_now = jnp.take(array, picked, axis=0)
            rows_now = jnp.where(keep_mask[:, None, None, None], rows_now, jnp.zeros_like(rows_now))
            return rows_now.reshape(GROUP_TOK, head_count, HEAD_DIM)

        q_grp = to_group(q_src, HEADS).reshape(GROUP_TOK, KV_HEADS, q_per_kv, HEAD_DIM)
        g_grp = to_group(grad_src, HEADS).reshape(GROUP_TOK, KV_HEADS, q_per_kv, HEAD_DIM)
        k_grp = to_group(k_src, KV_HEADS)
        v_grp = to_group(v_src, KV_HEADS)
        first_tok = first_tokens(group_id, doc_lengths, doc_groups, doc_offsets)
        grad_q, grad_k, grad_v = attend_all(q_grp, k_grp, v_grp, g_grp, first_tok)
        out_q = grad_q.astype(jnp.bfloat16).reshape(GROUP_ROWS, N_SP, HEADS * HEAD_DIM)
        out_k = paired_total(grad_k).reshape(GROUP_ROWS, N_SP, KV_HEADS * HEAD_DIM)
        out_v = paired_total(grad_v).reshape(GROUP_ROWS, N_SP, KV_HEADS * HEAD_DIM)
        return out_q, out_k, out_v

    dq_all, dk_all, dv_all = lax.map(one_group, jnp.arange(N_GRP, dtype=jnp.int32))
    return (dq_all, dk_all, dv_all)
```

```python
import math

import jax
import jax.numpy as jnp
from jax import lax
from jax.experimental import pallas as pl
from jax.experimental.pallas import tpu as pltpu
from jax.sharding import PartitionSpec as P

HEADS = 32
KV_HEADS = 8
HEAD_DIM = 128


NEG_FILL = -1e30


def unchanged(passed):
    return passed


def collapse(array):
    rounded = lax.optimization_barrier(array)
    return jnp.sum(rounded.astype(jnp.float32), axis=2)


def pair_fold(low_part, high_part):
    return lax.optimization_barrier(
        (low_part.astype(jnp.float32) + high_part.astype(jnp.float32)).astype(jnp.bfloat16)
    )


def halves_total(array):
    half = array.shape[2] // 2
    return collapse(pair_fold(array[:, :, :half], array[:, :, half:]))


def attend(q_heads, k_heads, v_heads, g_heads, first_tok):
    tokens_here, kv_local, q_per_kv, head_dim = q_heads.shape
    span_len = math.gcd(tokens_here, 512)
    blocks = tokens_here // span_len
    factor = head_dim ** (-0.5)
    lane_pos = jnp.arange(span_len, dtype=jnp.int32)
    block_low = jnp.min(first_tok.reshape(blocks, span_len), axis=1)
    heads_shape = (kv_local, q_per_kv, span_len)

    def cut_block(array, index):
        return lax.dynamic_slice_in_dim(array, index * span_len, span_len, 0)

    def pair_logits(q_block, first_q, q_index, k_index):
        k_block = cut_block(k_heads, k_index)
        logits = (
            jnp.einsum("qjih,kjh->jiqk", q_block, k_block, preferred_element_type=jnp.float32)
            * factor
        )
        q_pos = q_index * span_len + lane_pos
        k_pos = k_index * span_len + lane_pos
        allowed = (k_pos[None, :] <= q_pos[:, None]) & (k_pos[None, :] >= first_q[:, None])
        return (logits, allowed)

    def is_live(q_index, k_index):
        return block_low[q_index] <= k_index * span_len + span_len - 1

    def row_norm(q_index):
        q_block = cut_block(q_heads, q_index)
        first_q = cut_block(first_tok, q_index)

        def visit_key(k_index, running):

            def update(running):
                row_high, row_mass = running
                logits, allowed = pair_logits(q_block, first_q, q_index, k_index)
                logits = jnp.where(allowed, logits, NEG_FILL)
                new_high = jnp.maximum(row_high, jnp.max(logits, axis=-1))
                row_mass = row_mass * jnp.exp(row_high - new_high) + jnp.sum(
                    jnp.where(allowed, jnp.exp(logits - new_high[..., None]), 0.0), axis=-1
                )
                return (new_high, row_mass)

            return lax.cond(is_live(q_index, k_index), update, unchanged, running)

        initial = (
            jnp.full(heads_shape, NEG_FILL, jnp.float32),
            jnp.zeros(heads_shape, jnp.float32),
        )
        row_high, row_mass = lax.fori_loop(0, q_index + 1, visit_key, initial)
        return row_high + jnp.log(row_mass)

    log_norm = lax.map(row_norm, jnp.arange(blocks, dtype=jnp.int32))

    def row_delta(q_index):
        q_block = cut_block(q_heads, q_index)
        first_q = cut_block(first_tok, q_index)
        norm_row = log_norm[q_index]

        def visit_key(k_index, acc_out):

            def update(acc_out):
                logits, allowed = pair_logits(q_block, first_q, q_index, k_index)
                weights = jnp.where(allowed, jnp.exp(logits - norm_row[..., None]), 0.0).astype(
                    jnp.bfloat16
                )
                v_block = cut_block(v_heads, k_index)
                return acc_out + jnp.einsum(
                    "jiqk,kjh->jiqh", weights, v_block, preferred_element_type=jnp.float32
                )

            return lax.cond(is_live(q_index, k_index), update, unchanged, acc_out)

        acc_out = lax.fori_loop(
            0, q_index + 1, visit_key, jnp.zeros(heads_shape + (head_dim,), jnp.float32)
        )
        g_block = cut_block(g_heads, q_index)
        return jnp.einsum("jiqh,qjih->jiq", acc_out, g_block, preferred_element_type=jnp.float32)

    delta_all = lax.map(row_delta, jnp.arange(blocks, dtype=jnp.int32))

    def back_row(q_index, carried):
        grad_q, grad_k, grad_v = carried
        q_block = cut_block(q_heads, q_index)
        g_block = cut_block(g_heads, q_index)
        first_q = cut_block(first_tok, q_index)
        norm_row = log_norm[q_index]
        delta_row = delta_all[q_index]

        def visit_key(k_index, inner):

            def update(inner):
                q_acc, grad_k, grad_v = inner
                logits, allowed = pair_logits(q_block, first_q, q_index, k_index)
                probs = jnp.where(allowed, jnp.exp(logits - norm_row[..., None]), 0.0)
                probs_low = probs.astype(jnp.bfloat16)
                k_block = cut_block(k_heads, k_index)
                v_block = cut_block(v_heads, k_index)
                d_probs = jnp.einsum(
                    "qjih,kjh->jiqk", g_block, v_block, preferred_element_type=jnp.float32
                )
                d_logits = (probs * (d_probs - delta_row[..., None])).astype(jnp.bfloat16)
                q_acc = q_acc + jnp.einsum(
                    "jiqk,kjh->qjih", d_logits, k_block, preferred_element_type=jnp.float32
                )
                k_part = jnp.einsum(
                    "jiqk,qjih->kjih", d_logits, q_block, preferred_element_type=jnp.float32
                )
                v_part = jnp.einsum(
                    "jiqk,qjih->kjih", probs_low, g_block, preferred_element_type=jnp.float32
                )
                at_row = k_index * span_len
                grad_k = lax.dynamic_update_slice_in_dim(
                    grad_k, cut_block(grad_k, k_index) + k_part, at_row, 0
                )
                grad_v = lax.dynamic_update_slice_in_dim(
                    grad_v, cut_block(grad_v, k_index) + v_part, at_row, 0
                )
                return (q_acc, grad_k, grad_v)

            return lax.cond(is_live(q_index, k_index), update, unchanged, inner)

        q_start = jnp.zeros((span_len, kv_local, q_per_kv, head_dim), jnp.float32)
        q_acc, grad_k, grad_v = lax.fori_loop(0, q_index + 1, visit_key, (q_start, grad_k, grad_v))
        grad_q = lax.dynamic_update_slice_in_dim(grad_q, q_acc, q_index * span_len, 0)
        return (grad_q, grad_k, grad_v)

    empty = jnp.zeros((tokens_here, kv_local, q_per_kv, head_dim), jnp.float32)
    grad_q, grad_k, grad_v = lax.fori_loop(0, blocks, back_row, (empty, empty, empty))
    return (grad_q * factor, grad_k * factor, grad_v)


def on_device_wide(q_src, k_src, v_src, grad_src, doc_lengths, doc_groups, doc_offsets):
    grp_count = lax.axis_size("grp")
    sp_count = lax.axis_size("sp")
    unit_count = q_src.shape[0]
    slot_count = doc_lengths.shape[0]
    group_cap = slot_count // grp_count
    row_count = group_cap * grp_count
    unit_tok = grp_count * sp_count
    group_tok = row_count * sp_count
    head_dim = HEAD_DIM
    copies = max(1, sp_count // KV_HEADS)
    kv_local = max(1, KV_HEADS // sp_count)
    q_local = HEADS // sp_count
    q_per_kv = q_local // kv_local
    unit_ids = jnp.arange(unit_count, dtype=jnp.int32)
    starts = jnp.cumsum(doc_lengths) - doc_lengths
    inside = (
        (unit_ids[:, None] >= starts[None, :])
        & (unit_ids[:, None] < (starts + doc_lengths)[None, :])
    ).astype(jnp.int32)
    group_of = jnp.sum(inside * doc_groups[None, :], axis=1)
    place_of = jnp.sum(
        inside * (doc_offsets[None, :] + unit_ids[:, None] - starts[None, :]), axis=1
    )
    slot_of = group_of * group_cap + place_of
    slot_ids = jnp.arange(row_count, dtype=jnp.int32).reshape(grp_count, group_cap).T.reshape(-1)
    matches = (slot_of[None, :] == slot_ids[:, None]).astype(jnp.int32)
    source = jnp.sum(matches * unit_ids[None, :], axis=1)
    filled = jnp.sum(matches, axis=1) > 0

    def pack_rows(array):
        flat = array.reshape(unit_count, array.shape[-1])
        picked = jnp.take(flat, source, axis=0)
        picked = jnp.where(filled[:, None], picked, jnp.zeros_like(picked))
        return picked.reshape(group_cap, grp_count, array.shape[-1])

    arrived = (
        lax.all_to_all(pack_rows(q_src), "grp", split_axis=1, concat_axis=1, tiled=True),
        lax.all_to_all(pack_rows(k_src), "grp", split_axis=1, concat_axis=1, tiled=True),
        lax.all_to_all(pack_rows(v_src), "grp", split_axis=1, concat_axis=1, tiled=True),
        lax.all_to_all(pack_rows(grad_src), "grp", split_axis=1, concat_axis=1, tiled=True),
    )
    q_rows = arrived[0].reshape(row_count, 1, HEADS, head_dim)
    k_rows = arrived[1].reshape(row_count, KV_HEADS, head_dim)
    v_rows = arrived[2].reshape(row_count, KV_HEADS, head_dim)
    g_rows = arrived[3].reshape(row_count, 1, HEADS, head_dim)
    my_group = lax.axis_index("grp")
    unit_place = jnp.arange(group_cap, dtype=jnp.int32)
    member = (
        (doc_groups[None, :] == my_group)
        & (doc_lengths[None, :] > 0)
        & (doc_offsets[None, :] <= unit_place[:, None])
        & (unit_place[:, None] < (doc_offsets + doc_lengths)[None, :])
    ).astype(jnp.int32)
    first_unit = jnp.sum(member * doc_offsets[None, :], axis=1)
    occupied = jnp.sum(member, axis=1) > 0
    token_ids = jnp.arange(group_tok, dtype=jnp.int32)
    first_tok = jnp.where(
        jnp.repeat(occupied, unit_tok), jnp.repeat(first_unit * unit_tok, unit_tok), token_ids
    )
    k_wide = jnp.repeat(k_rows, copies, axis=1).reshape(row_count, 1, KV_HEADS * copies, head_dim)
    v_wide = jnp.repeat(v_rows, copies, axis=1).reshape(row_count, 1, KV_HEADS * copies, head_dim)
    q_back, g_back, k_back, v_back = (
        lax.all_to_all(q_rows, "sp", split_axis=2, concat_axis=1, tiled=True),
        lax.all_to_all(g_rows, "sp", split_axis=2, concat_axis=1, tiled=True),
        lax.all_to_all(k_wide, "sp", split_axis=2, concat_axis=1, tiled=True),
        lax.all_to_all(v_wide, "sp", split_axis=2, concat_axis=1, tiled=True),
    )
    k_heads = k_back.reshape(group_tok, kv_local, head_dim)
    v_heads = v_back.reshape(group_tok, kv_local, head_dim)
    q_heads = q_back.reshape(group_tok, kv_local, q_per_kv, head_dim)
    g_heads = g_back.reshape(group_tok, kv_local, q_per_kv, head_dim)
    grad_q, grad_k, grad_v = attend(q_heads, k_heads, v_heads, g_heads, first_tok)
    q_low = grad_q.astype(jnp.bfloat16).reshape(row_count, sp_count, q_local, head_dim)
    k_low = grad_k.astype(jnp.bfloat16)
    v_low = grad_v.astype(jnp.bfloat16)
    q_home, k_home, v_home = (
        lax.all_to_all(q_low, "sp", split_axis=1, concat_axis=2, tiled=True),
        lax.all_to_all(
            k_low.reshape(row_count, sp_count, q_local, head_dim),
            "sp",
            split_axis=1,
            concat_axis=2,
            tiled=True,
        ),
        lax.all_to_all(
            v_low.reshape(row_count, sp_count, q_local, head_dim),
            "sp",
            split_axis=1,
            concat_axis=2,
            tiled=True,
        ),
    )
    k_sum = halves_total(k_home.reshape(row_count, KV_HEADS, HEADS // KV_HEADS, head_dim))
    v_sum = halves_total(v_home.reshape(row_count, KV_HEADS, HEADS // KV_HEADS, head_dim))
    dk_out = k_sum.astype(jnp.bfloat16).reshape(1, row_count, 1, KV_HEADS * head_dim)
    dv_out = v_sum.astype(jnp.bfloat16).reshape(1, row_count, 1, KV_HEADS * head_dim)
    dq_out = q_home.reshape(1, row_count, 1, HEADS * head_dim)
    return (dq_out, dk_out, dv_out)


MESH = pl.DeviceIdType.MESH
STEP = 16
F32 = jnp.float32
BF16 = jnp.bfloat16


def dot_nt(left, right):
    return lax.dot_general(left, right, (((1,), (1,)), ((), ())), preferred_element_type=F32)


def dot_nn(left, right):
    return lax.dot_general(left, right, (((1,), (0,)), ((), ())), preferred_element_type=F32)


def fused_kernel(
    n_grp,
    n_sp,
    tiles,
    q_ref,
    k_ref,
    v_ref,
    g_ref,
    hot_ref,
    first_ref,
    dq_ref,
    dk_ref,
    dv_ref,
    send,
    recv,
    home_q,
    home_kv,
    back_q,
    back_kv,
    bias,
    k_turned,
    dk_acc,
    dv_acc,
    send_sem,
    recv_sem,
    own_sem,
    hq_send,
    hq_recv,
    hkv_send,
    hkv_recv,
    hown_sem,
):
    my_grp = lax.axis_index("grp")
    my_sp = lax.axis_index("sp")
    peers = n_grp * n_sp
    me = my_grp * n_sp + my_sp
    q_wide = q_ref.shape[1] // n_sp
    kv_wide = k_ref.shape[1] // n_sp
    heads = q_wide // kv_wide
    tile_tok = peers * STEP
    factor = HEAD_DIM ** (-0.5)

    barrier = pltpu.get_barrier_semaphore()

    @pl.loop(1, peers)
    def _(hop):
        there = {
            "grp": lax.rem(my_grp + hop // n_sp, n_grp),
            "sp": lax.rem(my_sp + lax.rem(hop, n_sp), n_sp),
        }
        pl.semaphore_signal(barrier, inc=1, device_id=there, device_id_type=MESH)

    def pack(tile):
        hot = hot_ref[tile]
        for to in range(n_sp):
            at = 0
            for ref, wide in ((q_ref, q_wide), (k_ref, kv_wide), (v_ref, kv_wide), (g_ref, q_wide)):
                part = dot_nn(hot, ref[:, to * wide : (to + 1) * wide]).astype(BF16)
                part = part.reshape(n_grp, STEP, wide)
                for grp in range(n_grp):
                    send[tile, grp * n_sp + to, :, at : at + wide] = part[grp]
                at += wide

    def scatter(tile):
        @pl.loop(1, peers)
        def _(hop):
            turned = lax.rem(hop + 2 * n_sp, peers)
            to_grp = lax.rem(my_grp + turned // n_sp, n_grp)
            to_sp = lax.rem(my_sp + lax.rem(turned, n_sp), n_sp)

            @pl.when(turned != 0)
            def _():
                pltpu.make_async_remote_copy(
                    src_ref=send.at[tile, to_grp * n_sp + to_sp],
                    dst_ref=recv.at[tile, me],
                    send_sem=send_sem.at[tile],
                    recv_sem=recv_sem.at[tile],
                    device_id={"grp": to_grp, "sp": to_sp},
                    device_id_type=MESH,
                ).start()

        turned_grp = lax.rem(my_grp + 2, n_grp)
        pltpu.make_async_remote_copy(
            src_ref=send.at[tile, turned_grp * n_sp + my_sp],
            dst_ref=recv.at[tile, me],
            send_sem=send_sem.at[tile],
            recv_sem=recv_sem.at[tile],
            device_id={"grp": turned_grp, "sp": my_sp},
            device_id_type=MESH,
        ).start()
        own = pltpu.make_async_copy(send.at[tile, me], recv.at[tile, me], own_sem.at[tile])
        own.start()
        return own

    own_copies = []
    pack(0)
    pl.semaphore_wait(barrier, peers - 1)
    for tile in range(tiles):
        if tile > 0:
            pack(tile)
        own_copies.append(scatter(tile))

    dk_acc[...] = jnp.zeros_like(dk_acc)
    dv_acc[...] = jnp.zeros_like(dv_acc)

    def go_home(here, back, sends, recvs, own_sem_ref):
        @pl.loop(1, n_sp)
        def _(hop):
            to_sp = lax.rem(my_sp + hop, n_sp)
            pltpu.make_async_remote_copy(
                src_ref=here.at[:, to_sp],
                dst_ref=back.at[:, my_sp],
                send_sem=sends,
                recv_sem=recvs,
                device_id={"grp": my_grp, "sp": to_sp},
                device_id_type=MESH,
            ).start()

        own = pltpu.make_async_copy(here.at[:, my_sp], back.at[:, my_sp], own_sem_ref)
        own.start()
        return own

    def kv_home(tile):
        shape = (n_grp, n_sp, STEP, HEAD_DIM)
        home_kv[tile, :, :, :, :HEAD_DIM] = (dk_acc[tile] * factor).astype(BF16).reshape(shape)
        home_kv[tile, :, :, :, HEAD_DIM:] = dv_acc[tile].astype(BF16).reshape(shape)
        return go_home(
            home_kv.at[tile], back_kv.at[tile], hkv_send.at[tile], hkv_recv.at[tile], hown_sem.at[1, tile]
        )

    def rows_of(tile, at):
        return recv[tile, :, :, at : at + HEAD_DIM].reshape(tile_tok, HEAD_DIM)

    k_at = q_wide
    v_at = q_wide + kv_wide
    g_at = q_wide + 2 * kv_wide
    home_own = []
    for tile in range(tiles):
        own_copies[tile].wait()
        pltpu.make_async_copy(
            recv.at[tile, pl.ds(0, peers - 1)], recv.at[tile, pl.ds(0, peers - 1)], recv_sem.at[tile]
        ).wait()
        key_tiles = [tile] if tile == 0 else [tile, tile - 1]
        lane = lax.broadcasted_iota(jnp.int32, (1, tile_tok), 1)
        row = lax.broadcasted_iota(jnp.int32, (tile_tok, 1), 0)
        q_pos = (tile * STEP + lax.rem(lane, STEP)) * peers + lane // STEP
        q_first = first_ref[tile : tile + 1, :]
        for n, key_tile in enumerate(key_tiles):
            k_pos = (key_tile * STEP + lax.rem(row, STEP)) * peers + row // STEP
            allowed = (k_pos <= q_pos) & (k_pos >= q_first)
            bias[n] = jnp.where(allowed, 0.0, NEG_FILL)
            k_turned[n] = rows_of(key_tile, k_at).astype(F32).T.astype(BF16)

        @pl.loop(0, heads)
        def _(head):
            at = pl.multiple_of(head * HEAD_DIM, HEAD_DIM)
            q_head = recv[tile, :, :, pl.ds(at, HEAD_DIM)].reshape(tile_tok, HEAD_DIM)
            g_head = recv[tile, :, :, pl.ds(at + g_at, HEAD_DIM)].reshape(tile_tok, HEAD_DIM)
            logits = [
                dot_nt(rows_of(key_tile, k_at), q_head) * factor + bias[n]
                for n, key_tile in enumerate(key_tiles)
            ]
            high = jnp.max(logits[0], axis=0, keepdims=True)
            for part in logits[1:]:
                high = jnp.maximum(high, jnp.max(part, axis=0, keepdims=True))
            probs = [jnp.exp(part - high) for part in logits]
            mass = sum(jnp.sum(part, axis=0, keepdims=True) for part in probs)
            scale = 1.0 / mass
            probs = [part * scale for part in probs]
            d_probs = [dot_nt(rows_of(key_tile, v_at), g_head) for key_tile in key_tiles]
            delta = sum(
                jnp.sum(part * d_part, axis=0, keepdims=True) for part, d_part in zip(probs, d_probs)
            )
            dq_turned = jnp.zeros((HEAD_DIM, tile_tok), F32)
            for n, key_tile in enumerate(key_tiles):
                d_logits = (probs[n] * (d_probs[n] - delta)).astype(BF16)
                dv_acc[key_tile] += dot_nn(probs[n].astype(BF16), g_head)
                dk_acc[key_tile] += dot_nn(d_logits, q_head)
                dq_turned += dot_nn(k_turned[n], d_logits)
            dq_head = (dq_turned * factor).T.astype(BF16)
            home_q[tile, :, :, :, pl.ds(at, HEAD_DIM)] = dq_head.reshape(n_grp, n_sp, STEP, HEAD_DIM)

        home_own.append(
            go_home(home_q.at[tile], back_q.at[tile], hq_send.at[tile], hq_recv.at[tile], hown_sem.at[0, tile])
        )
        if tile > 0:
            home_own.append(kv_home(tile - 1))
    home_own.append(kv_home(tiles - 1))

    out_rows = n_grp * STEP
    to_row = lax.broadcasted_iota(jnp.int32, (out_rows, out_rows), 0)
    from_row = lax.broadcasted_iota(jnp.int32, (out_rows, out_rows), 1)
    weave = (to_row == lax.rem(from_row, STEP) * n_grp + from_row // STEP).astype(BF16)
    for own in home_own:
        own.wait()
    for tile in range(tiles):
        rows = pl.ds(tile * out_rows, out_rows)
        arrived_q = back_q.at[tile, :, pl.ds(0, n_sp - 1)]
        pltpu.make_async_copy(arrived_q, arrived_q, hq_recv.at[tile]).wait()
        for sp in range(n_sp):
            part = back_q[tile, :, sp].reshape(out_rows, q_wide)
            dq_ref[rows, sp * q_wide : (sp + 1) * q_wide] = dot_nn(weave, part).astype(BF16)
    for tile in range(tiles):
        rows = pl.ds(tile * out_rows, out_rows)
        arrived_kv = back_kv.at[tile, :, pl.ds(0, n_sp - 1)]
        pltpu.make_async_copy(arrived_kv, arrived_kv, hkv_recv.at[tile]).wait()
        for sp in range(n_sp):
            part = back_kv[tile, :, sp].reshape(out_rows, 2 * kv_wide)
            both = dot_nn(weave, part).astype(BF16)
            dk_ref[rows, sp * kv_wide : (sp + 1) * kv_wide] = both[:, :kv_wide]
            dv_ref[rows, sp * kv_wide : (sp + 1) * kv_wide] = both[:, kv_wide:]
    for tile in range(tiles):
        sent = send.at[tile, pl.ds(0, peers - 1)]
        pltpu.make_async_copy(sent, sent, send_sem.at[tile]).wait()
        sent_q = home_q.at[tile, :, pl.ds(0, n_sp - 1)]
        pltpu.make_async_copy(sent_q, sent_q, hq_send.at[tile]).wait()
        sent_kv = home_kv.at[tile, :, pl.ds(0, n_sp - 1)]
        pltpu.make_async_copy(sent_kv, sent_kv, hkv_send.at[tile]).wait()


def on_device_fused(q_src, k_src, v_src, grad_src, doc_lengths, doc_groups, doc_offsets):
    n_grp = lax.axis_size("grp")
    n_sp = lax.axis_size("sp")
    units = q_src.shape[0]
    slots = doc_lengths.shape[0]
    cap = slots // n_grp
    tiles = cap // STEP
    peers = n_grp * n_sp
    q_all = q_src.shape[-1]
    kv_all = k_src.shape[-1]
    q_wide = q_all // n_sp
    kv_wide = kv_all // n_sp
    row_wide = 2 * (q_wide + kv_wide)
    tile_tok = peers * STEP

    starts = jnp.cumsum(doc_lengths) - doc_lengths
    unit_ids = jnp.arange(units, dtype=jnp.int32)
    inside = (unit_ids[:, None] >= starts[None, :]) & (
        unit_ids[:, None] < (starts + doc_lengths)[None, :]
    )
    slot_start = doc_groups * cap + doc_offsets - starts
    slot_of = jnp.sum(jnp.where(inside, slot_start[None, :], 0), axis=1) + unit_ids
    slot_ids = (
        jnp.arange(tiles, dtype=jnp.int32)[:, None, None] * STEP
        + jnp.arange(n_grp, dtype=jnp.int32)[None, :, None] * cap
        + jnp.arange(STEP, dtype=jnp.int32)[None, None, :]
    ).reshape(tiles, n_grp * STEP)
    hot = (slot_ids[:, :, None] == slot_of[None, None, :]).astype(BF16)

    my_group = lax.axis_index("grp")
    lane = jnp.arange(tile_tok, dtype=jnp.int32)
    block = jnp.arange(tiles, dtype=jnp.int32)[:, None] * STEP + (lane % STEP)[None, :]
    member = (
        (doc_groups == my_group)
        & (doc_lengths > 0)
        & (doc_offsets <= block[:, :, None])
        & (block[:, :, None] < doc_offsets + doc_lengths)
    )
    first_unit = jnp.sum(jnp.where(member, doc_offsets * peers, 0), axis=2)
    occupied = jnp.any(member, axis=2)
    first = jnp.where(occupied, first_unit, block * peers + (lane // STEP)[None, :])

    rows = cap * n_grp
    vmem = pl.BlockSpec(memory_space=pltpu.VMEM)
    dma = pltpu.SemaphoreType.DMA
    dq, dk, dv = pl.pallas_call(
        lambda *refs: fused_kernel(n_grp, n_sp, tiles, *refs),
        out_shape=(
            jax.ShapeDtypeStruct((rows, q_all), BF16),
            jax.ShapeDtypeStruct((rows, kv_all), BF16),
            jax.ShapeDtypeStruct((rows, kv_all), BF16),
        ),
        in_specs=[vmem] * 6,
        out_specs=(vmem,) * 3,
        scratch_shapes=[
            pltpu.VMEM((tiles, peers, STEP, row_wide), BF16),
            pltpu.VMEM((tiles, peers, STEP, row_wide), BF16),
            pltpu.VMEM((tiles, n_grp, n_sp, STEP, q_wide), BF16),
            pltpu.VMEM((tiles, n_grp, n_sp, STEP, 2 * kv_wide), BF16),
            pltpu.VMEM((tiles, n_grp, n_sp, STEP, q_wide), BF16),
            pltpu.VMEM((tiles, n_grp, n_sp, STEP, 2 * kv_wide), BF16),
            pltpu.VMEM((2, tile_tok, tile_tok), F32),
            pltpu.VMEM((2, HEAD_DIM, tile_tok), BF16),
            pltpu.VMEM((tiles, tile_tok, HEAD_DIM), F32),
            pltpu.VMEM((tiles, tile_tok, HEAD_DIM), F32),
            dma((tiles,)),
            dma((tiles,)),
            dma((tiles,)),
            dma((tiles,)),
            dma((tiles,)),
            dma((tiles,)),
            dma((tiles,)),
            dma((2, tiles)),
        ],
        compiler_params=pltpu.CompilerParams(
            collective_id=0, has_side_effects=True, vmem_limit_bytes=56 * 1024 * 1024
        ),
    )(
        q_src.reshape(units, q_all),
        k_src.reshape(units, kv_all),
        v_src.reshape(units, kv_all),
        grad_src.reshape(units, q_all),
        hot,
        first,
    )
    return (
        dq.reshape(1, rows, 1, q_all),
        dk.reshape(1, rows, 1, kv_all),
        dv.reshape(1, rows, 1, kv_all),
    )


def on_device(q_src, k_src, v_src, grad_src, doc_lengths, doc_groups, doc_offsets):
    n_grp = lax.axis_size("grp")
    cap = doc_lengths.shape[0] // n_grp
    fits = lax.axis_size("sp") == KV_HEADS and cap % STEP == 0
    chosen = on_device_fused if fits else on_device_wide
    return chosen(q_src, k_src, v_src, grad_src, doc_lengths, doc_groups, doc_offsets)


def solution(mesh):
    placed = (
        P(None, "grp", "sp", None),
        P(None, "grp", "sp", None),
        P(None, "grp", "sp", None),
        P(None, "grp", "sp", None),
        P(),
        P(),
        P(),
    )
    return jax.shard_map(
        on_device,
        mesh=mesh,
        in_specs=placed,
        out_specs=(
            P("grp", None, "sp", None),
            P("grp", None, "sp", None),
            P("grp", None, "sp", None),
        ),
        check_vma=False,
    )
```

```python
import math

import jax
import jax.numpy as jnp
from jax import lax
from jax.experimental import pallas as pl
from jax.experimental.pallas import tpu as pltpu
from jax.sharding import PartitionSpec as P

HEADS = 32
KV_HEADS = 8
HEAD_DIM = 128


NEG_FILL = -1e30


def unchanged(passed):
    return passed


def collapse(array):
    rounded = lax.optimization_barrier(array)
    return jnp.sum(rounded.astype(jnp.float32), axis=2)


def pair_fold(low_part, high_part):
    return lax.optimization_barrier(
        (low_part.astype(jnp.float32) + high_part.astype(jnp.float32)).astype(jnp.bfloat16)
    )


def halves_total(array):
    half = array.shape[2] // 2
    return collapse(pair_fold(array[:, :, :half], array[:, :, half:]))


def attend(q_heads, k_heads, v_heads, g_heads, first_tok):
    tokens_here, kv_local, q_per_kv, head_dim = q_heads.shape
    span_len = math.gcd(tokens_here, 512)
    blocks = tokens_here // span_len
    factor = head_dim ** (-0.5)
    lane_pos = jnp.arange(span_len, dtype=jnp.int32)
    block_low = jnp.min(first_tok.reshape(blocks, span_len), axis=1)
    heads_shape = (kv_local, q_per_kv, span_len)

    def cut_block(array, index):
        return lax.dynamic_slice_in_dim(array, index * span_len, span_len, 0)

    def pair_logits(q_block, first_q, q_index, k_index):
        k_block = cut_block(k_heads, k_index)
        logits = (
            jnp.einsum("qjih,kjh->jiqk", q_block, k_block, preferred_element_type=jnp.float32)
            * factor
        )
        q_pos = q_index * span_len + lane_pos
        k_pos = k_index * span_len + lane_pos
        allowed = (k_pos[None, :] <= q_pos[:, None]) & (k_pos[None, :] >= first_q[:, None])
        return (logits, allowed)

    def is_live(q_index, k_index):
        return block_low[q_index] <= k_index * span_len + span_len - 1

    def row_norm(q_index):
        q_block = cut_block(q_heads, q_index)
        first_q = cut_block(first_tok, q_index)

        def visit_key(k_index, running):

            def update(running):
                row_high, row_mass = running
                logits, allowed = pair_logits(q_block, first_q, q_index, k_index)
                logits = jnp.where(allowed, logits, NEG_FILL)
                new_high = jnp.maximum(row_high, jnp.max(logits, axis=-1))
                row_mass = row_mass * jnp.exp(row_high - new_high) + jnp.sum(
                    jnp.where(allowed, jnp.exp(logits - new_high[..., None]), 0.0), axis=-1
                )
                return (new_high, row_mass)

            return lax.cond(is_live(q_index, k_index), update, unchanged, running)

        initial = (
            jnp.full(heads_shape, NEG_FILL, jnp.float32),
            jnp.zeros(heads_shape, jnp.float32),
        )
        row_high, row_mass = lax.fori_loop(0, q_index + 1, visit_key, initial)
        return row_high + jnp.log(row_mass)

    log_norm = lax.map(row_norm, jnp.arange(blocks, dtype=jnp.int32))

    def row_delta(q_index):
        q_block = cut_block(q_heads, q_index)
        first_q = cut_block(first_tok, q_index)
        norm_row = log_norm[q_index]

        def visit_key(k_index, acc_out):

            def update(acc_out):
                logits, allowed = pair_logits(q_block, first_q, q_index, k_index)
                weights = jnp.where(allowed, jnp.exp(logits - norm_row[..., None]), 0.0).astype(
                    jnp.bfloat16
                )
                v_block = cut_block(v_heads, k_index)
                return acc_out + jnp.einsum(
                    "jiqk,kjh->jiqh", weights, v_block, preferred_element_type=jnp.float32
                )

            return lax.cond(is_live(q_index, k_index), update, unchanged, acc_out)

        acc_out = lax.fori_loop(
            0, q_index + 1, visit_key, jnp.zeros(heads_shape + (head_dim,), jnp.float32)
        )
        g_block = cut_block(g_heads, q_index)
        return jnp.einsum("jiqh,qjih->jiq", acc_out, g_block, preferred_element_type=jnp.float32)

    delta_all = lax.map(row_delta, jnp.arange(blocks, dtype=jnp.int32))

    def back_row(q_index, carried):
        grad_q, grad_k, grad_v = carried
        q_block = cut_block(q_heads, q_index)
        g_block = cut_block(g_heads, q_index)
        first_q = cut_block(first_tok, q_index)
        norm_row = log_norm[q_index]
        delta_row = delta_all[q_index]

        def visit_key(k_index, inner):

            def update(inner):
                q_acc, grad_k, grad_v = inner
                logits, allowed = pair_logits(q_block, first_q, q_index, k_index)
                probs = jnp.where(allowed, jnp.exp(logits - norm_row[..., None]), 0.0)
                probs_low = probs.astype(jnp.bfloat16)
                k_block = cut_block(k_heads, k_index)
                v_block = cut_block(v_heads, k_index)
                d_probs = jnp.einsum(
                    "qjih,kjh->jiqk", g_block, v_block, preferred_element_type=jnp.float32
                )
                d_logits = (probs * (d_probs - delta_row[..., None])).astype(jnp.bfloat16)
                q_acc = q_acc + jnp.einsum(
                    "jiqk,kjh->qjih", d_logits, k_block, preferred_element_type=jnp.float32
                )
                k_part = jnp.einsum(
                    "jiqk,qjih->kjih", d_logits, q_block, preferred_element_type=jnp.float32
                )
                v_part = jnp.einsum(
                    "jiqk,qjih->kjih", probs_low, g_block, preferred_element_type=jnp.float32
                )
                at_row = k_index * span_len
                grad_k = lax.dynamic_update_slice_in_dim(
                    grad_k, cut_block(grad_k, k_index) + k_part, at_row, 0
                )
                grad_v = lax.dynamic_update_slice_in_dim(
                    grad_v, cut_block(grad_v, k_index) + v_part, at_row, 0
                )
                return (q_acc, grad_k, grad_v)

            return lax.cond(is_live(q_index, k_index), update, unchanged, inner)

        q_start = jnp.zeros((span_len, kv_local, q_per_kv, head_dim), jnp.float32)
        q_acc, grad_k, grad_v = lax.fori_loop(0, q_index + 1, visit_key, (q_start, grad_k, grad_v))
        grad_q = lax.dynamic_update_slice_in_dim(grad_q, q_acc, q_index * span_len, 0)
        return (grad_q, grad_k, grad_v)

    empty = jnp.zeros((tokens_here, kv_local, q_per_kv, head_dim), jnp.float32)
    grad_q, grad_k, grad_v = lax.fori_loop(0, blocks, back_row, (empty, empty, empty))
    return (grad_q * factor, grad_k * factor, grad_v)


def on_device_wide(q_src, k_src, v_src, grad_src, doc_lengths, doc_groups, doc_offsets):
    grp_count = lax.axis_size("grp")
    sp_count = lax.axis_size("sp")
    unit_count = q_src.shape[0]
    slot_count = doc_lengths.shape[0]
    group_cap = slot_count // grp_count
    row_count = group_cap * grp_count
    unit_tok = grp_count * sp_count
    group_tok = row_count * sp_count
    head_dim = HEAD_DIM
    copies = max(1, sp_count // KV_HEADS)
    kv_local = max(1, KV_HEADS // sp_count)
    q_local = HEADS // sp_count
    q_per_kv = q_local // kv_local
    unit_ids = jnp.arange(unit_count, dtype=jnp.int32)
    starts = jnp.cumsum(doc_lengths) - doc_lengths
    inside = (
        (unit_ids[:, None] >= starts[None, :])
        & (unit_ids[:, None] < (starts + doc_lengths)[None, :])
    ).astype(jnp.int32)
    group_of = jnp.sum(inside * doc_groups[None, :], axis=1)
    place_of = jnp.sum(
        inside * (doc_offsets[None, :] + unit_ids[:, None] - starts[None, :]), axis=1
    )
    slot_of = group_of * group_cap + place_of
    slot_ids = jnp.arange(row_count, dtype=jnp.int32).reshape(grp_count, group_cap).T.reshape(-1)
    matches = (slot_of[None, :] == slot_ids[:, None]).astype(jnp.int32)
    source = jnp.sum(matches * unit_ids[None, :], axis=1)
    filled = jnp.sum(matches, axis=1) > 0

    def pack_rows(array):
        flat = array.reshape(unit_count, array.shape[-1])
        picked = jnp.take(flat, source, axis=0)
        picked = jnp.where(filled[:, None], picked, jnp.zeros_like(picked))
        return picked.reshape(group_cap, grp_count, array.shape[-1])

    arrived = (
        lax.all_to_all(pack_rows(q_src), "grp", split_axis=1, concat_axis=1, tiled=True),
        lax.all_to_all(pack_rows(k_src), "grp", split_axis=1, concat_axis=1, tiled=True),
        lax.all_to_all(pack_rows(v_src), "grp", split_axis=1, concat_axis=1, tiled=True),
        lax.all_to_all(pack_rows(grad_src), "grp", split_axis=1, concat_axis=1, tiled=True),
    )
    q_rows = arrived[0].reshape(row_count, 1, HEADS, head_dim)
    k_rows = arrived[1].reshape(row_count, KV_HEADS, head_dim)
    v_rows = arrived[2].reshape(row_count, KV_HEADS, head_dim)
    g_rows = arrived[3].reshape(row_count, 1, HEADS, head_dim)
    my_group = lax.axis_index("grp")
    unit_place = jnp.arange(group_cap, dtype=jnp.int32)
    member = (
        (doc_groups[None, :] == my_group)
        & (doc_lengths[None, :] > 0)
        & (doc_offsets[None, :] <= unit_place[:, None])
        & (unit_place[:, None] < (doc_offsets + doc_lengths)[None, :])
    ).astype(jnp.int32)
    first_unit = jnp.sum(member * doc_offsets[None, :], axis=1)
    occupied = jnp.sum(member, axis=1) > 0
    token_ids = jnp.arange(group_tok, dtype=jnp.int32)
    first_tok = jnp.where(
        jnp.repeat(occupied, unit_tok), jnp.repeat(first_unit * unit_tok, unit_tok), token_ids
    )
    k_wide = jnp.repeat(k_rows, copies, axis=1).reshape(row_count, 1, KV_HEADS * copies, head_dim)
    v_wide = jnp.repeat(v_rows, copies, axis=1).reshape(row_count, 1, KV_HEADS * copies, head_dim)
    q_back, g_back, k_back, v_back = (
        lax.all_to_all(q_rows, "sp", split_axis=2, concat_axis=1, tiled=True),
        lax.all_to_all(g_rows, "sp", split_axis=2, concat_axis=1, tiled=True),
        lax.all_to_all(k_wide, "sp", split_axis=2, concat_axis=1, tiled=True),
        lax.all_to_all(v_wide, "sp", split_axis=2, concat_axis=1, tiled=True),
    )
    k_heads = k_back.reshape(group_tok, kv_local, head_dim)
    v_heads = v_back.reshape(group_tok, kv_local, head_dim)
    q_heads = q_back.reshape(group_tok, kv_local, q_per_kv, head_dim)
    g_heads = g_back.reshape(group_tok, kv_local, q_per_kv, head_dim)
    grad_q, grad_k, grad_v = attend(q_heads, k_heads, v_heads, g_heads, first_tok)
    q_low = grad_q.astype(jnp.bfloat16).reshape(row_count, sp_count, q_local, head_dim)
    k_low = grad_k.astype(jnp.bfloat16)
    v_low = grad_v.astype(jnp.bfloat16)
    q_home, k_home, v_home = (
        lax.all_to_all(q_low, "sp", split_axis=1, concat_axis=2, tiled=True),
        lax.all_to_all(
            k_low.reshape(row_count, sp_count, q_local, head_dim),
            "sp",
            split_axis=1,
            concat_axis=2,
            tiled=True,
        ),
        lax.all_to_all(
            v_low.reshape(row_count, sp_count, q_local, head_dim),
            "sp",
            split_axis=1,
            concat_axis=2,
            tiled=True,
        ),
    )
    k_sum = halves_total(k_home.reshape(row_count, KV_HEADS, HEADS // KV_HEADS, head_dim))
    v_sum = halves_total(v_home.reshape(row_count, KV_HEADS, HEADS // KV_HEADS, head_dim))
    dk_out = k_sum.astype(jnp.bfloat16).reshape(1, row_count, 1, KV_HEADS * head_dim)
    dv_out = v_sum.astype(jnp.bfloat16).reshape(1, row_count, 1, KV_HEADS * head_dim)
    dq_out = q_home.reshape(1, row_count, 1, HEADS * head_dim)
    return (dq_out, dk_out, dv_out)


MESH = pl.DeviceIdType.MESH
STEP = 16
MAXDOC = 5
F32 = jnp.float32
BF16 = jnp.bfloat16


def dot_nt(left, right):
    return lax.dot_general(left, right, (((1,), (1,)), ((), ())), preferred_element_type=F32)


def dot_nn(left, right):
    return lax.dot_general(left, right, (((1,), (0,)), ((), ())), preferred_element_type=F32)


def lane_iota(rows, lanes):
    return lax.broadcasted_iota(jnp.int32, (rows, lanes), 1)


def row_iota(rows, lanes):
    return lax.broadcasted_iota(jnp.int32, (rows, lanes), 0)


def fused_kernel(
    n_grp,
    n_sp,
    tiles,
    q_ref,
    k_ref,
    v_ref,
    g_ref,
    len_ref,
    grp_ref,
    off_ref,
    back_q,
    back_kv,
    send,
    recv,
    home_q,
    home_kv,
    bias,
    halo_bias,
    halo_kv,
    k_turned,
    halo_turned,
    d_acc,
    halo_acc,
    send_sem,
    recv_sem,
    own_sem,
    hq_send,
    hq_recv,
    hq_own,
    hkv_send,
    hkv_recv,
    hkv_own,
):
    my_grp = lax.axis_index("grp")
    my_sp = lax.axis_index("sp")
    peers = n_grp * n_sp
    me = my_grp * n_sp + my_sp
    units = q_ref.shape[0]
    q_wide = q_ref.shape[1] // n_sp
    heads = q_wide // HEAD_DIM
    cap = tiles * STEP
    tile_tok = peers * STEP
    halo = MAXDOC - 1
    halo_tok = peers * halo
    factor = HEAD_DIM ** (-0.5)
    row_wide = 2 * HEAD_DIM * (heads + 1)
    last = tiles - 1
    kv_lanes = pl.ds(0, 2 * HEAD_DIM)

    barrier = pltpu.get_barrier_semaphore()

    @pl.loop(1, peers)
    def _(hop):
        there = {
            "grp": lax.rem(my_grp + hop // n_sp, n_grp),
            "sp": lax.rem(my_sp + lax.rem(hop, n_sp), n_sp),
        }
        pl.semaphore_signal(barrier, inc=1, device_id=there, device_id_type=MESH)

    slots = len_ref.shape[1]
    which = row_iota(8, slots)
    tables = jnp.where(
        which == 0, len_ref[...], jnp.where(which == 1, grp_ref[...], jnp.where(which == 2, off_ref[...], 0))
    )
    tables = tables.astype(F32).astype(BF16)
    down, across = row_iota(slots, slots), lane_iota(slots, slots)
    columns = dot_nt((down == across).astype(F32).astype(BF16), tables)
    length, group, offset = columns[:, 0:1], columns[:, 1:2], columns[:, 2:3]
    start = dot_nt((across < down).astype(F32).astype(BF16), tables)[:, 0:1]
    unit = lane_iota(1, units).astype(F32)
    inside = (unit >= start) & (unit < start + length)
    slot_of = unit + jnp.sum(
        jnp.where(inside, group * cap + offset - start, 0.0), axis=0, keepdims=True
    )

    def pack(tile):
        row = row_iota(n_grp * STEP, 1)
        slot = (row // STEP) * cap + tile * STEP + lax.rem(row, STEP)
        hot = (slot.astype(F32) == slot_of).astype(F32).astype(BF16)

        def put(to, at, ref, lane, wide):
            part = dot_nn(hot, ref[:, lane : lane + wide]).astype(BF16).reshape(n_grp, STEP, wide)
            for grp in range(n_grp):
                send[tile, grp * n_sp + to, :, at : at + wide] = part[grp]

        for to in range(n_sp):
            put(to, 0, k_ref, to * HEAD_DIM, HEAD_DIM)
            put(to, HEAD_DIM, v_ref, to * HEAD_DIM, HEAD_DIM)
            for head in range(heads):
                lane = to * q_wide + head * HEAD_DIM
                put(to, 2 * HEAD_DIM * (head + 1), q_ref, lane, HEAD_DIM)
                put(to, 2 * HEAD_DIM * (head + 1) + HEAD_DIM, g_ref, lane, HEAD_DIM)

    def scatter(tile, lane, wide, sem):
        lanes = pl.ds(lane, wide)

        def push(to_grp, to_sp):
            pltpu.make_async_remote_copy(
                src_ref=send.at[tile, to_grp * n_sp + to_sp, :, lanes],
                dst_ref=recv.at[tile, me, :, lanes],
                send_sem=send_sem.at[sem],
                recv_sem=recv_sem.at[sem],
                device_id={"grp": to_grp, "sp": to_sp},
                device_id_type=MESH,
            ).start()

        for turn in [n_grp // 2] + [t for t in range(1, n_grp) if t != n_grp // 2] + [0]:

            @pl.loop(1 if turn == 0 else 0, n_sp)
            def _(hop):
                push(lax.rem(my_grp + turn, n_grp), lax.rem(my_sp + hop, n_sp))

    def landed(tile, lane, wide, sem):
        block = recv.at[tile, pl.ds(0, peers - 1), :, pl.ds(lane, wide)]
        pltpu.make_async_copy(block, block, recv_sem.at[sem]).wait()

    def own_block(tile):
        return pltpu.make_async_copy(send.at[tile, me], recv.at[tile, me], own_sem.at[tile])

    pack(0)
    pl.semaphore_wait(barrier, peers - 1)
    for tile in range(last):
        if tile > 0:
            pack(tile)
        scatter(tile, 0, row_wide, tile)
    pack(last)
    pair = 2 * HEAD_DIM
    scatter(last, 0, 2 * pair, last)
    for head in range(1, heads):
        scatter(last, (head + 1) * pair, pair, last + head)
    for tile in range(tiles):
        own_block(tile).start()

    d_acc[...] = jnp.zeros_like(d_acc)

    def go_home(here, back, sends, recvs, own):
        @pl.loop(1, n_sp)
        def _(hop):
            to_sp = lax.rem(my_sp + hop, n_sp)
            pltpu.make_async_remote_copy(
                src_ref=here.at[:, to_sp],
                dst_ref=back.at[:, my_sp],
                send_sem=sends,
                recv_sem=recvs,
                device_id={"grp": my_grp, "sp": to_sp},
                device_id_type=MESH,
            ).start()

        pltpu.make_async_copy(here.at[:, my_sp], back.at[:, my_sp], own).start()

    def kv_home(tile):
        shape = (n_grp, n_sp, STEP, HEAD_DIM)
        home_kv[tile, :, :, :, :HEAD_DIM] = (
            (d_acc[tile, :, :HEAD_DIM] * factor).astype(BF16).reshape(shape)
        )
        home_kv[tile, :, :, :, HEAD_DIM:] = d_acc[tile, :, HEAD_DIM:].astype(BF16).reshape(shape)
        go_home(
            home_kv.at[tile], back_kv.at[tile], hkv_send.at[tile], hkv_recv.at[tile], hkv_own.at[tile]
        )

    halo_row = row_iota(halo_tok, 1)
    halo_from = (halo_row // halo) * STEP + STEP - halo + lax.rem(halo_row, halo)
    cut = (halo_from == lane_iota(1, tile_tok)).astype(F32).astype(BF16)
    row = row_iota(tile_tok, 1)
    halo_lane = lane_iota(1, halo_tok)
    paste = (
        row == (halo_lane // halo) * STEP + STEP - halo + lax.rem(halo_lane, halo)
    ).astype(F32)

    for tile in range(tiles):
        lane = lane_iota(1, tile_tok)
        q_block = tile * STEP + lax.rem(lane, STEP)
        q_pos = q_block * peers + lane // STEP
        place = q_block.astype(F32)
        member = (
            (group == my_grp.astype(F32))
            & (length > 0.0)
            & (offset <= place)
            & (place < offset + length)
        )
        first = jnp.sum(jnp.where(member, offset * peers, 0.0), axis=0, keepdims=True)
        occupied = jnp.sum(jnp.where(member, 1.0, 0.0), axis=0, keepdims=True) > 0.0
        first = jnp.where(occupied, first, q_pos.astype(F32)).astype(jnp.int32)
        k_pos = (tile * STEP + lax.rem(row, STEP)) * peers + row // STEP
        bias[...] = jnp.where((k_pos <= q_pos) & (k_pos >= first), 0.0, NEG_FILL)
        if tile > 0:
            halo_pos = (tile * STEP - halo + lax.rem(halo_row, halo)) * peers + halo_row // halo
            halo_bias[...] = jnp.where(halo_pos >= first, 0.0, NEG_FILL)
            kv_before = recv[tile - 1, :, :, : 2 * HEAD_DIM].reshape(tile_tok, 2 * HEAD_DIM)
            kv_cut = dot_nn(cut, kv_before)
            halo_kv[...] = kv_cut.astype(BF16)
            halo_turned[...] = kv_cut[:, :HEAD_DIM].T.astype(BF16)
            halo_acc[...] = jnp.zeros_like(halo_acc)

        own_block(tile).wait()
        landed(tile, 0, 2 * pair if tile == last else row_wide, tile)
        k_turned[...] = (
            recv[tile, :, :, :HEAD_DIM].reshape(tile_tok, HEAD_DIM).astype(F32).T.astype(BF16)
        )

        @pl.loop(0, heads)
        def _(head):
            if tile == last:

                @pl.when(head > 0)
                def _():
                    landed(last, pair, pair, last + head)

            at = pl.multiple_of(head * HEAD_DIM, HEAD_DIM)
            q_at = pl.multiple_of((head + 1) * pair, HEAD_DIM)
            g_at = pl.multiple_of((head + 1) * pair + HEAD_DIM, HEAD_DIM)
            q_head = recv[tile, :, :, pl.ds(q_at, HEAD_DIM)].reshape(tile_tok, HEAD_DIM)
            g_head = recv[tile, :, :, pl.ds(g_at, HEAD_DIM)].reshape(tile_tok, HEAD_DIM)
            keys = [recv[tile, :, :, :HEAD_DIM].reshape(tile_tok, HEAD_DIM)]
            vals = [recv[tile, :, :, HEAD_DIM : 2 * HEAD_DIM].reshape(tile_tok, HEAD_DIM)]
            masks = [bias]
            turned = [k_turned]
            if tile > 0:
                keys.append(halo_kv[:, :HEAD_DIM])
                vals.append(halo_kv[:, HEAD_DIM:])
                masks.append(halo_bias)
                turned.append(halo_turned)
            logits = [dot_nt(key, q_head) * factor + mask[...] for key, mask in zip(keys, masks)]
            high = jnp.max(logits[0], axis=0, keepdims=True)
            for part in logits[1:]:
                high = jnp.maximum(high, jnp.max(part, axis=0, keepdims=True))
            probs = [jnp.exp(part - high) for part in logits]
            mass = sum(jnp.sum(part, axis=0, keepdims=True) for part in probs)
            scale = 1.0 / mass
            probs = [part * scale for part in probs]
            d_probs = [dot_nt(val, g_head) for val in vals]
            delta = sum(
                jnp.sum(part * d_part, axis=0, keepdims=True) for part, d_part in zip(probs, d_probs)
            )
            dq_turned = jnp.zeros((HEAD_DIM, tile_tok), F32)
            for n in range(len(keys)):
                d_logits = (probs[n] * (d_probs[n] - delta)).astype(BF16)
                d_key = dot_nn(d_logits, q_head)
                d_val = dot_nn(probs[n].astype(BF16), g_head)
                if n == 0:
                    d_acc[tile, :, :HEAD_DIM] += d_key
                    d_acc[tile, :, HEAD_DIM:] += d_val
                else:
                    halo_acc[:, :HEAD_DIM] += d_key
                    halo_acc[:, HEAD_DIM:] += d_val
                dq_turned += dot_nn(turned[n][...], d_logits)
            dq_head = (dq_turned * factor).T.astype(BF16)
            lanes = pl.ds(at, HEAD_DIM)
            home_q[tile, :, :, :, lanes] = dq_head.reshape(n_grp, n_sp, STEP, HEAD_DIM)
            if tile == last:
                go_home(
                    home_q.at[tile, :, :, :, lanes],
                    back_q.at[tile, :, :, :, lanes],
                    hq_send.at[last + head],
                    hq_recv.at[last + head],
                    hq_own.at[last + head],
                )

        if tile < last:
            go_home(
                home_q.at[tile], back_q.at[tile], hq_send.at[tile], hq_recv.at[tile], hq_own.at[tile]
            )
        if tile > 0:
            d_acc[tile - 1] += lax.dot_general(
                paste,
                halo_acc[...],
                (((1,), (0,)), ((), ())),
                precision=lax.Precision.HIGHEST,
                preferred_element_type=F32,
            )
            kv_home(tile - 1)
    kv_home(last)

    def settle(block, sem):
        pltpu.make_async_copy(block, block, sem).wait()

    away = pl.ds(0, n_sp - 1)
    for tile in range(tiles):
        settle(home_kv.at[tile, :, 0], hkv_own.at[tile])
        settle(home_kv.at[tile, :, away], hkv_send.at[tile])
        settle(home_kv.at[tile, :, away], hkv_recv.at[tile])
    for tile in range(last):
        settle(home_q.at[tile, :, 0], hq_own.at[tile])
        settle(home_q.at[tile, :, away], hq_send.at[tile])
        settle(home_q.at[tile, :, away], hq_recv.at[tile])
        settle(send.at[tile, pl.ds(0, peers - 1)], send_sem.at[tile])
    for head in range(heads):
        settle(home_q.at[last, :, 0, :, :HEAD_DIM], hq_own.at[last + head])
        settle(home_q.at[last, :, away, :, :HEAD_DIM], hq_send.at[last + head])
        settle(home_q.at[last, :, away, :, :HEAD_DIM], hq_recv.at[last + head])
        wide = 2 * pair if head == 0 else pair
        settle(send.at[last, pl.ds(0, peers - 1), :, :wide], send_sem.at[last + head])


def weave_kernel(back_q, back_kv, dq_ref, dk_ref, dv_ref):
    n_grp, n_sp, step, q_wide = back_q.shape
    rows = n_grp * step
    from_row = lane_iota(rows, rows)
    weave = row_iota(rows, rows) == lax.rem(from_row, step) * n_grp + from_row // step
    weave = weave.astype(F32).astype(BF16)
    for sp in range(n_sp):
        part = dot_nn(weave, back_q[:, sp].reshape(rows, q_wide)).astype(BF16)
        dq_ref[:, sp * q_wide : (sp + 1) * q_wide] = part
        both = dot_nn(weave, back_kv[:, sp].reshape(rows, 2 * HEAD_DIM)).astype(BF16)
        dk_ref[:, sp * HEAD_DIM : (sp + 1) * HEAD_DIM] = both[:, :HEAD_DIM]
        dv_ref[:, sp * HEAD_DIM : (sp + 1) * HEAD_DIM] = both[:, HEAD_DIM:]


def on_device_fused(q_src, k_src, v_src, grad_src, doc_lengths, doc_groups, doc_offsets):
    n_grp = lax.axis_size("grp")
    n_sp = lax.axis_size("sp")
    units = q_src.shape[0]
    slots = doc_lengths.shape[0]
    cap = slots // n_grp
    tiles = cap // STEP
    peers = n_grp * n_sp
    q_all = q_src.shape[-1]
    kv_all = k_src.shape[-1]
    q_wide = q_all // n_sp
    heads = q_wide // HEAD_DIM
    row_wide = 2 * HEAD_DIM * (heads + 1)
    tile_tok = peers * STEP
    halo_tok = peers * (MAXDOC - 1)
    parts = tiles - 1 + heads

    vmem = pl.BlockSpec(memory_space=pltpu.VMEM)
    hbm = pl.BlockSpec(memory_space=pl.ANY)
    dma = pltpu.SemaphoreType.DMA
    back_q, back_kv = pl.pallas_call(
        lambda *refs: fused_kernel(n_grp, n_sp, tiles, *refs),
        out_shape=(
            jax.ShapeDtypeStruct((tiles, n_grp, n_sp, STEP, q_wide), BF16),
            jax.ShapeDtypeStruct((tiles, n_grp, n_sp, STEP, 2 * HEAD_DIM), BF16),
        ),
        in_specs=[vmem] * 7,
        out_specs=(hbm, hbm),
        scratch_shapes=[
            pltpu.VMEM((tiles, peers, STEP, row_wide), BF16),
            pltpu.VMEM((tiles, peers, STEP, row_wide), BF16),
            pltpu.VMEM((tiles, n_grp, n_sp, STEP, q_wide), BF16),
            pltpu.VMEM((tiles, n_grp, n_sp, STEP, 2 * HEAD_DIM), BF16),
            pltpu.VMEM((tile_tok, tile_tok), F32),
            pltpu.VMEM((halo_tok, tile_tok), F32),
            pltpu.VMEM((halo_tok, 2 * HEAD_DIM), BF16),
            pltpu.VMEM((HEAD_DIM, tile_tok), BF16),
            pltpu.VMEM((HEAD_DIM, halo_tok), BF16),
            pltpu.VMEM((tiles, tile_tok, 2 * HEAD_DIM), F32),
            pltpu.VMEM((halo_tok, 2 * HEAD_DIM), F32),
            dma((parts,)),
            dma((parts,)),
            dma((tiles,)),
            dma((parts,)),
            dma((parts,)),
            dma((parts,)),
            dma((tiles,)),
            dma((tiles,)),
            dma((tiles,)),
        ],
        compiler_params=pltpu.CompilerParams(
            collective_id=0, has_side_effects=True, vmem_limit_bytes=56 * 1024 * 1024
        ),
    )(
        q_src.reshape(units, q_all),
        k_src.reshape(units, kv_all),
        v_src.reshape(units, kv_all),
        grad_src.reshape(units, q_all),
        doc_lengths.reshape(1, slots),
        doc_groups.reshape(1, slots),
        doc_offsets.reshape(1, slots),
    )
    rows = cap * n_grp
    out_rows = n_grp * STEP
    dq, dk, dv = pl.pallas_call(
        weave_kernel,
        grid=(tiles,),
        out_shape=(
            jax.ShapeDtypeStruct((rows, q_all), BF16),
            jax.ShapeDtypeStruct((rows, kv_all), BF16),
            jax.ShapeDtypeStruct((rows, kv_all), BF16),
        ),
        in_specs=[
            pl.BlockSpec((None, n_grp, n_sp, STEP, q_wide), lambda t: (t, 0, 0, 0, 0)),
            pl.BlockSpec((None, n_grp, n_sp, STEP, 2 * HEAD_DIM), lambda t: (t, 0, 0, 0, 0)),
        ],
        out_specs=(
            pl.BlockSpec((out_rows, q_all), lambda t: (t, 0)),
            pl.BlockSpec((out_rows, kv_all), lambda t: (t, 0)),
            pl.BlockSpec((out_rows, kv_all), lambda t: (t, 0)),
        ),
        compiler_params=pltpu.CompilerParams(vmem_limit_bytes=56 * 1024 * 1024),
    )(back_q, back_kv)
    return (
        dq.reshape(1, rows, 1, q_all),
        dk.reshape(1, rows, 1, kv_all),
        dv.reshape(1, rows, 1, kv_all),
    )


def on_device(q_src, k_src, v_src, grad_src, doc_lengths, doc_groups, doc_offsets):
    n_grp = lax.axis_size("grp")
    cap = doc_lengths.shape[0] // n_grp
    fits = lax.axis_size("sp") == KV_HEADS and cap % STEP == 0
    chosen = on_device_fused if fits else on_device_wide
    return chosen(q_src, k_src, v_src, grad_src, doc_lengths, doc_groups, doc_offsets)


def solution(mesh):
    placed = (
        P(None, "grp", "sp", None),
        P(None, "grp", "sp", None),
        P(None, "grp", "sp", None),
        P(None, "grp", "sp", None),
        P(),
        P(),
        P(),
    )
    return jax.shard_map(
        on_device,
        mesh=mesh,
        in_specs=placed,
        out_specs=(
            P("grp", None, "sp", None),
            P("grp", None, "sp", None),
            P("grp", None, "sp", None),
        ),
        check_vma=False,
    )
```

```python
import math

import jax
import jax.numpy as jnp
from jax import lax
from jax.experimental import pallas as pl
from jax.experimental.pallas import tpu as pltpu
from jax.sharding import PartitionSpec as P

HEADS = 32
KV_HEADS = 8
HEAD_DIM = 128


NEG_FILL = -1e30


def unchanged(passed):
    return passed


def collapse(array):
    rounded = lax.optimization_barrier(array)
    return jnp.sum(rounded.astype(jnp.float32), axis=2)


def pair_fold(low_part, high_part):
    return lax.optimization_barrier(
        (low_part.astype(jnp.float32) + high_part.astype(jnp.float32)).astype(jnp.bfloat16)
    )


def halves_total(array):
    half = array.shape[2] // 2
    return collapse(pair_fold(array[:, :, :half], array[:, :, half:]))


def attend(q_heads, k_heads, v_heads, g_heads, first_tok):
    tokens_here, kv_local, q_per_kv, head_dim = q_heads.shape
    span_len = math.gcd(tokens_here, 512)
    blocks = tokens_here // span_len
    factor = head_dim ** (-0.5)
    lane_pos = jnp.arange(span_len, dtype=jnp.int32)
    block_low = jnp.min(first_tok.reshape(blocks, span_len), axis=1)
    heads_shape = (kv_local, q_per_kv, span_len)

    def cut_block(array, index):
        return lax.dynamic_slice_in_dim(array, index * span_len, span_len, 0)

    def pair_logits(q_block, first_q, q_index, k_index):
        k_block = cut_block(k_heads, k_index)
        logits = (
            jnp.einsum("qjih,kjh->jiqk", q_block, k_block, preferred_element_type=jnp.float32)
            * factor
        )
        q_pos = q_index * span_len + lane_pos
        k_pos = k_index * span_len + lane_pos
        allowed = (k_pos[None, :] <= q_pos[:, None]) & (k_pos[None, :] >= first_q[:, None])
        return (logits, allowed)

    def is_live(q_index, k_index):
        return block_low[q_index] <= k_index * span_len + span_len - 1

    def row_norm(q_index):
        q_block = cut_block(q_heads, q_index)
        first_q = cut_block(first_tok, q_index)

        def visit_key(k_index, running):

            def update(running):
                row_high, row_mass = running
                logits, allowed = pair_logits(q_block, first_q, q_index, k_index)
                logits = jnp.where(allowed, logits, NEG_FILL)
                new_high = jnp.maximum(row_high, jnp.max(logits, axis=-1))
                row_mass = row_mass * jnp.exp(row_high - new_high) + jnp.sum(
                    jnp.where(allowed, jnp.exp(logits - new_high[..., None]), 0.0), axis=-1
                )
                return (new_high, row_mass)

            return lax.cond(is_live(q_index, k_index), update, unchanged, running)

        initial = (
            jnp.full(heads_shape, NEG_FILL, jnp.float32),
            jnp.zeros(heads_shape, jnp.float32),
        )
        row_high, row_mass = lax.fori_loop(0, q_index + 1, visit_key, initial)
        return row_high + jnp.log(row_mass)

    log_norm = lax.map(row_norm, jnp.arange(blocks, dtype=jnp.int32))

    def row_delta(q_index):
        q_block = cut_block(q_heads, q_index)
        first_q = cut_block(first_tok, q_index)
        norm_row = log_norm[q_index]

        def visit_key(k_index, acc_out):

            def update(acc_out):
                logits, allowed = pair_logits(q_block, first_q, q_index, k_index)
                weights = jnp.where(allowed, jnp.exp(logits - norm_row[..., None]), 0.0).astype(
                    jnp.bfloat16
                )
                v_block = cut_block(v_heads, k_index)
                return acc_out + jnp.einsum(
                    "jiqk,kjh->jiqh", weights, v_block, preferred_element_type=jnp.float32
                )

            return lax.cond(is_live(q_index, k_index), update, unchanged, acc_out)

        acc_out = lax.fori_loop(
            0, q_index + 1, visit_key, jnp.zeros(heads_shape + (head_dim,), jnp.float32)
        )
        g_block = cut_block(g_heads, q_index)
        return jnp.einsum("jiqh,qjih->jiq", acc_out, g_block, preferred_element_type=jnp.float32)

    delta_all = lax.map(row_delta, jnp.arange(blocks, dtype=jnp.int32))

    def back_row(q_index, carried):
        grad_q, grad_k, grad_v = carried
        q_block = cut_block(q_heads, q_index)
        g_block = cut_block(g_heads, q_index)
        first_q = cut_block(first_tok, q_index)
        norm_row = log_norm[q_index]
        delta_row = delta_all[q_index]

        def visit_key(k_index, inner):

            def update(inner):
                q_acc, grad_k, grad_v = inner
                logits, allowed = pair_logits(q_block, first_q, q_index, k_index)
                probs = jnp.where(allowed, jnp.exp(logits - norm_row[..., None]), 0.0)
                probs_low = probs.astype(jnp.bfloat16)
                k_block = cut_block(k_heads, k_index)
                v_block = cut_block(v_heads, k_index)
                d_probs = jnp.einsum(
                    "qjih,kjh->jiqk", g_block, v_block, preferred_element_type=jnp.float32
                )
                d_logits = (probs * (d_probs - delta_row[..., None])).astype(jnp.bfloat16)
                q_acc = q_acc + jnp.einsum(
                    "jiqk,kjh->qjih", d_logits, k_block, preferred_element_type=jnp.float32
                )
                k_part = jnp.einsum(
                    "jiqk,qjih->kjih", d_logits, q_block, preferred_element_type=jnp.float32
                )
                v_part = jnp.einsum(
                    "jiqk,qjih->kjih", probs_low, g_block, preferred_element_type=jnp.float32
                )
                at_row = k_index * span_len
                grad_k = lax.dynamic_update_slice_in_dim(
                    grad_k, cut_block(grad_k, k_index) + k_part, at_row, 0
                )
                grad_v = lax.dynamic_update_slice_in_dim(
                    grad_v, cut_block(grad_v, k_index) + v_part, at_row, 0
                )
                return (q_acc, grad_k, grad_v)

            return lax.cond(is_live(q_index, k_index), update, unchanged, inner)

        q_start = jnp.zeros((span_len, kv_local, q_per_kv, head_dim), jnp.float32)
        q_acc, grad_k, grad_v = lax.fori_loop(0, q_index + 1, visit_key, (q_start, grad_k, grad_v))
        grad_q = lax.dynamic_update_slice_in_dim(grad_q, q_acc, q_index * span_len, 0)
        return (grad_q, grad_k, grad_v)

    empty = jnp.zeros((tokens_here, kv_local, q_per_kv, head_dim), jnp.float32)
    grad_q, grad_k, grad_v = lax.fori_loop(0, blocks, back_row, (empty, empty, empty))
    return (grad_q * factor, grad_k * factor, grad_v)


def on_device_wide(q_src, k_src, v_src, grad_src, doc_lengths, doc_groups, doc_offsets):
    grp_count = lax.axis_size("grp")
    sp_count = lax.axis_size("sp")
    unit_count = q_src.shape[0]
    slot_count = doc_lengths.shape[0]
    group_cap = slot_count // grp_count
    row_count = group_cap * grp_count
    unit_tok = grp_count * sp_count
    group_tok = row_count * sp_count
    head_dim = HEAD_DIM
    copies = max(1, sp_count // KV_HEADS)
    kv_local = max(1, KV_HEADS // sp_count)
    q_local = HEADS // sp_count
    q_per_kv = q_local // kv_local
    unit_ids = jnp.arange(unit_count, dtype=jnp.int32)
    starts = jnp.cumsum(doc_lengths) - doc_lengths
    inside = (
        (unit_ids[:, None] >= starts[None, :])
        & (unit_ids[:, None] < (starts + doc_lengths)[None, :])
    ).astype(jnp.int32)
    group_of = jnp.sum(inside * doc_groups[None, :], axis=1)
    place_of = jnp.sum(
        inside * (doc_offsets[None, :] + unit_ids[:, None] - starts[None, :]), axis=1
    )
    slot_of = group_of * group_cap + place_of
    slot_ids = jnp.arange(row_count, dtype=jnp.int32).reshape(grp_count, group_cap).T.reshape(-1)
    matches = (slot_of[None, :] == slot_ids[:, None]).astype(jnp.int32)
    source = jnp.sum(matches * unit_ids[None, :], axis=1)
    filled = jnp.sum(matches, axis=1) > 0

    def pack_rows(array):
        flat = array.reshape(unit_count, array.shape[-1])
        picked = jnp.take(flat, source, axis=0)
        picked = jnp.where(filled[:, None], picked, jnp.zeros_like(picked))
        return picked.reshape(group_cap, grp_count, array.shape[-1])

    arrived = (
        lax.all_to_all(pack_rows(q_src), "grp", split_axis=1, concat_axis=1, tiled=True),
        lax.all_to_all(pack_rows(k_src), "grp", split_axis=1, concat_axis=1, tiled=True),
        lax.all_to_all(pack_rows(v_src), "grp", split_axis=1, concat_axis=1, tiled=True),
        lax.all_to_all(pack_rows(grad_src), "grp", split_axis=1, concat_axis=1, tiled=True),
    )
    q_rows = arrived[0].reshape(row_count, 1, HEADS, head_dim)
    k_rows = arrived[1].reshape(row_count, KV_HEADS, head_dim)
    v_rows = arrived[2].reshape(row_count, KV_HEADS, head_dim)
    g_rows = arrived[3].reshape(row_count, 1, HEADS, head_dim)
    my_group = lax.axis_index("grp")
    unit_place = jnp.arange(group_cap, dtype=jnp.int32)
    member = (
        (doc_groups[None, :] == my_group)
        & (doc_lengths[None, :] > 0)
        & (doc_offsets[None, :] <= unit_place[:, None])
        & (unit_place[:, None] < (doc_offsets + doc_lengths)[None, :])
    ).astype(jnp.int32)
    first_unit = jnp.sum(member * doc_offsets[None, :], axis=1)
    occupied = jnp.sum(member, axis=1) > 0
    token_ids = jnp.arange(group_tok, dtype=jnp.int32)
    first_tok = jnp.where(
        jnp.repeat(occupied, unit_tok), jnp.repeat(first_unit * unit_tok, unit_tok), token_ids
    )
    k_wide = jnp.repeat(k_rows, copies, axis=1).reshape(row_count, 1, KV_HEADS * copies, head_dim)
    v_wide = jnp.repeat(v_rows, copies, axis=1).reshape(row_count, 1, KV_HEADS * copies, head_dim)
    q_back, g_back, k_back, v_back = (
        lax.all_to_all(q_rows, "sp", split_axis=2, concat_axis=1, tiled=True),
        lax.all_to_all(g_rows, "sp", split_axis=2, concat_axis=1, tiled=True),
        lax.all_to_all(k_wide, "sp", split_axis=2, concat_axis=1, tiled=True),
        lax.all_to_all(v_wide, "sp", split_axis=2, concat_axis=1, tiled=True),
    )
    k_heads = k_back.reshape(group_tok, kv_local, head_dim)
    v_heads = v_back.reshape(group_tok, kv_local, head_dim)
    q_heads = q_back.reshape(group_tok, kv_local, q_per_kv, head_dim)
    g_heads = g_back.reshape(group_tok, kv_local, q_per_kv, head_dim)
    grad_q, grad_k, grad_v = attend(q_heads, k_heads, v_heads, g_heads, first_tok)
    q_low = grad_q.astype(jnp.bfloat16).reshape(row_count, sp_count, q_local, head_dim)
    k_low = grad_k.astype(jnp.bfloat16)
    v_low = grad_v.astype(jnp.bfloat16)
    q_home, k_home, v_home = (
        lax.all_to_all(q_low, "sp", split_axis=1, concat_axis=2, tiled=True),
        lax.all_to_all(
            k_low.reshape(row_count, sp_count, q_local, head_dim),
            "sp",
            split_axis=1,
            concat_axis=2,
            tiled=True,
        ),
        lax.all_to_all(
            v_low.reshape(row_count, sp_count, q_local, head_dim),
            "sp",
            split_axis=1,
            concat_axis=2,
            tiled=True,
        ),
    )
    k_sum = halves_total(k_home.reshape(row_count, KV_HEADS, HEADS // KV_HEADS, head_dim))
    v_sum = halves_total(v_home.reshape(row_count, KV_HEADS, HEADS // KV_HEADS, head_dim))
    dk_out = k_sum.astype(jnp.bfloat16).reshape(1, row_count, 1, KV_HEADS * head_dim)
    dv_out = v_sum.astype(jnp.bfloat16).reshape(1, row_count, 1, KV_HEADS * head_dim)
    dq_out = q_home.reshape(1, row_count, 1, HEADS * head_dim)
    return (dq_out, dk_out, dv_out)


MESH = pl.DeviceIdType.MESH
STEP = 16
MAXDOC = 5
F32 = jnp.float32
BF16 = jnp.bfloat16


def dot_nt(left, right):
    return lax.dot_general(left, right, (((1,), (1,)), ((), ())), preferred_element_type=F32)


def dot_nn(left, right):
    return lax.dot_general(left, right, (((1,), (0,)), ((), ())), preferred_element_type=F32)


def lane_iota(rows, lanes):
    return lax.broadcasted_iota(jnp.int32, (rows, lanes), 1)


def row_iota(rows, lanes):
    return lax.broadcasted_iota(jnp.int32, (rows, lanes), 0)


def fused_kernel(
    n_grp,
    n_sp,
    tiles,
    full_grps,
    q_ref,
    k_ref,
    v_ref,
    g_ref,
    len_ref,
    grp_ref,
    off_ref,
    dq_ref,
    dk_ref,
    dv_ref,
    send,
    recv,
    home_q,
    home_k,
    home_v,
    order,
    bias,
    halo_bias,
    halo_kv,
    k_turned,
    halo_turned,
    d_acc,
    halo_acc,
    send_sem,
    recv_sem,
    own_sem,
    hq_send,
    hq_recv,
    hq_own,
    hk_send,
    hk_recv,
    hk_own,
    hv_send,
    hv_recv,
    hv_own,
):
    my_grp = lax.axis_index("grp")
    my_sp = lax.axis_index("sp")
    peers = n_grp * n_sp
    me = my_grp * n_sp + my_sp
    units = q_ref.shape[0]
    q_wide = q_ref.shape[1] // n_sp
    heads = q_wide // HEAD_DIM
    cap = tiles * STEP
    tile_tok = peers * STEP
    halo = MAXDOC - 1
    halo_tok = peers * halo
    factor = HEAD_DIM ** (-0.5)
    row_wide = 2 * HEAD_DIM * (heads + 1)
    last = tiles - 1
    kv_lanes = pl.ds(0, 2 * HEAD_DIM)

    barrier = pltpu.get_barrier_semaphore()

    @pl.loop(1, peers)
    def _(hop):
        there = {
            "grp": lax.rem(my_grp + hop // n_sp, n_grp),
            "sp": lax.rem(my_sp + lax.rem(hop, n_sp), n_sp),
        }
        pl.semaphore_signal(barrier, inc=1, device_id=there, device_id_type=MESH)

    slots = len_ref.shape[1]
    which = row_iota(8, slots)
    tables = jnp.where(
        which == 0, len_ref[...], jnp.where(which == 1, grp_ref[...], jnp.where(which == 2, off_ref[...], 0))
    )
    tables = tables.astype(F32).astype(BF16)
    down, across = row_iota(slots, slots), lane_iota(slots, slots)
    columns = dot_nt((down == across).astype(F32).astype(BF16), tables)
    length, group, offset = columns[:, 0:1], columns[:, 1:2], columns[:, 2:3]
    start = dot_nt((across < down).astype(F32).astype(BF16), tables)[:, 0:1]
    unit = lane_iota(1, units).astype(F32)
    inside = (unit >= start) & (unit < start + length)
    slot_of = unit + jnp.sum(
        jnp.where(inside, group * cap + offset - start, 0.0), axis=0, keepdims=True
    )

    def pack(tile):
        row = row_iota(n_grp * STEP, 1)
        slot = (row // STEP) * cap + tile * STEP + lax.rem(row, STEP)
        hot = (slot.astype(F32) == slot_of).astype(F32).astype(BF16)

        def put(to, at, ref, lane, wide):
            part = dot_nn(hot, ref[:, lane : lane + wide]).astype(BF16).reshape(n_grp, STEP, wide)
            for grp in range(n_grp):
                send[tile, grp * n_sp + to, :, at : at + wide] = part[grp]

        for to in range(n_sp):
            put(to, 0, k_ref, to * HEAD_DIM, HEAD_DIM)
            put(to, HEAD_DIM, v_ref, to * HEAD_DIM, HEAD_DIM)
            for head in range(heads):
                lane = to * q_wide + head * HEAD_DIM
                put(to, 2 * HEAD_DIM * (head + 1), q_ref, lane, HEAD_DIM)
                put(to, 2 * HEAD_DIM * (head + 1) + HEAD_DIM, g_ref, lane, HEAD_DIM)

    def push(tile, lanes, sem, to_grp, to_sp):
        pltpu.make_async_remote_copy(
            src_ref=send.at[tile, to_grp * n_sp + to_sp, :, lanes],
            dst_ref=recv.at[tile, me, :, lanes],
            send_sem=send_sem.at[sem],
            recv_sem=recv_sem.at[sem],
            device_id={"grp": to_grp, "sp": to_sp},
            device_id_type=MESH,
        ).start()

    half = n_grp // 2

    def scatter(tile, lane, wide, sem):
        @pl.loop(0, peers)
        def _(hop):
            turn = hop // n_sp
            side = lax.rem(my_grp // half + 1 + turn // half, 2)
            to_grp = side * half + lax.rem(my_grp + turn, half)
            to_sp = lax.rem(my_sp + hop, n_sp)

            @pl.when((to_grp != my_grp) | (to_sp != my_sp))
            def _():
                push(tile, pl.ds(lane, wide), sem, to_grp, to_sp)

    def landed(tile, lane, wide, sem):
        block = recv.at[tile, pl.ds(0, peers - 1), :, pl.ds(lane, wide)]
        pltpu.make_async_copy(block, block, recv_sem.at[sem]).wait()

    def own_block(tile):
        return pltpu.make_async_copy(send.at[tile, me], recv.at[tile, me], own_sem.at[tile])

    pair = 2 * HEAD_DIM
    takes_last = sum(((my_grp == grp).astype(jnp.int32) for grp in full_grps), jnp.int32(0)) > 0

    pack(last)
    pl.semaphore_wait(barrier, peers - 1)
    if len(full_grps) == n_grp:
        scatter(last, 0, row_wide, last)
    else:
        for to_grp in full_grps:

            @pl.loop(0, n_sp)
            def _(hop):
                @pl.when((my_grp != to_grp) | (hop > 0))
                def _():
                    push(last, pl.ds(0, row_wide), last, to_grp, lax.rem(my_sp + hop, n_sp))

    for tile in range(last - 1, 0, -1):
        pack(tile)
        scatter(tile, 0, row_wide, tile)
    pack(0)
    scatter(0, 0, pair, 0)
    for head in range(heads):
        scatter(0, (head + 1) * pair, pair, tiles + head)
    for tile in range(last):
        own_block(tile).start()

    @pl.when(takes_last)
    def _():
        own_block(last).start()

    @pl.when(jnp.logical_not(takes_last))
    def _():
        recv[last] = jnp.zeros(recv.shape[1:], BF16)

    d_acc[...] = jnp.zeros_like(d_acc)
    to_row = row_iota(tile_tok, 1)
    out_rows = n_grp * STEP
    of_row = (
        (lax.rem(to_row, n_grp) * n_sp + to_row // out_rows) * STEP + lax.rem(to_row, out_rows) // n_grp
    )
    order[...] = (of_row == lane_iota(1, tile_tok)).astype(F32).astype(BF16)

    def go_home(here, out, tile, lane, sends, recvs, own):
        wide = here.shape[-1]
        there = out.at[pl.ds(tile * out_rows, out_rows), pl.ds(pl.multiple_of(lane, HEAD_DIM), wide)]

        @pl.loop(1, n_sp)
        def _(hop):
            to_sp = lax.rem(my_sp + hop, n_sp)
            pltpu.make_async_remote_copy(
                src_ref=here.at[to_sp],
                dst_ref=there,
                send_sem=sends,
                recv_sem=recvs,
                device_id={"grp": my_grp, "sp": to_sp},
                device_id_type=MESH,
            ).start()

        pltpu.make_async_copy(here.at[my_sp], there, own).start()

    def kv_home(tile):
        shape = (n_sp, out_rows, HEAD_DIM)
        d_key = (d_acc[tile, :, :HEAD_DIM] * factor).astype(BF16)
        home_k[tile] = dot_nn(order[...], d_key).astype(BF16).reshape(shape)
        lane = my_sp * HEAD_DIM
        go_home(home_k.at[tile], dk_ref, tile, lane, hk_send.at[tile], hk_recv.at[tile], hk_own.at[tile])
        d_val = d_acc[tile, :, HEAD_DIM:].astype(BF16)
        home_v[tile] = dot_nn(order[...], d_val).astype(BF16).reshape(shape)
        go_home(home_v.at[tile], dv_ref, tile, lane, hv_send.at[tile], hv_recv.at[tile], hv_own.at[tile])

    halo_row = row_iota(halo_tok, 1)
    halo_from = (halo_row // halo) * STEP + STEP - halo + lax.rem(halo_row, halo)
    cut = (halo_from == lane_iota(1, tile_tok)).astype(F32).astype(BF16)
    row = row_iota(tile_tok, 1)
    halo_lane = lane_iota(1, halo_tok)
    paste = (
        row == (halo_lane // halo) * STEP + STEP - halo + lax.rem(halo_lane, halo)
    ).astype(F32)

    @pl.when(takes_last)
    def _():
        own_block(last).wait()
        landed(last, 0, row_wide, last)

    for tile in range(last, -1, -1):
        lane = lane_iota(1, tile_tok)
        q_block = tile * STEP + lax.rem(lane, STEP)
        q_pos = q_block * peers + lane // STEP
        place = q_block.astype(F32)
        member = (
            (group == my_grp.astype(F32))
            & (length > 0.0)
            & (offset <= place)
            & (place < offset + length)
        )
        first = jnp.sum(jnp.where(member, offset * peers, 0.0), axis=0, keepdims=True)
        occupied = jnp.sum(jnp.where(member, 1.0, 0.0), axis=0, keepdims=True) > 0.0
        first = jnp.where(occupied, first, q_pos.astype(F32)).astype(jnp.int32)
        k_pos = (tile * STEP + lax.rem(row, STEP)) * peers + row // STEP
        bias[...] = jnp.where((k_pos <= q_pos) & (k_pos >= first), 0.0, NEG_FILL)
        if tile > 0:
            own_block(tile - 1).wait()
            landed(tile - 1, 0, row_wide if tile > 1 else pair, tile - 1)
            halo_pos = (tile * STEP - halo + lax.rem(halo_row, halo)) * peers + halo_row // halo
            halo_bias[...] = jnp.where(halo_pos >= first, 0.0, NEG_FILL)
            kv_before = recv[tile - 1, :, :, : 2 * HEAD_DIM].reshape(tile_tok, 2 * HEAD_DIM)
            kv_cut = dot_nn(cut, kv_before)
            halo_kv[...] = kv_cut.astype(BF16)
            halo_turned[...] = kv_cut[:, :HEAD_DIM].T.astype(BF16)
            halo_acc[...] = jnp.zeros_like(halo_acc)

        k_turned[...] = (
            recv[tile, :, :, :HEAD_DIM].reshape(tile_tok, HEAD_DIM).astype(F32).T.astype(BF16)
        )

        @pl.loop(0, heads)
        def _(head):
            if tile == 0:
                landed(0, pair, pair, tiles + head)

            at = pl.multiple_of(head * HEAD_DIM, HEAD_DIM)
            q_at = pl.multiple_of((head + 1) * pair, HEAD_DIM)
            g_at = pl.multiple_of((head + 1) * pair + HEAD_DIM, HEAD_DIM)
            q_head = recv[tile, :, :, pl.ds(q_at, HEAD_DIM)].reshape(tile_tok, HEAD_DIM)
            g_head = recv[tile, :, :, pl.ds(g_at, HEAD_DIM)].reshape(tile_tok, HEAD_DIM)
            keys = [recv[tile, :, :, :HEAD_DIM].reshape(tile_tok, HEAD_DIM)]
            vals = [recv[tile, :, :, HEAD_DIM : 2 * HEAD_DIM].reshape(tile_tok, HEAD_DIM)]
            masks = [bias]
            turned = [k_turned]
            if tile > 0:
                keys.append(halo_kv[:, :HEAD_DIM])
                vals.append(halo_kv[:, HEAD_DIM:])
                masks.append(halo_bias)
                turned.append(halo_turned)
            logits = [dot_nt(key, q_head) * factor + mask[...] for key, mask in zip(keys, masks)]
            high = jnp.max(logits[0], axis=0, keepdims=True)
            for part in logits[1:]:
                high = jnp.maximum(high, jnp.max(part, axis=0, keepdims=True))
            probs = [jnp.exp(part - high) for part in logits]
            mass = sum(jnp.sum(part, axis=0, keepdims=True) for part in probs)
            scale = 1.0 / mass
            probs = [part * scale for part in probs]
            d_probs = [dot_nt(val, g_head) for val in vals]
            delta = sum(
                jnp.sum(part * d_part, axis=0, keepdims=True) for part, d_part in zip(probs, d_probs)
            )
            dq_turned = jnp.zeros((HEAD_DIM, tile_tok), F32)
            for n in range(len(keys)):
                d_logits = (probs[n] * (d_probs[n] - delta)).astype(BF16)
                d_key = dot_nn(d_logits, q_head)
                d_val = dot_nn(probs[n].astype(BF16), g_head)
                if n == 0:
                    d_acc[tile, :, :HEAD_DIM] += d_key
                    d_acc[tile, :, HEAD_DIM:] += d_val
                else:
                    halo_acc[:, :HEAD_DIM] += d_key
                    halo_acc[:, HEAD_DIM:] += d_val
                dq_turned += dot_nn(turned[n][...], d_logits)
            dq_head = dot_nt(order[...], (dq_turned * factor).astype(BF16)).astype(BF16)
            lanes = pl.ds(at, HEAD_DIM)
            home_q[tile, :, :, lanes] = dq_head.reshape(n_sp, out_rows, HEAD_DIM)
            if tile == 0:
                go_home(
                    home_q.at[0, :, :, lanes],
                    dq_ref,
                    0,
                    my_sp * q_wide + head * HEAD_DIM,
                    hq_send.at[last + head],
                    hq_recv.at[last + head],
                    hq_own.at[last + head],
                )

        if tile > 0:
            go_home(
                home_q.at[tile],
                dq_ref,
                tile,
                my_sp * q_wide,
                hq_send.at[tile - 1],
                hq_recv.at[tile - 1],
                hq_own.at[tile - 1],
            )
        kv_home(tile)
        if tile > 0:
            d_acc[tile - 1] += lax.dot_general(
                paste,
                halo_acc[...],
                (((1,), (0,)), ((), ())),
                precision=lax.Precision.HIGHEST,
                preferred_element_type=F32,
            )

    def settle(block, sem):
        pltpu.make_async_copy(block, block, sem).wait()

    def settle_home(here, sends, recvs, own):
        away = here.at[pl.ds(0, n_sp - 1)]
        settle(here.at[0], own)
        settle(away, sends)
        settle(away, recvs)

    def settle_sent(tile, lane, wide, count, sem):
        settle(send.at[tile, pl.ds(0, count), :, pl.ds(lane, wide)], send_sem.at[sem])

    for tile in range(tiles):
        settle_home(home_k.at[tile], hk_send.at[tile], hk_recv.at[tile], hk_own.at[tile])
        settle_home(home_v.at[tile], hv_send.at[tile], hv_recv.at[tile], hv_own.at[tile])
    for n in range(last):
        settle_home(home_q.at[n + 1], hq_send.at[n], hq_recv.at[n], hq_own.at[n])
    for head in range(heads):
        n = last + head
        settle_home(home_q.at[0, :, :, pl.ds(0, HEAD_DIM)], hq_send.at[n], hq_recv.at[n], hq_own.at[n])
        settle_sent(0, 0, pair, peers - 1, tiles + head)
    settle_sent(0, 0, pair, peers - 1, 0)
    for tile in range(1, last):
        settle_sent(tile, 0, row_wide, peers - 1, tile)

    @pl.when(takes_last)
    def _():
        settle_sent(last, 0, row_wide, len(full_grps) * n_sp - 1, last)

    if len(full_grps) < n_grp:

        @pl.when(jnp.logical_not(takes_last))
        def _():
            settle_sent(last, 0, row_wide, len(full_grps) * n_sp, last)


def result_kernel(*refs):
    sources, results, held = refs[:3], refs[3:6], refs[6:9]
    load_sem, store_sem = refs[9:]
    rows = held[0].shape[0]
    cuts = [(0, pl.ds(n * rows // 4, rows // 4)) for n in range(4)] + [(1, pl.ds(0, rows)), (2, pl.ds(0, rows))]
    loads = [
        pltpu.make_async_copy(sources[n].at[cut], held[n].at[cut], load_sem.at[i])
        for i, (n, cut) in enumerate(cuts)
    ]
    stores = [
        pltpu.make_async_copy(held[n].at[cut], results[n].at[cut], store_sem.at[i])
        for i, (n, cut) in enumerate(cuts)
    ]
    for load in loads:
        load.start()
    for load, store in zip(loads, stores):
        load.wait()
        store.start()
    for store in stores:
        store.wait()


def on_device_fused(q_src, k_src, v_src, grad_src, doc_lengths, doc_groups, doc_offsets):
    n_grp = lax.axis_size("grp")
    n_sp = lax.axis_size("sp")
    units = q_src.shape[0]
    slots = doc_lengths.shape[0]
    cap = slots // n_grp
    tiles = cap // STEP
    peers = n_grp * n_sp
    q_all = q_src.shape[-1]
    kv_all = k_src.shape[-1]
    q_wide = q_all // n_sp
    heads = q_wide // HEAD_DIM
    row_wide = 2 * HEAD_DIM * (heads + 1)
    tile_tok = peers * STEP
    halo_tok = peers * (MAXDOC - 1)
    out_rows = n_grp * STEP
    rows = cap * n_grp
    shapes = (
        jax.ShapeDtypeStruct((rows, q_all), BF16),
        jax.ShapeDtypeStruct((rows, kv_all), BF16),
        jax.ShapeDtypeStruct((rows, kv_all), BF16),
    )
    vmem = pl.BlockSpec(memory_space=pltpu.VMEM)
    hbm = pl.BlockSpec(memory_space=pl.ANY)
    dma = pltpu.SemaphoreType.DMA

    def run(full_grps, number):
        return pl.pallas_call(
            lambda *refs: fused_kernel(n_grp, n_sp, tiles, full_grps, *refs),
            out_shape=shapes,
            in_specs=[vmem] * 7,
            out_specs=(hbm,) * 3,
            scratch_shapes=[
                pltpu.VMEM((tiles, peers, STEP, row_wide), BF16),
                pltpu.VMEM((tiles, peers, STEP, row_wide), BF16),
                pltpu.VMEM((tiles, n_sp, out_rows, q_wide), BF16),
                pltpu.VMEM((tiles, n_sp, out_rows, HEAD_DIM), BF16),
                pltpu.VMEM((tiles, n_sp, out_rows, HEAD_DIM), BF16),
                pltpu.VMEM((tile_tok, tile_tok), BF16),
                pltpu.VMEM((tile_tok, tile_tok), F32),
                pltpu.VMEM((halo_tok, tile_tok), F32),
                pltpu.VMEM((halo_tok, 2 * HEAD_DIM), BF16),
                pltpu.VMEM((HEAD_DIM, tile_tok), BF16),
                pltpu.VMEM((HEAD_DIM, halo_tok), BF16),
                pltpu.VMEM((tiles, tile_tok, 2 * HEAD_DIM), F32),
                pltpu.VMEM((halo_tok, 2 * HEAD_DIM), F32),
                dma((tiles + heads,)),
                dma((tiles + heads,)),
                dma((tiles,)),
                dma((tiles - 1 + heads,)),
                dma((tiles - 1 + heads,)),
                dma((tiles - 1 + heads,)),
            ]
            + [dma((tiles,))] * 6,
            compiler_params=pltpu.CompilerParams(
                collective_id=number, has_side_effects=True, vmem_limit_bytes=56 * 1024 * 1024
            ),
        )(
            q_src.reshape(units, q_all),
            k_src.reshape(units, kv_all),
            v_src.reshape(units, kv_all),
            grad_src.reshape(units, q_all),
            doc_lengths.reshape(1, slots),
            doc_groups.reshape(1, slots),
            doc_offsets.reshape(1, slots),
        )

    passed = run(tuple(range(n_grp)), 0)
    dq, dk, dv = pl.pallas_call(
        result_kernel,
        out_shape=shapes,
        in_specs=[hbm] * 3,
        out_specs=(hbm,) * 3,
        scratch_shapes=[pltpu.VMEM(shape.shape, BF16) for shape in shapes] + [dma((6,)), dma((6,))],
        compiler_params=pltpu.CompilerParams(vmem_limit_bytes=56 * 1024 * 1024),
    )(*passed)
    return (
        dq.reshape(1, rows, 1, q_all),
        dk.reshape(1, rows, 1, kv_all),
        dv.reshape(1, rows, 1, kv_all),
    )


def on_device(q_src, k_src, v_src, grad_src, doc_lengths, doc_groups, doc_offsets):
    n_grp = lax.axis_size("grp")
    cap = doc_lengths.shape[0] // n_grp
    fits = lax.axis_size("sp") == KV_HEADS and cap % STEP == 0 and cap > STEP and n_grp % 2 == 0
    chosen = on_device_fused if fits else on_device_wide
    return chosen(q_src, k_src, v_src, grad_src, doc_lengths, doc_groups, doc_offsets)


def solution(mesh):
    placed = (
        P(None, "grp", "sp", None),
        P(None, "grp", "sp", None),
        P(None, "grp", "sp", None),
        P(None, "grp", "sp", None),
        P(),
        P(),
        P(),
    )
    return jax.shard_map(
        on_device,
        mesh=mesh,
        in_specs=placed,
        out_specs=(
            P("grp", None, "sp", None),
            P("grp", None, "sp", None),
            P("grp", None, "sp", None),
        ),
        check_vma=False,
    )
```

```python
import math

import jax
import jax.numpy as jnp
from jax import lax
from jax.experimental import pallas as pl
from jax.experimental.pallas import tpu as pltpu
from jax.sharding import PartitionSpec as P

HEADS = 32
KV_HEADS = 8
HEAD_DIM = 128


NEG_FILL = -1e30


def unchanged(passed):
    return passed


def collapse(array):
    rounded = lax.optimization_barrier(array)
    return jnp.sum(rounded.astype(jnp.float32), axis=2)


def pair_fold(low_part, high_part):
    return lax.optimization_barrier(
        (low_part.astype(jnp.float32) + high_part.astype(jnp.float32)).astype(jnp.bfloat16)
    )


def halves_total(array):
    half = array.shape[2] // 2
    return collapse(pair_fold(array[:, :, :half], array[:, :, half:]))


def attend(q_heads, k_heads, v_heads, g_heads, first_tok):
    tokens_here, kv_local, q_per_kv, head_dim = q_heads.shape
    span_len = math.gcd(tokens_here, 512)
    blocks = tokens_here // span_len
    factor = head_dim ** (-0.5)
    lane_pos = jnp.arange(span_len, dtype=jnp.int32)
    block_low = jnp.min(first_tok.reshape(blocks, span_len), axis=1)
    heads_shape = (kv_local, q_per_kv, span_len)

    def cut_block(array, index):
        return lax.dynamic_slice_in_dim(array, index * span_len, span_len, 0)

    def pair_logits(q_block, first_q, q_index, k_index):
        k_block = cut_block(k_heads, k_index)
        logits = (
            jnp.einsum("qjih,kjh->jiqk", q_block, k_block, preferred_element_type=jnp.float32)
            * factor
        )
        q_pos = q_index * span_len + lane_pos
        k_pos = k_index * span_len + lane_pos
        allowed = (k_pos[None, :] <= q_pos[:, None]) & (k_pos[None, :] >= first_q[:, None])
        return (logits, allowed)

    def is_live(q_index, k_index):
        return block_low[q_index] <= k_index * span_len + span_len - 1

    def row_norm(q_index):
        q_block = cut_block(q_heads, q_index)
        first_q = cut_block(first_tok, q_index)

        def visit_key(k_index, running):

            def update(running):
                row_high, row_mass = running
                logits, allowed = pair_logits(q_block, first_q, q_index, k_index)
                logits = jnp.where(allowed, logits, NEG_FILL)
                new_high = jnp.maximum(row_high, jnp.max(logits, axis=-1))
                row_mass = row_mass * jnp.exp(row_high - new_high) + jnp.sum(
                    jnp.where(allowed, jnp.exp(logits - new_high[..., None]), 0.0), axis=-1
                )
                return (new_high, row_mass)

            return lax.cond(is_live(q_index, k_index), update, unchanged, running)

        initial = (
            jnp.full(heads_shape, NEG_FILL, jnp.float32),
            jnp.zeros(heads_shape, jnp.float32),
        )
        row_high, row_mass = lax.fori_loop(0, q_index + 1, visit_key, initial)
        return row_high + jnp.log(row_mass)

    log_norm = lax.map(row_norm, jnp.arange(blocks, dtype=jnp.int32))

    def row_delta(q_index):
        q_block = cut_block(q_heads, q_index)
        first_q = cut_block(first_tok, q_index)
        norm_row = log_norm[q_index]

        def visit_key(k_index, acc_out):

            def update(acc_out):
                logits, allowed = pair_logits(q_block, first_q, q_index, k_index)
                weights = jnp.where(allowed, jnp.exp(logits - norm_row[..., None]), 0.0).astype(
                    jnp.bfloat16
                )
                v_block = cut_block(v_heads, k_index)
                return acc_out + jnp.einsum(
                    "jiqk,kjh->jiqh", weights, v_block, preferred_element_type=jnp.float32
                )

            return lax.cond(is_live(q_index, k_index), update, unchanged, acc_out)

        acc_out = lax.fori_loop(
            0, q_index + 1, visit_key, jnp.zeros(heads_shape + (head_dim,), jnp.float32)
        )
        g_block = cut_block(g_heads, q_index)
        return jnp.einsum("jiqh,qjih->jiq", acc_out, g_block, preferred_element_type=jnp.float32)

    delta_all = lax.map(row_delta, jnp.arange(blocks, dtype=jnp.int32))

    def back_row(q_index, carried):
        grad_q, grad_k, grad_v = carried
        q_block = cut_block(q_heads, q_index)
        g_block = cut_block(g_heads, q_index)
        first_q = cut_block(first_tok, q_index)
        norm_row = log_norm[q_index]
        delta_row = delta_all[q_index]

        def visit_key(k_index, inner):

            def update(inner):
                q_acc, grad_k, grad_v = inner
                logits, allowed = pair_logits(q_block, first_q, q_index, k_index)
                probs = jnp.where(allowed, jnp.exp(logits - norm_row[..., None]), 0.0)
                probs_low = probs.astype(jnp.bfloat16)
                k_block = cut_block(k_heads, k_index)
                v_block = cut_block(v_heads, k_index)
                d_probs = jnp.einsum(
                    "qjih,kjh->jiqk", g_block, v_block, preferred_element_type=jnp.float32
                )
                d_logits = (probs * (d_probs - delta_row[..., None])).astype(jnp.bfloat16)
                q_acc = q_acc + jnp.einsum(
                    "jiqk,kjh->qjih", d_logits, k_block, preferred_element_type=jnp.float32
                )
                k_part = jnp.einsum(
                    "jiqk,qjih->kjih", d_logits, q_block, preferred_element_type=jnp.float32
                )
                v_part = jnp.einsum(
                    "jiqk,qjih->kjih", probs_low, g_block, preferred_element_type=jnp.float32
                )
                at_row = k_index * span_len
                grad_k = lax.dynamic_update_slice_in_dim(
                    grad_k, cut_block(grad_k, k_index) + k_part, at_row, 0
                )
                grad_v = lax.dynamic_update_slice_in_dim(
                    grad_v, cut_block(grad_v, k_index) + v_part, at_row, 0
                )
                return (q_acc, grad_k, grad_v)

            return lax.cond(is_live(q_index, k_index), update, unchanged, inner)

        q_start = jnp.zeros((span_len, kv_local, q_per_kv, head_dim), jnp.float32)
        q_acc, grad_k, grad_v = lax.fori_loop(0, q_index + 1, visit_key, (q_start, grad_k, grad_v))
        grad_q = lax.dynamic_update_slice_in_dim(grad_q, q_acc, q_index * span_len, 0)
        return (grad_q, grad_k, grad_v)

    empty = jnp.zeros((tokens_here, kv_local, q_per_kv, head_dim), jnp.float32)
    grad_q, grad_k, grad_v = lax.fori_loop(0, blocks, back_row, (empty, empty, empty))
    return (grad_q * factor, grad_k * factor, grad_v)


def on_device_wide(q_src, k_src, v_src, grad_src, doc_lengths, doc_groups, doc_offsets):
    grp_count = lax.axis_size("grp")
    sp_count = lax.axis_size("sp")
    unit_count = q_src.shape[0]
    slot_count = doc_lengths.shape[0]
    group_cap = slot_count // grp_count
    row_count = group_cap * grp_count
    unit_tok = grp_count * sp_count
    group_tok = row_count * sp_count
    head_dim = HEAD_DIM
    copies = max(1, sp_count // KV_HEADS)
    kv_local = max(1, KV_HEADS // sp_count)
    q_local = HEADS // sp_count
    q_per_kv = q_local // kv_local
    unit_ids = jnp.arange(unit_count, dtype=jnp.int32)
    starts = jnp.cumsum(doc_lengths) - doc_lengths
    inside = (
        (unit_ids[:, None] >= starts[None, :])
        & (unit_ids[:, None] < (starts + doc_lengths)[None, :])
    ).astype(jnp.int32)
    group_of = jnp.sum(inside * doc_groups[None, :], axis=1)
    place_of = jnp.sum(
        inside * (doc_offsets[None, :] + unit_ids[:, None] - starts[None, :]), axis=1
    )
    slot_of = group_of * group_cap + place_of
    slot_ids = jnp.arange(row_count, dtype=jnp.int32).reshape(grp_count, group_cap).T.reshape(-1)
    matches = (slot_of[None, :] == slot_ids[:, None]).astype(jnp.int32)
    source = jnp.sum(matches * unit_ids[None, :], axis=1)
    filled = jnp.sum(matches, axis=1) > 0

    def pack_rows(array):
        flat = array.reshape(unit_count, array.shape[-1])
        picked = jnp.take(flat, source, axis=0)
        picked = jnp.where(filled[:, None], picked, jnp.zeros_like(picked))
        return picked.reshape(group_cap, grp_count, array.shape[-1])

    arrived = (
        lax.all_to_all(pack_rows(q_src), "grp", split_axis=1, concat_axis=1, tiled=True),
        lax.all_to_all(pack_rows(k_src), "grp", split_axis=1, concat_axis=1, tiled=True),
        lax.all_to_all(pack_rows(v_src), "grp", split_axis=1, concat_axis=1, tiled=True),
        lax.all_to_all(pack_rows(grad_src), "grp", split_axis=1, concat_axis=1, tiled=True),
    )
    q_rows = arrived[0].reshape(row_count, 1, HEADS, head_dim)
    k_rows = arrived[1].reshape(row_count, KV_HEADS, head_dim)
    v_rows = arrived[2].reshape(row_count, KV_HEADS, head_dim)
    g_rows = arrived[3].reshape(row_count, 1, HEADS, head_dim)
    my_group = lax.axis_index("grp")
    unit_place = jnp.arange(group_cap, dtype=jnp.int32)
    member = (
        (doc_groups[None, :] == my_group)
        & (doc_lengths[None, :] > 0)
        & (doc_offsets[None, :] <= unit_place[:, None])
        & (unit_place[:, None] < (doc_offsets + doc_lengths)[None, :])
    ).astype(jnp.int32)
    first_unit = jnp.sum(member * doc_offsets[None, :], axis=1)
    occupied = jnp.sum(member, axis=1) > 0
    token_ids = jnp.arange(group_tok, dtype=jnp.int32)
    first_tok = jnp.where(
        jnp.repeat(occupied, unit_tok), jnp.repeat(first_unit * unit_tok, unit_tok), token_ids
    )
    k_wide = jnp.repeat(k_rows, copies, axis=1).reshape(row_count, 1, KV_HEADS * copies, head_dim)
    v_wide = jnp.repeat(v_rows, copies, axis=1).reshape(row_count, 1, KV_HEADS * copies, head_dim)
    q_back, g_back, k_back, v_back = (
        lax.all_to_all(q_rows, "sp", split_axis=2, concat_axis=1, tiled=True),
        lax.all_to_all(g_rows, "sp", split_axis=2, concat_axis=1, tiled=True),
        lax.all_to_all(k_wide, "sp", split_axis=2, concat_axis=1, tiled=True),
        lax.all_to_all(v_wide, "sp", split_axis=2, concat_axis=1, tiled=True),
    )
    k_heads = k_back.reshape(group_tok, kv_local, head_dim)
    v_heads = v_back.reshape(group_tok, kv_local, head_dim)
    q_heads = q_back.reshape(group_tok, kv_local, q_per_kv, head_dim)
    g_heads = g_back.reshape(group_tok, kv_local, q_per_kv, head_dim)
    grad_q, grad_k, grad_v = attend(q_heads, k_heads, v_heads, g_heads, first_tok)
    q_low = grad_q.astype(jnp.bfloat16).reshape(row_count, sp_count, q_local, head_dim)
    k_low = grad_k.astype(jnp.bfloat16)
    v_low = grad_v.astype(jnp.bfloat16)
    q_home, k_home, v_home = (
        lax.all_to_all(q_low, "sp", split_axis=1, concat_axis=2, tiled=True),
        lax.all_to_all(
            k_low.reshape(row_count, sp_count, q_local, head_dim),
            "sp",
            split_axis=1,
            concat_axis=2,
            tiled=True,
        ),
        lax.all_to_all(
            v_low.reshape(row_count, sp_count, q_local, head_dim),
            "sp",
            split_axis=1,
            concat_axis=2,
            tiled=True,
        ),
    )
    k_sum = halves_total(k_home.reshape(row_count, KV_HEADS, HEADS // KV_HEADS, head_dim))
    v_sum = halves_total(v_home.reshape(row_count, KV_HEADS, HEADS // KV_HEADS, head_dim))
    dk_out = k_sum.astype(jnp.bfloat16).reshape(1, row_count, 1, KV_HEADS * head_dim)
    dv_out = v_sum.astype(jnp.bfloat16).reshape(1, row_count, 1, KV_HEADS * head_dim)
    dq_out = q_home.reshape(1, row_count, 1, HEADS * head_dim)
    return (dq_out, dk_out, dv_out)


MESH = pl.DeviceIdType.MESH
STEP = 16
MAXDOC = 5
F32 = jnp.float32
BF16 = jnp.bfloat16


def dot_nt(left, right):
    return lax.dot_general(left, right, (((1,), (1,)), ((), ())), preferred_element_type=F32)


def dot_nn(left, right):
    return lax.dot_general(left, right, (((1,), (0,)), ((), ())), preferred_element_type=F32)


def lane_iota(rows, lanes):
    return lax.broadcasted_iota(jnp.int32, (rows, lanes), 1)


def row_iota(rows, lanes):
    return lax.broadcasted_iota(jnp.int32, (rows, lanes), 0)


def fused_kernel(
    n_grp,
    n_sp,
    tiles,
    full_grps,
    q_ref,
    k_ref,
    v_ref,
    g_ref,
    len_ref,
    grp_ref,
    off_ref,
    dq_ref,
    dk_ref,
    dv_ref,
    send,
    recv,
    home_q,
    home_k,
    home_v,
    order,
    bias,
    halo_bias,
    halo_kv,
    k_turned,
    halo_turned,
    d_acc,
    halo_acc,
    send_sem,
    recv_sem,
    own_sem,
    hq_send,
    hq_recv,
    hq_own,
    hk_send,
    hk_recv,
    hk_own,
    hv_send,
    hv_recv,
    hv_own,
):
    my_grp = lax.axis_index("grp")
    my_sp = lax.axis_index("sp")
    peers = n_grp * n_sp
    me = my_grp * n_sp + my_sp
    units = q_ref.shape[0]
    q_wide = q_ref.shape[1] // n_sp
    heads = q_wide // HEAD_DIM
    cap = tiles * STEP
    tile_tok = peers * STEP
    halo = MAXDOC - 1
    halo_tok = peers * halo
    factor = HEAD_DIM ** (-0.5)
    row_wide = 2 * HEAD_DIM * (heads + 1)
    last = tiles - 1
    kv_lanes = pl.ds(0, 2 * HEAD_DIM)

    barrier = pltpu.get_barrier_semaphore()

    @pl.loop(1, peers)
    def _(hop):
        there = {
            "grp": lax.rem(my_grp + hop // n_sp, n_grp),
            "sp": lax.rem(my_sp + lax.rem(hop, n_sp), n_sp),
        }
        pl.semaphore_signal(barrier, inc=1, device_id=there, device_id_type=MESH)

    slots = len_ref.shape[1]
    which = row_iota(8, slots)
    tables = jnp.where(
        which == 0, len_ref[...], jnp.where(which == 1, grp_ref[...], jnp.where(which == 2, off_ref[...], 0))
    )
    tables = tables.astype(F32).astype(BF16)
    down, across = row_iota(slots, slots), lane_iota(slots, slots)
    columns = dot_nt((down == across).astype(F32).astype(BF16), tables)
    length, group, offset = columns[:, 0:1], columns[:, 1:2], columns[:, 2:3]
    start = dot_nt((across < down).astype(F32).astype(BF16), tables)[:, 0:1]
    unit = lane_iota(1, units).astype(F32)
    inside = (unit >= start) & (unit < start + length)
    slot_of = unit + jnp.sum(
        jnp.where(inside, group * cap + offset - start, 0.0), axis=0, keepdims=True
    )

    def pack(tile):
        row = row_iota(n_grp * STEP, 1)
        slot = (row // STEP) * cap + tile * STEP + lax.rem(row, STEP)
        hot = (slot.astype(F32) == slot_of).astype(F32).astype(BF16)

        def put(to, at, ref, lane, wide):
            part = dot_nn(hot, ref[:, lane : lane + wide]).astype(BF16).reshape(n_grp, STEP, wide)
            for grp in range(n_grp):
                send[tile, grp * n_sp + to, :, at : at + wide] = part[grp]

        for to in range(n_sp):
            put(to, 0, k_ref, to * HEAD_DIM, HEAD_DIM)
            put(to, HEAD_DIM, v_ref, to * HEAD_DIM, HEAD_DIM)
            for head in range(heads):
                lane = to * q_wide + head * HEAD_DIM
                put(to, 2 * HEAD_DIM * (head + 1), q_ref, lane, HEAD_DIM)
                put(to, 2 * HEAD_DIM * (head + 1) + HEAD_DIM, g_ref, lane, HEAD_DIM)

    def push(tile, lanes, sem, to_grp, to_sp):
        pltpu.make_async_remote_copy(
            src_ref=send.at[tile, to_grp * n_sp + to_sp, :, lanes],
            dst_ref=recv.at[tile, me, :, lanes],
            send_sem=send_sem.at[sem],
            recv_sem=recv_sem.at[sem],
            device_id={"grp": to_grp, "sp": to_sp},
            device_id_type=MESH,
        ).start()

    half = n_grp // 2

    def scatter(tile, lane, wide, sem):
        @pl.loop(0, peers)
        def _(hop):
            to_grp = lax.rem(my_grp + half + hop, n_grp)
            to_sp = lax.rem(my_sp + hop // n_grp, n_sp)

            @pl.when((to_grp != my_grp) | (to_sp != my_sp))
            def _():
                push(tile, pl.ds(lane, wide), sem, to_grp, to_sp)

    def landed(tile, lane, wide, sem):
        block = recv.at[tile, pl.ds(0, peers - 1), :, pl.ds(lane, wide)]
        pltpu.make_async_copy(block, block, recv_sem.at[sem]).wait()

    def own_block(tile):
        return pltpu.make_async_copy(send.at[tile, me], recv.at[tile, me], own_sem.at[tile])

    pair = 2 * HEAD_DIM
    takes_last = sum(((my_grp == grp).astype(jnp.int32) for grp in full_grps), jnp.int32(0)) > 0

    pack(last)
    pl.semaphore_wait(barrier, peers - 1)
    if len(full_grps) == n_grp:
        scatter(last, 0, row_wide, last)
    else:

        @pl.loop(0, n_sp)
        def _(hop):
            for to_grp in full_grps:

                @pl.when((my_grp != to_grp) | (hop > 0))
                def _():
                    push(last, pl.ds(0, row_wide), last, to_grp, lax.rem(my_sp + hop, n_sp))

    for tile in range(last - 1, 0, -1):
        pack(tile)
        scatter(tile, 0, pair, tile)
        scatter(tile, pair, row_wide - pair, tiles + heads + tile)
    pack(0)
    scatter(0, 0, pair, 0)
    for head in range(heads):
        scatter(0, (head + 1) * pair, pair, tiles + head)
    for tile in range(last):
        own_block(tile).start()

    @pl.when(takes_last)
    def _():
        own_block(last).start()

    @pl.when(jnp.logical_not(takes_last))
    def _():
        recv[last] = jnp.zeros(recv.shape[1:], BF16)

    d_acc[...] = jnp.zeros_like(d_acc)
    to_row = row_iota(tile_tok, 1)
    out_rows = n_grp * STEP
    of_row = (
        (lax.rem(to_row, n_grp) * n_sp + to_row // out_rows) * STEP + lax.rem(to_row, out_rows) // n_grp
    )
    order[...] = (of_row == lane_iota(1, tile_tok)).astype(F32).astype(BF16)

    def go_home(here, out, tile, lane, sends, recvs, own):
        wide = here.shape[-1]
        there = out.at[pl.ds(tile * out_rows, out_rows), pl.ds(pl.multiple_of(lane, HEAD_DIM), wide)]

        @pl.loop(1, n_sp)
        def _(hop):
            to_sp = lax.rem(my_sp + hop, n_sp)
            pltpu.make_async_remote_copy(
                src_ref=here.at[to_sp],
                dst_ref=there,
                send_sem=sends,
                recv_sem=recvs,
                device_id={"grp": my_grp, "sp": to_sp},
                device_id_type=MESH,
            ).start()

        pltpu.make_async_copy(here.at[my_sp], there, own).start()

    def kv_home(tile):
        shape = (n_sp, out_rows, HEAD_DIM)
        d_key = (d_acc[tile, :, :HEAD_DIM] * factor).astype(BF16)
        home_k[tile] = dot_nn(order[...], d_key).astype(BF16).reshape(shape)
        lane = my_sp * HEAD_DIM
        go_home(home_k.at[tile], dk_ref, tile, lane, hk_send.at[tile], hk_recv.at[tile], hk_own.at[tile])
        d_val = d_acc[tile, :, HEAD_DIM:].astype(BF16)
        home_v[tile] = dot_nn(order[...], d_val).astype(BF16).reshape(shape)
        go_home(home_v.at[tile], dv_ref, tile, lane, hv_send.at[tile], hv_recv.at[tile], hv_own.at[tile])

    halo_row = row_iota(halo_tok, 1)
    halo_from = (halo_row // halo) * STEP + STEP - halo + lax.rem(halo_row, halo)
    cut = (halo_from == lane_iota(1, tile_tok)).astype(F32).astype(BF16)
    row = row_iota(tile_tok, 1)
    halo_lane = lane_iota(1, halo_tok)
    paste = (
        row == (halo_lane // halo) * STEP + STEP - halo + lax.rem(halo_lane, halo)
    ).astype(F32)

    @pl.when(takes_last)
    def _():
        own_block(last).wait()
        landed(last, 0, row_wide, last)

    for tile in range(last, -1, -1):
        lane = lane_iota(1, tile_tok)
        q_block = tile * STEP + lax.rem(lane, STEP)
        q_pos = q_block * peers + lane // STEP
        place = q_block.astype(F32)
        member = (
            (group == my_grp.astype(F32))
            & (length > 0.0)
            & (offset <= place)
            & (place < offset + length)
        )
        first = jnp.sum(jnp.where(member, offset * peers, 0.0), axis=0, keepdims=True)
        occupied = jnp.sum(jnp.where(member, 1.0, 0.0), axis=0, keepdims=True) > 0.0
        first = jnp.where(occupied, first, q_pos.astype(F32)).astype(jnp.int32)
        k_pos = (tile * STEP + lax.rem(row, STEP)) * peers + row // STEP
        bias[...] = jnp.where((k_pos <= q_pos) & (k_pos >= first), 0.0, NEG_FILL)
        if tile > 0:
            if tile < last:
                landed(tile, pair, row_wide - pair, tiles + heads + tile)
            own_block(tile - 1).wait()
            landed(tile - 1, 0, pair, tile - 1)
            halo_pos = (tile * STEP - halo + lax.rem(halo_row, halo)) * peers + halo_row // halo
            halo_bias[...] = jnp.where(halo_pos >= first, 0.0, NEG_FILL)
            kv_before = recv[tile - 1, :, :, : 2 * HEAD_DIM].reshape(tile_tok, 2 * HEAD_DIM)
            kv_cut = dot_nn(cut, kv_before)
            halo_kv[...] = kv_cut.astype(BF16)
            halo_turned[...] = kv_cut[:, :HEAD_DIM].T.astype(BF16)
            halo_acc[...] = jnp.zeros_like(halo_acc)

        k_turned[...] = (
            recv[tile, :, :, :HEAD_DIM].reshape(tile_tok, HEAD_DIM).astype(F32).T.astype(BF16)
        )

        @pl.loop(0, heads)
        def _(head):
            if tile == 0:
                landed(0, pair, pair, tiles + head)

            at = pl.multiple_of(head * HEAD_DIM, HEAD_DIM)
            q_at = pl.multiple_of((head + 1) * pair, HEAD_DIM)
            g_at = pl.multiple_of((head + 1) * pair + HEAD_DIM, HEAD_DIM)
            q_head = recv[tile, :, :, pl.ds(q_at, HEAD_DIM)].reshape(tile_tok, HEAD_DIM)
            g_head = recv[tile, :, :, pl.ds(g_at, HEAD_DIM)].reshape(tile_tok, HEAD_DIM)
            keys = [recv[tile, :, :, :HEAD_DIM].reshape(tile_tok, HEAD_DIM)]
            vals = [recv[tile, :, :, HEAD_DIM : 2 * HEAD_DIM].reshape(tile_tok, HEAD_DIM)]
            masks = [bias]
            turned = [k_turned]
            if tile > 0:
                keys.append(halo_kv[:, :HEAD_DIM])
                vals.append(halo_kv[:, HEAD_DIM:])
                masks.append(halo_bias)
                turned.append(halo_turned)
            logits = [dot_nt(key, q_head) * factor + mask[...] for key, mask in zip(keys, masks)]
            high = jnp.max(logits[0], axis=0, keepdims=True)
            for part in logits[1:]:
                high = jnp.maximum(high, jnp.max(part, axis=0, keepdims=True))
            probs = [jnp.exp(part - high) for part in logits]
            mass = sum(jnp.sum(part, axis=0, keepdims=True) for part in probs)
            scale = 1.0 / mass
            probs = [part * scale for part in probs]
            d_probs = [dot_nt(val, g_head) for val in vals]
            delta = sum(
                jnp.sum(part * d_part, axis=0, keepdims=True) for part, d_part in zip(probs, d_probs)
            )
            dq_turned = jnp.zeros((HEAD_DIM, tile_tok), F32)
            for n in range(len(keys)):
                d_logits = (probs[n] * (d_probs[n] - delta)).astype(BF16)
                d_key = dot_nn(d_logits, q_head)
                d_val = dot_nn(probs[n].astype(BF16), g_head)
                if n == 0:
                    d_acc[tile, :, :HEAD_DIM] += d_key
                    d_acc[tile, :, HEAD_DIM:] += d_val
                else:
                    halo_acc[:, :HEAD_DIM] += d_key
                    halo_acc[:, HEAD_DIM:] += d_val
                dq_turned += dot_nn(turned[n][...], d_logits)
            dq_head = dot_nt(order[...], (dq_turned * factor).astype(BF16)).astype(BF16)
            lanes = pl.ds(at, HEAD_DIM)
            home_q[tile, :, :, lanes] = dq_head.reshape(n_sp, out_rows, HEAD_DIM)
            if tile == 0:
                go_home(
                    home_q.at[0, :, :, lanes],
                    dq_ref,
                    0,
                    my_sp * q_wide + head * HEAD_DIM,
                    hq_send.at[last + head],
                    hq_recv.at[last + head],
                    hq_own.at[last + head],
                )

        if tile > 0:
            go_home(
                home_q.at[tile],
                dq_ref,
                tile,
                my_sp * q_wide,
                hq_send.at[tile - 1],
                hq_recv.at[tile - 1],
                hq_own.at[tile - 1],
            )
        kv_home(tile)
        if tile > 0:
            d_acc[tile - 1] += lax.dot_general(
                paste,
                halo_acc[...],
                (((1,), (0,)), ((), ())),
                precision=lax.Precision.HIGHEST,
                preferred_element_type=F32,
            )

    def settle(block, sem):
        pltpu.make_async_copy(block, block, sem).wait()

    def settle_home(here, sends, recvs, own):
        away = here.at[pl.ds(0, n_sp - 1)]
        settle(here.at[0], own)
        settle(away, sends)
        settle(away, recvs)

    def settle_sent(tile, lane, wide, count, sem):
        settle(send.at[tile, pl.ds(0, count), :, pl.ds(lane, wide)], send_sem.at[sem])

    for tile in range(tiles):
        settle_home(home_k.at[tile], hk_send.at[tile], hk_recv.at[tile], hk_own.at[tile])
        settle_home(home_v.at[tile], hv_send.at[tile], hv_recv.at[tile], hv_own.at[tile])
    for n in range(last):
        settle_home(home_q.at[n + 1], hq_send.at[n], hq_recv.at[n], hq_own.at[n])
    for head in range(heads):
        n = last + head
        settle_home(home_q.at[0, :, :, pl.ds(0, HEAD_DIM)], hq_send.at[n], hq_recv.at[n], hq_own.at[n])
        settle_sent(0, 0, pair, peers - 1, tiles + head)
    settle_sent(0, 0, pair, peers - 1, 0)
    for tile in range(1, last):
        settle_sent(tile, 0, pair, peers - 1, tile)
        settle_sent(tile, pair, row_wide - pair, peers - 1, tiles + heads + tile)

    @pl.when(takes_last)
    def _():
        settle_sent(last, 0, row_wide, len(full_grps) * n_sp - 1, last)

    if len(full_grps) < n_grp:

        @pl.when(jnp.logical_not(takes_last))
        def _():
            settle_sent(last, 0, row_wide, len(full_grps) * n_sp, last)


def result_kernel(*refs):
    sources, results, held = refs[:3], refs[3:6], refs[6:9]
    load_sem, store_sem = refs[9:]
    rows = held[0].shape[0]
    cuts = [(0, pl.ds(n * rows // 4, rows // 4)) for n in range(4)] + [(1, pl.ds(0, rows)), (2, pl.ds(0, rows))]
    loads = [
        pltpu.make_async_copy(sources[n].at[cut], held[n].at[cut], load_sem.at[i])
        for i, (n, cut) in enumerate(cuts)
    ]
    stores = [
        pltpu.make_async_copy(held[n].at[cut], results[n].at[cut], store_sem.at[i])
        for i, (n, cut) in enumerate(cuts)
    ]
    for load in loads:
        load.start()
    for load, store in zip(loads, stores):
        load.wait()
        store.start()
    for store in stores:
        store.wait()


def on_device_fused(q_src, k_src, v_src, grad_src, doc_lengths, doc_groups, doc_offsets):
    n_grp = lax.axis_size("grp")
    n_sp = lax.axis_size("sp")
    units = q_src.shape[0]
    slots = doc_lengths.shape[0]
    cap = slots // n_grp
    tiles = cap // STEP
    peers = n_grp * n_sp
    q_all = q_src.shape[-1]
    kv_all = k_src.shape[-1]
    q_wide = q_all // n_sp
    heads = q_wide // HEAD_DIM
    row_wide = 2 * HEAD_DIM * (heads + 1)
    tile_tok = peers * STEP
    halo_tok = peers * (MAXDOC - 1)
    out_rows = n_grp * STEP
    rows = cap * n_grp
    shapes = (
        jax.ShapeDtypeStruct((rows, q_all), BF16),
        jax.ShapeDtypeStruct((rows, kv_all), BF16),
        jax.ShapeDtypeStruct((rows, kv_all), BF16),
    )
    vmem = pl.BlockSpec(memory_space=pltpu.VMEM)
    hbm = pl.BlockSpec(memory_space=pl.ANY)
    dma = pltpu.SemaphoreType.DMA

    def run(full_grps, number):
        return pl.pallas_call(
            lambda *refs: fused_kernel(n_grp, n_sp, tiles, full_grps, *refs),
            out_shape=shapes,
            in_specs=[vmem] * 7,
            out_specs=(hbm,) * 3,
            scratch_shapes=[
                pltpu.VMEM((tiles, peers, STEP, row_wide), BF16),
                pltpu.VMEM((tiles, peers, STEP, row_wide), BF16),
                pltpu.VMEM((tiles, n_sp, out_rows, q_wide), BF16),
                pltpu.VMEM((tiles, n_sp, out_rows, HEAD_DIM), BF16),
                pltpu.VMEM((tiles, n_sp, out_rows, HEAD_DIM), BF16),
                pltpu.VMEM((tile_tok, tile_tok), BF16),
                pltpu.VMEM((tile_tok, tile_tok), F32),
                pltpu.VMEM((halo_tok, tile_tok), F32),
                pltpu.VMEM((halo_tok, 2 * HEAD_DIM), BF16),
                pltpu.VMEM((HEAD_DIM, tile_tok), BF16),
                pltpu.VMEM((HEAD_DIM, halo_tok), BF16),
                pltpu.VMEM((tiles, tile_tok, 2 * HEAD_DIM), F32),
                pltpu.VMEM((halo_tok, 2 * HEAD_DIM), F32),
                dma((2 * tiles + heads,)),
                dma((2 * tiles + heads,)),
                dma((tiles,)),
                dma((tiles - 1 + heads,)),
                dma((tiles - 1 + heads,)),
                dma((tiles - 1 + heads,)),
            ]
            + [dma((tiles,))] * 6,
            compiler_params=pltpu.CompilerParams(
                collective_id=number, has_side_effects=True, vmem_limit_bytes=56 * 1024 * 1024
            ),
        )(
            q_src.reshape(units, q_all),
            k_src.reshape(units, kv_all),
            v_src.reshape(units, kv_all),
            grad_src.reshape(units, q_all),
            doc_lengths.reshape(1, slots),
            doc_groups.reshape(1, slots),
            doc_offsets.reshape(1, slots),
        )

    passed = run(tuple(range(n_grp)), 0)
    dq, dk, dv = pl.pallas_call(
        result_kernel,
        out_shape=shapes,
        in_specs=[hbm] * 3,
        out_specs=(hbm,) * 3,
        scratch_shapes=[pltpu.VMEM(shape.shape, BF16) for shape in shapes] + [dma((6,)), dma((6,))],
        compiler_params=pltpu.CompilerParams(vmem_limit_bytes=56 * 1024 * 1024),
    )(*passed)
    return (
        dq.reshape(1, rows, 1, q_all),
        dk.reshape(1, rows, 1, kv_all),
        dv.reshape(1, rows, 1, kv_all),
    )


def on_device(q_src, k_src, v_src, grad_src, doc_lengths, doc_groups, doc_offsets):
    n_grp = lax.axis_size("grp")
    cap = doc_lengths.shape[0] // n_grp
    fits = lax.axis_size("sp") == KV_HEADS and cap % STEP == 0 and cap > STEP and n_grp % 2 == 0
    chosen = on_device_fused if fits else on_device_wide
    return chosen(q_src, k_src, v_src, grad_src, doc_lengths, doc_groups, doc_offsets)


def solution(mesh):
    placed = (
        P(None, "grp", "sp", None),
        P(None, "grp", "sp", None),
        P(None, "grp", "sp", None),
        P(None, "grp", "sp", None),
        P(),
        P(),
        P(),
    )
    return jax.shard_map(
        on_device,
        mesh=mesh,
        in_specs=placed,
        out_specs=(
            P("grp", None, "sp", None),
            P("grp", None, "sp", None),
            P("grp", None, "sp", None),
        ),
        check_vma=False,
    )
```

```python
import math

import jax
import jax.numpy as jnp
from jax import lax
from jax.experimental import pallas as pl
from jax.experimental.pallas import tpu as pltpu
from jax.sharding import PartitionSpec as P

HEADS = 32
KV_HEADS = 8
HEAD_DIM = 128


NEG_FILL = -1e30


def unchanged(passed):
    return passed


def collapse(array):
    rounded = lax.optimization_barrier(array)
    return jnp.sum(rounded.astype(jnp.float32), axis=2)


def pair_fold(low_part, high_part):
    return lax.optimization_barrier(
        (low_part.astype(jnp.float32) + high_part.astype(jnp.float32)).astype(jnp.bfloat16)
    )


def halves_total(array):
    half = array.shape[2] // 2
    return collapse(pair_fold(array[:, :, :half], array[:, :, half:]))


def attend(q_heads, k_heads, v_heads, g_heads, first_tok):
    tokens_here, kv_local, q_per_kv, head_dim = q_heads.shape
    span_len = math.gcd(tokens_here, 512)
    blocks = tokens_here // span_len
    factor = head_dim ** (-0.5)
    lane_pos = jnp.arange(span_len, dtype=jnp.int32)
    block_low = jnp.min(first_tok.reshape(blocks, span_len), axis=1)
    heads_shape = (kv_local, q_per_kv, span_len)

    def cut_block(array, index):
        return lax.dynamic_slice_in_dim(array, index * span_len, span_len, 0)

    def pair_logits(q_block, first_q, q_index, k_index):
        k_block = cut_block(k_heads, k_index)
        logits = (
            jnp.einsum("qjih,kjh->jiqk", q_block, k_block, preferred_element_type=jnp.float32)
            * factor
        )
        q_pos = q_index * span_len + lane_pos
        k_pos = k_index * span_len + lane_pos
        allowed = (k_pos[None, :] <= q_pos[:, None]) & (k_pos[None, :] >= first_q[:, None])
        return (logits, allowed)

    def is_live(q_index, k_index):
        return block_low[q_index] <= k_index * span_len + span_len - 1

    def row_norm(q_index):
        q_block = cut_block(q_heads, q_index)
        first_q = cut_block(first_tok, q_index)

        def visit_key(k_index, running):

            def update(running):
                row_high, row_mass = running
                logits, allowed = pair_logits(q_block, first_q, q_index, k_index)
                logits = jnp.where(allowed, logits, NEG_FILL)
                new_high = jnp.maximum(row_high, jnp.max(logits, axis=-1))
                row_mass = row_mass * jnp.exp(row_high - new_high) + jnp.sum(
                    jnp.where(allowed, jnp.exp(logits - new_high[..., None]), 0.0), axis=-1
                )
                return (new_high, row_mass)

            return lax.cond(is_live(q_index, k_index), update, unchanged, running)

        initial = (
            jnp.full(heads_shape, NEG_FILL, jnp.float32),
            jnp.zeros(heads_shape, jnp.float32),
        )
        row_high, row_mass = lax.fori_loop(0, q_index + 1, visit_key, initial)
        return row_high + jnp.log(row_mass)

    log_norm = lax.map(row_norm, jnp.arange(blocks, dtype=jnp.int32))

    def row_delta(q_index):
        q_block = cut_block(q_heads, q_index)
        first_q = cut_block(first_tok, q_index)
        norm_row = log_norm[q_index]

        def visit_key(k_index, acc_out):

            def update(acc_out):
                logits, allowed = pair_logits(q_block, first_q, q_index, k_index)
                weights = jnp.where(allowed, jnp.exp(logits - norm_row[..., None]), 0.0).astype(
                    jnp.bfloat16
                )
                v_block = cut_block(v_heads, k_index)
                return acc_out + jnp.einsum(
                    "jiqk,kjh->jiqh", weights, v_block, preferred_element_type=jnp.float32
                )

            return lax.cond(is_live(q_index, k_index), update, unchanged, acc_out)

        acc_out = lax.fori_loop(
            0, q_index + 1, visit_key, jnp.zeros(heads_shape + (head_dim,), jnp.float32)
        )
        g_block = cut_block(g_heads, q_index)
        return jnp.einsum("jiqh,qjih->jiq", acc_out, g_block, preferred_element_type=jnp.float32)

    delta_all = lax.map(row_delta, jnp.arange(blocks, dtype=jnp.int32))

    def back_row(q_index, carried):
        grad_q, grad_k, grad_v = carried
        q_block = cut_block(q_heads, q_index)
        g_block = cut_block(g_heads, q_index)
        first_q = cut_block(first_tok, q_index)
        norm_row = log_norm[q_index]
        delta_row = delta_all[q_index]

        def visit_key(k_index, inner):

            def update(inner):
                q_acc, grad_k, grad_v = inner
                logits, allowed = pair_logits(q_block, first_q, q_index, k_index)
                probs = jnp.where(allowed, jnp.exp(logits - norm_row[..., None]), 0.0)
                probs_low = probs.astype(jnp.bfloat16)
                k_block = cut_block(k_heads, k_index)
                v_block = cut_block(v_heads, k_index)
                d_probs = jnp.einsum(
                    "qjih,kjh->jiqk", g_block, v_block, preferred_element_type=jnp.float32
                )
                d_logits = (probs * (d_probs - delta_row[..., None])).astype(jnp.bfloat16)
                q_acc = q_acc + jnp.einsum(
                    "jiqk,kjh->qjih", d_logits, k_block, preferred_element_type=jnp.float32
                )
                k_part = jnp.einsum(
                    "jiqk,qjih->kjih", d_logits, q_block, preferred_element_type=jnp.float32
                )
                v_part = jnp.einsum(
                    "jiqk,qjih->kjih", probs_low, g_block, preferred_element_type=jnp.float32
                )
                at_row = k_index * span_len
                grad_k = lax.dynamic_update_slice_in_dim(
                    grad_k, cut_block(grad_k, k_index) + k_part, at_row, 0
                )
                grad_v = lax.dynamic_update_slice_in_dim(
                    grad_v, cut_block(grad_v, k_index) + v_part, at_row, 0
                )
                return (q_acc, grad_k, grad_v)

            return lax.cond(is_live(q_index, k_index), update, unchanged, inner)

        q_start = jnp.zeros((span_len, kv_local, q_per_kv, head_dim), jnp.float32)
        q_acc, grad_k, grad_v = lax.fori_loop(0, q_index + 1, visit_key, (q_start, grad_k, grad_v))
        grad_q = lax.dynamic_update_slice_in_dim(grad_q, q_acc, q_index * span_len, 0)
        return (grad_q, grad_k, grad_v)

    empty = jnp.zeros((tokens_here, kv_local, q_per_kv, head_dim), jnp.float32)
    grad_q, grad_k, grad_v = lax.fori_loop(0, blocks, back_row, (empty, empty, empty))
    return (grad_q * factor, grad_k * factor, grad_v)


def on_device_wide(q_src, k_src, v_src, grad_src, doc_lengths, doc_groups, doc_offsets):
    grp_count = lax.axis_size("grp")
    sp_count = lax.axis_size("sp")
    unit_count = q_src.shape[0]
    slot_count = doc_lengths.shape[0]
    group_cap = slot_count // grp_count
    row_count = group_cap * grp_count
    unit_tok = grp_count * sp_count
    group_tok = row_count * sp_count
    head_dim = HEAD_DIM
    copies = max(1, sp_count // KV_HEADS)
    kv_local = max(1, KV_HEADS // sp_count)
    q_local = HEADS // sp_count
    q_per_kv = q_local // kv_local
    unit_ids = jnp.arange(unit_count, dtype=jnp.int32)
    starts = jnp.cumsum(doc_lengths) - doc_lengths
    inside = (
        (unit_ids[:, None] >= starts[None, :])
        & (unit_ids[:, None] < (starts + doc_lengths)[None, :])
    ).astype(jnp.int32)
    group_of = jnp.sum(inside * doc_groups[None, :], axis=1)
    place_of = jnp.sum(
        inside * (doc_offsets[None, :] + unit_ids[:, None] - starts[None, :]), axis=1
    )
    slot_of = group_of * group_cap + place_of
    slot_ids = jnp.arange(row_count, dtype=jnp.int32).reshape(grp_count, group_cap).T.reshape(-1)
    matches = (slot_of[None, :] == slot_ids[:, None]).astype(jnp.int32)
    source = jnp.sum(matches * unit_ids[None, :], axis=1)
    filled = jnp.sum(matches, axis=1) > 0

    def pack_rows(array):
        flat = array.reshape(unit_count, array.shape[-1])
        picked = jnp.take(flat, source, axis=0)
        picked = jnp.where(filled[:, None], picked, jnp.zeros_like(picked))
        return picked.reshape(group_cap, grp_count, array.shape[-1])

    arrived = (
        lax.all_to_all(pack_rows(q_src), "grp", split_axis=1, concat_axis=1, tiled=True),
        lax.all_to_all(pack_rows(k_src), "grp", split_axis=1, concat_axis=1, tiled=True),
        lax.all_to_all(pack_rows(v_src), "grp", split_axis=1, concat_axis=1, tiled=True),
        lax.all_to_all(pack_rows(grad_src), "grp", split_axis=1, concat_axis=1, tiled=True),
    )
    q_rows = arrived[0].reshape(row_count, 1, HEADS, head_dim)
    k_rows = arrived[1].reshape(row_count, KV_HEADS, head_dim)
    v_rows = arrived[2].reshape(row_count, KV_HEADS, head_dim)
    g_rows = arrived[3].reshape(row_count, 1, HEADS, head_dim)
    my_group = lax.axis_index("grp")
    unit_place = jnp.arange(group_cap, dtype=jnp.int32)
    member = (
        (doc_groups[None, :] == my_group)
        & (doc_lengths[None, :] > 0)
        & (doc_offsets[None, :] <= unit_place[:, None])
        & (unit_place[:, None] < (doc_offsets + doc_lengths)[None, :])
    ).astype(jnp.int32)
    first_unit = jnp.sum(member * doc_offsets[None, :], axis=1)
    occupied = jnp.sum(member, axis=1) > 0
    token_ids = jnp.arange(group_tok, dtype=jnp.int32)
    first_tok = jnp.where(
        jnp.repeat(occupied, unit_tok), jnp.repeat(first_unit * unit_tok, unit_tok), token_ids
    )
    k_wide = jnp.repeat(k_rows, copies, axis=1).reshape(row_count, 1, KV_HEADS * copies, head_dim)
    v_wide = jnp.repeat(v_rows, copies, axis=1).reshape(row_count, 1, KV_HEADS * copies, head_dim)
    q_back, g_back, k_back, v_back = (
        lax.all_to_all(q_rows, "sp", split_axis=2, concat_axis=1, tiled=True),
        lax.all_to_all(g_rows, "sp", split_axis=2, concat_axis=1, tiled=True),
        lax.all_to_all(k_wide, "sp", split_axis=2, concat_axis=1, tiled=True),
        lax.all_to_all(v_wide, "sp", split_axis=2, concat_axis=1, tiled=True),
    )
    k_heads = k_back.reshape(group_tok, kv_local, head_dim)
    v_heads = v_back.reshape(group_tok, kv_local, head_dim)
    q_heads = q_back.reshape(group_tok, kv_local, q_per_kv, head_dim)
    g_heads = g_back.reshape(group_tok, kv_local, q_per_kv, head_dim)
    grad_q, grad_k, grad_v = attend(q_heads, k_heads, v_heads, g_heads, first_tok)
    q_low = grad_q.astype(jnp.bfloat16).reshape(row_count, sp_count, q_local, head_dim)
    k_low = grad_k.astype(jnp.bfloat16)
    v_low = grad_v.astype(jnp.bfloat16)
    q_home, k_home, v_home = (
        lax.all_to_all(q_low, "sp", split_axis=1, concat_axis=2, tiled=True),
        lax.all_to_all(
            k_low.reshape(row_count, sp_count, q_local, head_dim),
            "sp",
            split_axis=1,
            concat_axis=2,
            tiled=True,
        ),
        lax.all_to_all(
            v_low.reshape(row_count, sp_count, q_local, head_dim),
            "sp",
            split_axis=1,
            concat_axis=2,
            tiled=True,
        ),
    )
    k_sum = halves_total(k_home.reshape(row_count, KV_HEADS, HEADS // KV_HEADS, head_dim))
    v_sum = halves_total(v_home.reshape(row_count, KV_HEADS, HEADS // KV_HEADS, head_dim))
    dk_out = k_sum.astype(jnp.bfloat16).reshape(1, row_count, 1, KV_HEADS * head_dim)
    dv_out = v_sum.astype(jnp.bfloat16).reshape(1, row_count, 1, KV_HEADS * head_dim)
    dq_out = q_home.reshape(1, row_count, 1, HEADS * head_dim)
    return (dq_out, dk_out, dv_out)


MESH = pl.DeviceIdType.MESH
STEP = 16
MAXDOC = 5
F32 = jnp.float32
BF16 = jnp.bfloat16


def dot_nt(left, right):
    return lax.dot_general(left, right, (((1,), (1,)), ((), ())), preferred_element_type=F32)


def dot_nn(left, right):
    return lax.dot_general(left, right, (((1,), (0,)), ((), ())), preferred_element_type=F32)


def lane_iota(rows, lanes):
    return lax.broadcasted_iota(jnp.int32, (rows, lanes), 1)


def row_iota(rows, lanes):
    return lax.broadcasted_iota(jnp.int32, (rows, lanes), 0)


def fused_kernel(
    n_grp,
    n_sp,
    tiles,
    full_grps,
    q_ref,
    k_ref,
    v_ref,
    g_ref,
    len_ref,
    grp_ref,
    off_ref,
    dq_ref,
    dk_ref,
    dv_ref,
    send,
    recv,
    home_q,
    home_k,
    home_v,
    order,
    bias,
    halo_bias,
    halo_kv,
    k_turned,
    halo_turned,
    d_acc,
    halo_acc,
    send_sem,
    recv_sem,
    own_sem,
    hq_send,
    hq_recv,
    hq_own,
    hk_send,
    hk_recv,
    hk_own,
    hv_send,
    hv_recv,
    hv_own,
):
    my_grp = lax.axis_index("grp")
    my_sp = lax.axis_index("sp")
    peers = n_grp * n_sp
    me = my_grp * n_sp + my_sp
    units = q_ref.shape[0]
    q_wide = q_ref.shape[1] // n_sp
    heads = q_wide // HEAD_DIM
    cap = tiles * STEP
    tile_tok = peers * STEP
    halo = MAXDOC - 1
    halo_tok = peers * halo
    factor = HEAD_DIM ** (-0.5)
    row_wide = 2 * HEAD_DIM * (heads + 1)
    last = tiles - 1
    kv_lanes = pl.ds(0, 2 * HEAD_DIM)

    barrier = pltpu.get_barrier_semaphore()

    @pl.loop(1, peers)
    def _(hop):
        there = {
            "grp": lax.rem(my_grp + hop // n_sp, n_grp),
            "sp": lax.rem(my_sp + lax.rem(hop, n_sp), n_sp),
        }
        pl.semaphore_signal(barrier, inc=1, device_id=there, device_id_type=MESH)

    slots = len_ref.shape[1]
    which = row_iota(8, slots)
    tables = jnp.where(
        which == 0, len_ref[...], jnp.where(which == 1, grp_ref[...], jnp.where(which == 2, off_ref[...], 0))
    )
    tables = tables.astype(F32).astype(BF16)
    down, across = row_iota(slots, slots), lane_iota(slots, slots)
    columns = dot_nt((down == across).astype(F32).astype(BF16), tables)
    length, group, offset = columns[:, 0:1], columns[:, 1:2], columns[:, 2:3]
    start = dot_nt((across < down).astype(F32).astype(BF16), tables)[:, 0:1]
    unit = lane_iota(1, units).astype(F32)
    inside = (unit >= start) & (unit < start + length)
    slot_of = unit + jnp.sum(
        jnp.where(inside, group * cap + offset - start, 0.0), axis=0, keepdims=True
    )

    def pack(tile):
        row = row_iota(n_grp * STEP, 1)
        slot = (row // STEP) * cap + tile * STEP + lax.rem(row, STEP)
        hot = (slot.astype(F32) == slot_of).astype(F32).astype(BF16)

        def put(to, at, ref, lane, wide):
            part = dot_nn(hot, ref[:, lane : lane + wide]).astype(BF16).reshape(n_grp, STEP, wide)
            for grp in range(n_grp):
                send[tile, grp * n_sp + to, :, at : at + wide] = part[grp]

        for to in range(n_sp):
            put(to, 0, k_ref, to * HEAD_DIM, HEAD_DIM)
            put(to, HEAD_DIM, v_ref, to * HEAD_DIM, HEAD_DIM)
            for head in range(heads):
                lane = to * q_wide + head * HEAD_DIM
                put(to, 2 * HEAD_DIM * (head + 1), q_ref, lane, HEAD_DIM)
                put(to, 2 * HEAD_DIM * (head + 1) + HEAD_DIM, g_ref, lane, HEAD_DIM)

    def push(tile, lanes, sem, to_grp, to_sp):
        pltpu.make_async_remote_copy(
            src_ref=send.at[tile, to_grp * n_sp + to_sp, :, lanes],
            dst_ref=recv.at[tile, me, :, lanes],
            send_sem=send_sem.at[sem],
            recv_sem=recv_sem.at[sem],
            device_id={"grp": to_grp, "sp": to_sp},
            device_id_type=MESH,
        ).start()

    half = n_grp // 2

    def scatter(tile, lane, wide, sem):
        @pl.loop(0, peers)
        def _(hop):
            to_grp = lax.rem(my_grp + half + hop, n_grp)
            to_sp = lax.rem(my_sp + hop // n_grp, n_sp)

            @pl.when((to_grp != my_grp) | (to_sp != my_sp))
            def _():
                push(tile, pl.ds(lane, wide), sem, to_grp, to_sp)

    def landed(tile, lane, wide, sem):
        block = recv.at[tile, pl.ds(0, peers - 1), :, pl.ds(lane, wide)]
        pltpu.make_async_copy(block, block, recv_sem.at[sem]).wait()

    def own_block(tile):
        return pltpu.make_async_copy(send.at[tile, me], recv.at[tile, me], own_sem.at[tile])

    pair = 2 * HEAD_DIM
    takes_last = sum(((my_grp == grp).astype(jnp.int32) for grp in full_grps), jnp.int32(0)) > 0

    pack(last)
    pl.semaphore_wait(barrier, peers - 1)
    if len(full_grps) == n_grp:
        scatter(last, 0, row_wide, last)
    else:

        @pl.loop(0, n_sp)
        def _(hop):
            for to_grp in full_grps:

                @pl.when((my_grp != to_grp) | (hop > 0))
                def _():
                    push(last, pl.ds(0, row_wide), last, to_grp, lax.rem(my_sp + hop, n_sp))

    for tile in range(last - 1, 0, -1):
        pack(tile)
        scatter(tile, 0, pair, tile)
        scatter(tile, pair, row_wide - pair, tiles + heads + tile)
    pack(0)
    scatter(0, 0, pair, 0)
    for head in range(heads):
        scatter(0, (head + 1) * pair, pair, tiles + head)
    for tile in range(last):
        own_block(tile).start()

    @pl.when(takes_last)
    def _():
        own_block(last).start()

    @pl.when(jnp.logical_not(takes_last))
    def _():
        recv[last] = jnp.zeros(recv.shape[1:], BF16)

    d_acc[...] = jnp.zeros_like(d_acc)
    to_row = row_iota(tile_tok, 1)
    out_rows = n_grp * STEP
    of_row = (
        (lax.rem(to_row, n_grp) * n_sp + to_row // out_rows) * STEP + lax.rem(to_row, out_rows) // n_grp
    )
    order[...] = (of_row == lane_iota(1, tile_tok)).astype(F32).astype(BF16)

    def go_home(here, out, tile, lane, sends, recvs, own):
        wide = here.shape[-1]
        there = out.at[pl.ds(tile * out_rows, out_rows), pl.ds(pl.multiple_of(lane, HEAD_DIM), wide)]

        @pl.loop(1, n_sp)
        def _(hop):
            to_sp = lax.rem(my_sp + hop, n_sp)
            pltpu.make_async_remote_copy(
                src_ref=here.at[to_sp],
                dst_ref=there,
                send_sem=sends,
                recv_sem=recvs,
                device_id={"grp": my_grp, "sp": to_sp},
                device_id_type=MESH,
            ).start()

        pltpu.make_async_copy(here.at[my_sp], there, own).start()

    def kv_home(tile):
        shape = (n_sp, out_rows, HEAD_DIM)
        d_key = (d_acc[tile, :, :HEAD_DIM] * factor).astype(BF16)
        home_k[tile] = dot_nn(order[...], d_key).astype(BF16).reshape(shape)
        lane = my_sp * HEAD_DIM
        go_home(home_k.at[tile], dk_ref, tile, lane, hk_send.at[tile], hk_recv.at[tile], hk_own.at[tile])
        d_val = d_acc[tile, :, HEAD_DIM:].astype(BF16)
        home_v[tile] = dot_nn(order[...], d_val).astype(BF16).reshape(shape)
        go_home(home_v.at[tile], dv_ref, tile, lane, hv_send.at[tile], hv_recv.at[tile], hv_own.at[tile])

    halo_row = row_iota(halo_tok, 1)
    halo_from = (halo_row // halo) * STEP + STEP - halo + lax.rem(halo_row, halo)
    cut = (halo_from == lane_iota(1, tile_tok)).astype(F32).astype(BF16)
    row = row_iota(tile_tok, 1)
    halo_lane = lane_iota(1, halo_tok)
    paste = (
        row == (halo_lane // halo) * STEP + STEP - halo + lax.rem(halo_lane, halo)
    ).astype(F32)

    @pl.when(takes_last)
    def _():
        own_block(last).wait()
        landed(last, 0, row_wide, last)

    for tile in range(last, -1, -1):
        lane = lane_iota(1, tile_tok)
        q_block = tile * STEP + lax.rem(lane, STEP)
        q_pos = q_block * peers + lane // STEP
        place = q_block.astype(F32)
        member = (
            (group == my_grp.astype(F32))
            & (length > 0.0)
            & (offset <= place)
            & (place < offset + length)
        )
        first = jnp.sum(jnp.where(member, offset * peers, 0.0), axis=0, keepdims=True)
        occupied = jnp.sum(jnp.where(member, 1.0, 0.0), axis=0, keepdims=True) > 0.0
        first = jnp.where(occupied, first, q_pos.astype(F32)).astype(jnp.int32)
        k_pos = (tile * STEP + lax.rem(row, STEP)) * peers + row // STEP
        bias[...] = jnp.where((k_pos <= q_pos) & (k_pos >= first), 0.0, NEG_FILL)
        if tile > 0:
            if tile < last:
                landed(tile, pair, row_wide - pair, tiles + heads + tile)
            own_block(tile - 1).wait()
            landed(tile - 1, 0, pair, tile - 1)
            halo_pos = (tile * STEP - halo + lax.rem(halo_row, halo)) * peers + halo_row // halo
            halo_bias[...] = jnp.where(halo_pos >= first, 0.0, NEG_FILL)
            kv_before = recv[tile - 1, :, :, : 2 * HEAD_DIM].reshape(tile_tok, 2 * HEAD_DIM)
            kv_cut = dot_nn(cut, kv_before)
            halo_kv[...] = kv_cut.astype(BF16)
            halo_turned[...] = kv_cut[:, :HEAD_DIM].T.astype(BF16)
            halo_acc[...] = jnp.zeros_like(halo_acc)

        k_turned[...] = (
            recv[tile, :, :, :HEAD_DIM].reshape(tile_tok, HEAD_DIM).astype(F32).T.astype(BF16)
        )

        @pl.loop(0, heads)
        def _(head):
            if tile == 0:
                landed(0, pair, pair, tiles + head)

            at = pl.multiple_of(head * HEAD_DIM, HEAD_DIM)
            q_at = pl.multiple_of((head + 1) * pair, HEAD_DIM)
            g_at = pl.multiple_of((head + 1) * pair + HEAD_DIM, HEAD_DIM)
            q_head = recv[tile, :, :, pl.ds(q_at, HEAD_DIM)].reshape(tile_tok, HEAD_DIM)
            g_head = recv[tile, :, :, pl.ds(g_at, HEAD_DIM)].reshape(tile_tok, HEAD_DIM)
            keys = [recv[tile, :, :, :HEAD_DIM].reshape(tile_tok, HEAD_DIM)]
            vals = [recv[tile, :, :, HEAD_DIM : 2 * HEAD_DIM].reshape(tile_tok, HEAD_DIM)]
            masks = [bias]
            turned = [k_turned]
            if tile > 0:
                keys.append(halo_kv[:, :HEAD_DIM])
                vals.append(halo_kv[:, HEAD_DIM:])
                masks.append(halo_bias)
                turned.append(halo_turned)
            logits = [dot_nt(key, q_head) * factor + mask[...] for key, mask in zip(keys, masks)]
            high = jnp.max(logits[0], axis=0, keepdims=True)
            for part in logits[1:]:
                high = jnp.maximum(high, jnp.max(part, axis=0, keepdims=True))
            probs = [jnp.exp(part - high) for part in logits]
            mass = sum(jnp.sum(part, axis=0, keepdims=True) for part in probs)
            scale = 1.0 / mass
            probs = [part * scale for part in probs]
            d_probs = [dot_nt(val, g_head) for val in vals]
            delta = sum(
                jnp.sum(part * d_part, axis=0, keepdims=True) for part, d_part in zip(probs, d_probs)
            )
            dq_turned = jnp.zeros((HEAD_DIM, tile_tok), F32)
            for n in range(len(keys)):
                d_logits = (probs[n] * (d_probs[n] - delta)).astype(BF16)
                d_key = dot_nn(d_logits, q_head)
                d_val = dot_nn(probs[n].astype(BF16), g_head)
                if n == 0:
                    d_acc[tile, :, :HEAD_DIM] += d_key
                    d_acc[tile, :, HEAD_DIM:] += d_val
                else:
                    halo_acc[:, :HEAD_DIM] += d_key
                    halo_acc[:, HEAD_DIM:] += d_val
                dq_turned += dot_nn(turned[n][...], d_logits)
            dq_head = dot_nt(order[...], (dq_turned * factor).astype(BF16)).astype(BF16)
            lanes = pl.ds(at, HEAD_DIM)
            home_q[tile, :, :, lanes] = dq_head.reshape(n_sp, out_rows, HEAD_DIM)
            if tile == 0:
                go_home(
                    home_q.at[0, :, :, lanes],
                    dq_ref,
                    0,
                    my_sp * q_wide + head * HEAD_DIM,
                    hq_send.at[last + head],
                    hq_recv.at[last + head],
                    hq_own.at[last + head],
                )

        if tile > 0:
            go_home(
                home_q.at[tile],
                dq_ref,
                tile,
                my_sp * q_wide,
                hq_send.at[tile - 1],
                hq_recv.at[tile - 1],
                hq_own.at[tile - 1],
            )
        kv_home(tile)
        if tile > 0:
            d_acc[tile - 1] += lax.dot_general(
                paste,
                halo_acc[...],
                (((1,), (0,)), ((), ())),
                precision=lax.Precision.HIGHEST,
                preferred_element_type=F32,
            )

    def settle(block, sem):
        pltpu.make_async_copy(block, block, sem).wait()

    def settle_home(here, sends, recvs, own):
        away = here.at[pl.ds(0, n_sp - 1)]
        settle(here.at[0], own)
        settle(away, sends)
        settle(away, recvs)

    def settle_sent(tile, lane, wide, count, sem):
        settle(send.at[tile, pl.ds(0, count), :, pl.ds(lane, wide)], send_sem.at[sem])

    for tile in range(tiles):
        settle_home(home_k.at[tile], hk_send.at[tile], hk_recv.at[tile], hk_own.at[tile])
        settle_home(home_v.at[tile], hv_send.at[tile], hv_recv.at[tile], hv_own.at[tile])
    for n in range(last):
        settle_home(home_q.at[n + 1], hq_send.at[n], hq_recv.at[n], hq_own.at[n])
    for head in range(heads):
        n = last + head
        settle_home(home_q.at[0, :, :, pl.ds(0, HEAD_DIM)], hq_send.at[n], hq_recv.at[n], hq_own.at[n])
        settle_sent(0, 0, pair, peers - 1, tiles + head)
    settle_sent(0, 0, pair, peers - 1, 0)
    for tile in range(1, last):
        settle_sent(tile, 0, pair, peers - 1, tile)
        settle_sent(tile, pair, row_wide - pair, peers - 1, tiles + heads + tile)

    @pl.when(takes_last)
    def _():
        settle_sent(last, 0, row_wide, len(full_grps) * n_sp - 1, last)

    if len(full_grps) < n_grp:

        @pl.when(jnp.logical_not(takes_last))
        def _():
            settle_sent(last, 0, row_wide, len(full_grps) * n_sp, last)


def result_kernel(*refs):
    sources, results, held = refs[:3], refs[3:6], refs[6:9]
    load_sem, store_sem = refs[9:]
    rows = held[0].shape[0]
    cuts = [(0, pl.ds(n * rows // 4, rows // 4)) for n in range(4)] + [(1, pl.ds(0, rows)), (2, pl.ds(0, rows))]
    loads = [
        pltpu.make_async_copy(sources[n].at[cut], held[n].at[cut], load_sem.at[i])
        for i, (n, cut) in enumerate(cuts)
    ]
    stores = [
        pltpu.make_async_copy(held[n].at[cut], results[n].at[cut], store_sem.at[i])
        for i, (n, cut) in enumerate(cuts)
    ]
    for load in loads:
        load.start()
    for load, store in zip(loads, stores):
        load.wait()
        store.start()
    for store in stores:
        store.wait()


def on_device_fused(q_src, k_src, v_src, grad_src, doc_lengths, doc_groups, doc_offsets):
    n_grp = lax.axis_size("grp")
    n_sp = lax.axis_size("sp")
    units = q_src.shape[0]
    slots = doc_lengths.shape[0]
    cap = slots // n_grp
    tiles = cap // STEP
    peers = n_grp * n_sp
    q_all = q_src.shape[-1]
    kv_all = k_src.shape[-1]
    q_wide = q_all // n_sp
    heads = q_wide // HEAD_DIM
    row_wide = 2 * HEAD_DIM * (heads + 1)
    tile_tok = peers * STEP
    halo_tok = peers * (MAXDOC - 1)
    out_rows = n_grp * STEP
    rows = cap * n_grp
    shapes = (
        jax.ShapeDtypeStruct((rows, q_all), BF16),
        jax.ShapeDtypeStruct((rows, kv_all), BF16),
        jax.ShapeDtypeStruct((rows, kv_all), BF16),
    )
    vmem = pl.BlockSpec(memory_space=pltpu.VMEM)
    hbm = pl.BlockSpec(memory_space=pl.ANY)
    dma = pltpu.SemaphoreType.DMA

    def run(full_grps, number):
        return pl.pallas_call(
            lambda *refs: fused_kernel(n_grp, n_sp, tiles, full_grps, *refs),
            out_shape=shapes,
            in_specs=[vmem] * 7,
            out_specs=(hbm,) * 3,
            scratch_shapes=[
                pltpu.VMEM((tiles, peers, STEP, row_wide), BF16),
                pltpu.VMEM((tiles, peers, STEP, row_wide), BF16),
                pltpu.VMEM((tiles, n_sp, out_rows, q_wide), BF16),
                pltpu.VMEM((tiles, n_sp, out_rows, HEAD_DIM), BF16),
                pltpu.VMEM((tiles, n_sp, out_rows, HEAD_DIM), BF16),
                pltpu.VMEM((tile_tok, tile_tok), BF16),
                pltpu.VMEM((tile_tok, tile_tok), F32),
                pltpu.VMEM((halo_tok, tile_tok), F32),
                pltpu.VMEM((halo_tok, 2 * HEAD_DIM), BF16),
                pltpu.VMEM((HEAD_DIM, tile_tok), BF16),
                pltpu.VMEM((HEAD_DIM, halo_tok), BF16),
                pltpu.VMEM((tiles, tile_tok, 2 * HEAD_DIM), F32),
                pltpu.VMEM((halo_tok, 2 * HEAD_DIM), F32),
                dma((2 * tiles + heads,)),
                dma((2 * tiles + heads,)),
                dma((tiles,)),
                dma((tiles - 1 + heads,)),
                dma((tiles - 1 + heads,)),
                dma((tiles - 1 + heads,)),
            ]
            + [dma((tiles,))] * 6,
            compiler_params=pltpu.CompilerParams(
                collective_id=number, has_side_effects=True, vmem_limit_bytes=56 * 1024 * 1024
            ),
        )(
            q_src.reshape(units, q_all),
            k_src.reshape(units, kv_all),
            v_src.reshape(units, kv_all),
            grad_src.reshape(units, q_all),
            doc_lengths.reshape(1, slots),
            doc_groups.reshape(1, slots),
            doc_offsets.reshape(1, slots),
        )

    half = n_grp // 2
    everyone = tuple(range(n_grp))
    choices = [everyone] + [(low, high) for low in everyone[:half] for high in everyone[half:]]
    of_group = doc_groups[None, :] == jnp.arange(n_grp, dtype=jnp.int32)[:, None]
    loads = jnp.sum(jnp.where(of_group, doc_lengths[None, :], 0), axis=1)
    large = loads > cap - STEP
    sides = large.astype(jnp.int32).reshape(2, half)
    single = jnp.all(jnp.sum(sides, axis=1) <= 1)
    picked = jnp.sum(sides * jnp.arange(half, dtype=jnp.int32)[None, :], axis=1)
    choice = jnp.where(single, 1 + picked[0] * half + picked[1], 0)
    passed = lax.switch(
        choice, [lambda n=n, chosen=chosen: run(chosen, n) for n, chosen in enumerate(choices)]
    )
    dq, dk, dv = pl.pallas_call(
        result_kernel,
        out_shape=shapes,
        in_specs=[hbm] * 3,
        out_specs=(hbm,) * 3,
        scratch_shapes=[pltpu.VMEM(shape.shape, BF16) for shape in shapes] + [dma((6,)), dma((6,))],
        compiler_params=pltpu.CompilerParams(vmem_limit_bytes=56 * 1024 * 1024),
    )(*passed)
    return (
        dq.reshape(1, rows, 1, q_all),
        dk.reshape(1, rows, 1, kv_all),
        dv.reshape(1, rows, 1, kv_all),
    )


def on_device(q_src, k_src, v_src, grad_src, doc_lengths, doc_groups, doc_offsets):
    n_grp = lax.axis_size("grp")
    cap = doc_lengths.shape[0] // n_grp
    fits = lax.axis_size("sp") == KV_HEADS and cap % STEP == 0 and cap > STEP and n_grp % 2 == 0
    chosen = on_device_fused if fits else on_device_wide
    return chosen(q_src, k_src, v_src, grad_src, doc_lengths, doc_groups, doc_offsets)


def solution(mesh):
    placed = (
        P(None, "grp", "sp", None),
        P(None, "grp", "sp", None),
        P(None, "grp", "sp", None),
        P(None, "grp", "sp", None),
        P(),
        P(),
        P(),
    )
    return jax.shard_map(
        on_device,
        mesh=mesh,
        in_specs=placed,
        out_specs=(
            P("grp", None, "sp", None),
            P("grp", None, "sp", None),
            P("grp", None, "sp", None),
        ),
        check_vma=False,
    )
```

```python
import math

import jax
import jax.numpy as jnp
from jax import lax
from jax.experimental import pallas as pl
from jax.experimental.pallas import tpu as pltpu
from jax.sharding import PartitionSpec as P

HEADS = 32
KV_HEADS = 8
HEAD_DIM = 128


NEG_FILL = -1e30


def unchanged(passed):
    return passed


def collapse(array):
    rounded = lax.optimization_barrier(array)
    return jnp.sum(rounded.astype(jnp.float32), axis=2)


def pair_fold(low_part, high_part):
    return lax.optimization_barrier(
        (low_part.astype(jnp.float32) + high_part.astype(jnp.float32)).astype(jnp.bfloat16)
    )


def halves_total(array):
    half = array.shape[2] // 2
    return collapse(pair_fold(array[:, :, :half], array[:, :, half:]))


def attend(q_heads, k_heads, v_heads, g_heads, first_tok):
    tokens_here, kv_local, q_per_kv, head_dim = q_heads.shape
    span_len = math.gcd(tokens_here, 512)
    blocks = tokens_here // span_len
    factor = head_dim ** (-0.5)
    lane_pos = jnp.arange(span_len, dtype=jnp.int32)
    block_low = jnp.min(first_tok.reshape(blocks, span_len), axis=1)
    heads_shape = (kv_local, q_per_kv, span_len)

    def cut_block(array, index):
        return lax.dynamic_slice_in_dim(array, index * span_len, span_len, 0)

    def pair_logits(q_block, first_q, q_index, k_index):
        k_block = cut_block(k_heads, k_index)
        logits = (
            jnp.einsum("qjih,kjh->jiqk", q_block, k_block, preferred_element_type=jnp.float32)
            * factor
        )
        q_pos = q_index * span_len + lane_pos
        k_pos = k_index * span_len + lane_pos
        allowed = (k_pos[None, :] <= q_pos[:, None]) & (k_pos[None, :] >= first_q[:, None])
        return (logits, allowed)

    def is_live(q_index, k_index):
        return block_low[q_index] <= k_index * span_len + span_len - 1

    def row_norm(q_index):
        q_block = cut_block(q_heads, q_index)
        first_q = cut_block(first_tok, q_index)

        def visit_key(k_index, running):

            def update(running):
                row_high, row_mass = running
                logits, allowed = pair_logits(q_block, first_q, q_index, k_index)
                logits = jnp.where(allowed, logits, NEG_FILL)
                new_high = jnp.maximum(row_high, jnp.max(logits, axis=-1))
                row_mass = row_mass * jnp.exp(row_high - new_high) + jnp.sum(
                    jnp.where(allowed, jnp.exp(logits - new_high[..., None]), 0.0), axis=-1
                )
                return (new_high, row_mass)

            return lax.cond(is_live(q_index, k_index), update, unchanged, running)

        initial = (
            jnp.full(heads_shape, NEG_FILL, jnp.float32),
            jnp.zeros(heads_shape, jnp.float32),
        )
        row_high, row_mass = lax.fori_loop(0, q_index + 1, visit_key, initial)
        return row_high + jnp.log(row_mass)

    log_norm = lax.map(row_norm, jnp.arange(blocks, dtype=jnp.int32))

    def row_delta(q_index):
        q_block = cut_block(q_heads, q_index)
        first_q = cut_block(first_tok, q_index)
        norm_row = log_norm[q_index]

        def visit_key(k_index, acc_out):

            def update(acc_out):
                logits, allowed = pair_logits(q_block, first_q, q_index, k_index)
                weights = jnp.where(allowed, jnp.exp(logits - norm_row[..., None]), 0.0).astype(
                    jnp.bfloat16
                )
                v_block = cut_block(v_heads, k_index)
                return acc_out + jnp.einsum(
                    "jiqk,kjh->jiqh", weights, v_block, preferred_element_type=jnp.float32
                )

            return lax.cond(is_live(q_index, k_index), update, unchanged, acc_out)

        acc_out = lax.fori_loop(
            0, q_index + 1, visit_key, jnp.zeros(heads_shape + (head_dim,), jnp.float32)
        )
        g_block = cut_block(g_heads, q_index)
        return jnp.einsum("jiqh,qjih->jiq", acc_out, g_block, preferred_element_type=jnp.float32)

    delta_all = lax.map(row_delta, jnp.arange(blocks, dtype=jnp.int32))

    def back_row(q_index, carried):
        grad_q, grad_k, grad_v = carried
        q_block = cut_block(q_heads, q_index)
        g_block = cut_block(g_heads, q_index)
        first_q = cut_block(first_tok, q_index)
        norm_row = log_norm[q_index]
        delta_row = delta_all[q_index]

        def visit_key(k_index, inner):

            def update(inner):
                q_acc, grad_k, grad_v = inner
                logits, allowed = pair_logits(q_block, first_q, q_index, k_index)
                probs = jnp.where(allowed, jnp.exp(logits - norm_row[..., None]), 0.0)
                probs_low = probs.astype(jnp.bfloat16)
                k_block = cut_block(k_heads, k_index)
                v_block = cut_block(v_heads, k_index)
                d_probs = jnp.einsum(
                    "qjih,kjh->jiqk", g_block, v_block, preferred_element_type=jnp.float32
                )
                d_logits = (probs * (d_probs - delta_row[..., None])).astype(jnp.bfloat16)
                q_acc = q_acc + jnp.einsum(
                    "jiqk,kjh->qjih", d_logits, k_block, preferred_element_type=jnp.float32
                )
                k_part = jnp.einsum(
                    "jiqk,qjih->kjih", d_logits, q_block, preferred_element_type=jnp.float32
                )
                v_part = jnp.einsum(
                    "jiqk,qjih->kjih", probs_low, g_block, preferred_element_type=jnp.float32
                )
                at_row = k_index * span_len
                grad_k = lax.dynamic_update_slice_in_dim(
                    grad_k, cut_block(grad_k, k_index) + k_part, at_row, 0
                )
                grad_v = lax.dynamic_update_slice_in_dim(
                    grad_v, cut_block(grad_v, k_index) + v_part, at_row, 0
                )
                return (q_acc, grad_k, grad_v)

            return lax.cond(is_live(q_index, k_index), update, unchanged, inner)

        q_start = jnp.zeros((span_len, kv_local, q_per_kv, head_dim), jnp.float32)
        q_acc, grad_k, grad_v = lax.fori_loop(0, q_index + 1, visit_key, (q_start, grad_k, grad_v))
        grad_q = lax.dynamic_update_slice_in_dim(grad_q, q_acc, q_index * span_len, 0)
        return (grad_q, grad_k, grad_v)

    empty = jnp.zeros((tokens_here, kv_local, q_per_kv, head_dim), jnp.float32)
    grad_q, grad_k, grad_v = lax.fori_loop(0, blocks, back_row, (empty, empty, empty))
    return (grad_q * factor, grad_k * factor, grad_v)


def on_device_wide(q_src, k_src, v_src, grad_src, doc_lengths, doc_groups, doc_offsets):
    grp_count = lax.axis_size("grp")
    sp_count = lax.axis_size("sp")
    unit_count = q_src.shape[0]
    slot_count = doc_lengths.shape[0]
    group_cap = slot_count // grp_count
    row_count = group_cap * grp_count
    unit_tok = grp_count * sp_count
    group_tok = row_count * sp_count
    head_dim = HEAD_DIM
    copies = max(1, sp_count // KV_HEADS)
    kv_local = max(1, KV_HEADS // sp_count)
    q_local = HEADS // sp_count
    q_per_kv = q_local // kv_local
    unit_ids = jnp.arange(unit_count, dtype=jnp.int32)
    starts = jnp.cumsum(doc_lengths) - doc_lengths
    inside = (
        (unit_ids[:, None] >= starts[None, :])
        & (unit_ids[:, None] < (starts + doc_lengths)[None, :])
    ).astype(jnp.int32)
    group_of = jnp.sum(inside * doc_groups[None, :], axis=1)
    place_of = jnp.sum(
        inside * (doc_offsets[None, :] + unit_ids[:, None] - starts[None, :]), axis=1
    )
    slot_of = group_of * group_cap + place_of
    slot_ids = jnp.arange(row_count, dtype=jnp.int32).reshape(grp_count, group_cap).T.reshape(-1)
    matches = (slot_of[None, :] == slot_ids[:, None]).astype(jnp.int32)
    source = jnp.sum(matches * unit_ids[None, :], axis=1)
    filled = jnp.sum(matches, axis=1) > 0

    def pack_rows(array):
        flat = array.reshape(unit_count, array.shape[-1])
        picked = jnp.take(flat, source, axis=0)
        picked = jnp.where(filled[:, None], picked, jnp.zeros_like(picked))
        return picked.reshape(group_cap, grp_count, array.shape[-1])

    arrived = (
        lax.all_to_all(pack_rows(q_src), "grp", split_axis=1, concat_axis=1, tiled=True),
        lax.all_to_all(pack_rows(k_src), "grp", split_axis=1, concat_axis=1, tiled=True),
        lax.all_to_all(pack_rows(v_src), "grp", split_axis=1, concat_axis=1, tiled=True),
        lax.all_to_all(pack_rows(grad_src), "grp", split_axis=1, concat_axis=1, tiled=True),
    )
    q_rows = arrived[0].reshape(row_count, 1, HEADS, head_dim)
    k_rows = arrived[1].reshape(row_count, KV_HEADS, head_dim)
    v_rows = arrived[2].reshape(row_count, KV_HEADS, head_dim)
    g_rows = arrived[3].reshape(row_count, 1, HEADS, head_dim)
    my_group = lax.axis_index("grp")
    unit_place = jnp.arange(group_cap, dtype=jnp.int32)
    member = (
        (doc_groups[None, :] == my_group)
        & (doc_lengths[None, :] > 0)
        & (doc_offsets[None, :] <= unit_place[:, None])
        & (unit_place[:, None] < (doc_offsets + doc_lengths)[None, :])
    ).astype(jnp.int32)
    first_unit = jnp.sum(member * doc_offsets[None, :], axis=1)
    occupied = jnp.sum(member, axis=1) > 0
    token_ids = jnp.arange(group_tok, dtype=jnp.int32)
    first_tok = jnp.where(
        jnp.repeat(occupied, unit_tok), jnp.repeat(first_unit * unit_tok, unit_tok), token_ids
    )
    k_wide = jnp.repeat(k_rows, copies, axis=1).reshape(row_count, 1, KV_HEADS * copies, head_dim)
    v_wide = jnp.repeat(v_rows, copies, axis=1).reshape(row_count, 1, KV_HEADS * copies, head_dim)
    q_back, g_back, k_back, v_back = (
        lax.all_to_all(q_rows, "sp", split_axis=2, concat_axis=1, tiled=True),
        lax.all_to_all(g_rows, "sp", split_axis=2, concat_axis=1, tiled=True),
        lax.all_to_all(k_wide, "sp", split_axis=2, concat_axis=1, tiled=True),
        lax.all_to_all(v_wide, "sp", split_axis=2, concat_axis=1, tiled=True),
    )
    k_heads = k_back.reshape(group_tok, kv_local, head_dim)
    v_heads = v_back.reshape(group_tok, kv_local, head_dim)
    q_heads = q_back.reshape(group_tok, kv_local, q_per_kv, head_dim)
    g_heads = g_back.reshape(group_tok, kv_local, q_per_kv, head_dim)
    grad_q, grad_k, grad_v = attend(q_heads, k_heads, v_heads, g_heads, first_tok)
    q_low = grad_q.astype(jnp.bfloat16).reshape(row_count, sp_count, q_local, head_dim)
    k_low = grad_k.astype(jnp.bfloat16)
    v_low = grad_v.astype(jnp.bfloat16)
    q_home, k_home, v_home = (
        lax.all_to_all(q_low, "sp", split_axis=1, concat_axis=2, tiled=True),
        lax.all_to_all(
            k_low.reshape(row_count, sp_count, q_local, head_dim),
            "sp",
            split_axis=1,
            concat_axis=2,
            tiled=True,
        ),
        lax.all_to_all(
            v_low.reshape(row_count, sp_count, q_local, head_dim),
            "sp",
            split_axis=1,
            concat_axis=2,
            tiled=True,
        ),
    )
    k_sum = halves_total(k_home.reshape(row_count, KV_HEADS, HEADS // KV_HEADS, head_dim))
    v_sum = halves_total(v_home.reshape(row_count, KV_HEADS, HEADS // KV_HEADS, head_dim))
    dk_out = k_sum.astype(jnp.bfloat16).reshape(1, row_count, 1, KV_HEADS * head_dim)
    dv_out = v_sum.astype(jnp.bfloat16).reshape(1, row_count, 1, KV_HEADS * head_dim)
    dq_out = q_home.reshape(1, row_count, 1, HEADS * head_dim)
    return (dq_out, dk_out, dv_out)


MESH = pl.DeviceIdType.MESH
STEP = 16
MAXDOC = 5
F32 = jnp.float32
BF16 = jnp.bfloat16


def dot_nt(left, right):
    return lax.dot_general(left, right, (((1,), (1,)), ((), ())), preferred_element_type=F32)


def dot_nn(left, right):
    return lax.dot_general(left, right, (((1,), (0,)), ((), ())), preferred_element_type=F32)


def lane_iota(rows, lanes):
    return lax.broadcasted_iota(jnp.int32, (rows, lanes), 1)


def row_iota(rows, lanes):
    return lax.broadcasted_iota(jnp.int32, (rows, lanes), 0)


def fused_kernel(
    n_grp,
    n_sp,
    tiles,
    full_grps,
    q_ref,
    k_ref,
    v_ref,
    g_ref,
    len_ref,
    grp_ref,
    off_ref,
    dq_ref,
    dk_ref,
    dv_ref,
    send,
    recv,
    home_q,
    home_k,
    home_v,
    order,
    bias,
    halo_bias,
    halo_kv,
    k_turned,
    halo_turned,
    d_acc,
    halo_acc,
    send_sem,
    recv_sem,
    own_sem,
    hq_send,
    hq_recv,
    hq_own,
    hk_send,
    hk_recv,
    hk_own,
    hv_send,
    hv_recv,
    hv_own,
):
    my_grp = lax.axis_index("grp")
    my_sp = lax.axis_index("sp")
    peers = n_grp * n_sp
    me = my_grp * n_sp + my_sp
    units = q_ref.shape[0]
    q_wide = q_ref.shape[1] // n_sp
    heads = q_wide // HEAD_DIM
    cap = tiles * STEP
    tile_tok = peers * STEP
    halo = MAXDOC - 1
    halo_tok = peers * halo
    factor = HEAD_DIM ** (-0.5)
    row_wide = 2 * HEAD_DIM * (heads + 1)
    last = tiles - 1
    kv_lanes = pl.ds(0, 2 * HEAD_DIM)

    barrier = pltpu.get_barrier_semaphore()

    @pl.loop(1, peers)
    def _(hop):
        there = {
            "grp": lax.rem(my_grp + hop // n_sp, n_grp),
            "sp": lax.rem(my_sp + lax.rem(hop, n_sp), n_sp),
        }
        pl.semaphore_signal(barrier, inc=1, device_id=there, device_id_type=MESH)

    slots = len_ref.shape[1]
    which = row_iota(8, slots)
    tables = jnp.where(
        which == 0, len_ref[...], jnp.where(which == 1, grp_ref[...], jnp.where(which == 2, off_ref[...], 0))
    )
    tables = tables.astype(F32).astype(BF16)
    down, across = row_iota(slots, slots), lane_iota(slots, slots)
    columns = dot_nt((down == across).astype(F32).astype(BF16), tables)
    length, group, offset = columns[:, 0:1], columns[:, 1:2], columns[:, 2:3]
    start = dot_nt((across < down).astype(F32).astype(BF16), tables)[:, 0:1]
    unit = lane_iota(1, units).astype(F32)
    inside = (unit >= start) & (unit < start + length)
    slot_of = unit + jnp.sum(
        jnp.where(inside, group * cap + offset - start, 0.0), axis=0, keepdims=True
    )

    def pack(tile):
        row = row_iota(n_grp * STEP, 1)
        slot = (row // STEP) * cap + tile * STEP + lax.rem(row, STEP)
        hot = (slot.astype(F32) == slot_of).astype(F32).astype(BF16)

        def put(to, at, ref, lane, wide):
            part = dot_nn(hot, ref[:, lane : lane + wide]).astype(BF16).reshape(n_grp, STEP, wide)
            for grp in range(n_grp):
                send[tile, grp * n_sp + to, :, at : at + wide] = part[grp]

        for to in range(n_sp):
            put(to, 0, k_ref, to * HEAD_DIM, HEAD_DIM)
            put(to, HEAD_DIM, v_ref, to * HEAD_DIM, HEAD_DIM)
            for head in range(heads):
                lane = to * q_wide + head * HEAD_DIM
                put(to, 2 * HEAD_DIM * (head + 1), q_ref, lane, HEAD_DIM)
                put(to, 2 * HEAD_DIM * (head + 1) + HEAD_DIM, g_ref, lane, HEAD_DIM)

    def push(tile, lanes, sem, to_grp, to_sp):
        pltpu.make_async_remote_copy(
            src_ref=send.at[tile, to_grp * n_sp + to_sp, :, lanes],
            dst_ref=recv.at[tile, me, :, lanes],
            send_sem=send_sem.at[sem],
            recv_sem=recv_sem.at[sem],
            device_id={"grp": to_grp, "sp": to_sp},
            device_id_type=MESH,
        ).start()

    half = n_grp // 2

    def scatter(tile, lane, wide, sem):
        for turn in [half] + [t for t in range(1, n_grp) if t != half] + [0]:

            @pl.loop(1 if turn == 0 else 0, n_sp)
            def _(hop):
                to_grp = lax.rem(my_grp + turn, n_grp)
                push(tile, pl.ds(lane, wide), sem, to_grp, lax.rem(my_sp + hop, n_sp))

    def landed(tile, lane, wide, sem):
        block = recv.at[tile, pl.ds(0, peers - 1), :, pl.ds(lane, wide)]
        pltpu.make_async_copy(block, block, recv_sem.at[sem]).wait()

    def own_block(tile):
        return pltpu.make_async_copy(send.at[tile, me], recv.at[tile, me], own_sem.at[tile])

    pair = 2 * HEAD_DIM
    takes_last = sum(((my_grp == grp).astype(jnp.int32) for grp in full_grps), jnp.int32(0)) > 0

    pack(last)
    pl.semaphore_wait(barrier, peers - 1)
    if len(full_grps) == n_grp:
        scatter(last, 0, row_wide, last)
    else:

        @pl.loop(0, n_sp)
        def _(hop):
            for to_grp in full_grps:

                @pl.when((my_grp != to_grp) | (hop > 0))
                def _():
                    push(last, pl.ds(0, row_wide), last, to_grp, lax.rem(my_sp + hop, n_sp))

    for tile in range(last - 1, 0, -1):
        pack(tile)
        scatter(tile, 0, pair, tile)
        scatter(tile, pair, row_wide - pair, tiles + heads + tile)
    pack(0)
    scatter(0, 0, pair, 0)
    for head in range(heads):
        scatter(0, (head + 1) * pair, pair, tiles + head)
    for tile in range(last):
        own_block(tile).start()

    @pl.when(takes_last)
    def _():
        own_block(last).start()

    @pl.when(jnp.logical_not(takes_last))
    def _():
        recv[last] = jnp.zeros(recv.shape[1:], BF16)

    d_acc[...] = jnp.zeros_like(d_acc)
    to_row = row_iota(tile_tok, 1)
    out_rows = n_grp * STEP
    of_row = (
        (lax.rem(to_row, n_grp) * n_sp + to_row // out_rows) * STEP + lax.rem(to_row, out_rows) // n_grp
    )
    order[...] = (of_row == lane_iota(1, tile_tok)).astype(F32).astype(BF16)

    def go_home(here, out, tile, lane, sends, recvs, own):
        wide = here.shape[-1]
        there = out.at[pl.ds(tile * out_rows, out_rows), pl.ds(pl.multiple_of(lane, HEAD_DIM), wide)]

        @pl.loop(1, n_sp)
        def _(hop):
            to_sp = lax.rem(my_sp + hop, n_sp)
            pltpu.make_async_remote_copy(
                src_ref=here.at[to_sp],
                dst_ref=there,
                send_sem=sends,
                recv_sem=recvs,
                device_id={"grp": my_grp, "sp": to_sp},
                device_id_type=MESH,
            ).start()

        pltpu.make_async_copy(here.at[my_sp], there, own).start()

    def kv_home(tile):
        shape = (n_sp, out_rows, HEAD_DIM)
        d_key = (d_acc[tile, :, :HEAD_DIM] * factor).astype(BF16)
        home_k[tile] = dot_nn(order[...], d_key).astype(BF16).reshape(shape)
        lane = my_sp * HEAD_DIM
        go_home(home_k.at[tile], dk_ref, tile, lane, hk_send.at[tile], hk_recv.at[tile], hk_own.at[tile])
        d_val = d_acc[tile, :, HEAD_DIM:].astype(BF16)
        home_v[tile] = dot_nn(order[...], d_val).astype(BF16).reshape(shape)
        go_home(home_v.at[tile], dv_ref, tile, lane, hv_send.at[tile], hv_recv.at[tile], hv_own.at[tile])

    halo_row = row_iota(halo_tok, 1)
    halo_from = (halo_row // halo) * STEP + STEP - halo + lax.rem(halo_row, halo)
    cut = (halo_from == lane_iota(1, tile_tok)).astype(F32).astype(BF16)
    row = row_iota(tile_tok, 1)
    halo_lane = lane_iota(1, halo_tok)
    paste = (
        row == (halo_lane // halo) * STEP + STEP - halo + lax.rem(halo_lane, halo)
    ).astype(F32)

    @pl.when(takes_last)
    def _():
        own_block(last).wait()
        landed(last, 0, row_wide, last)

    for tile in range(last, -1, -1):
        lane = lane_iota(1, tile_tok)
        q_block = tile * STEP + lax.rem(lane, STEP)
        q_pos = q_block * peers + lane // STEP
        place = q_block.astype(F32)
        member = (
            (group == my_grp.astype(F32))
            & (length > 0.0)
            & (offset <= place)
            & (place < offset + length)
        )
        first = jnp.sum(jnp.where(member, offset * peers, 0.0), axis=0, keepdims=True)
        occupied = jnp.sum(jnp.where(member, 1.0, 0.0), axis=0, keepdims=True) > 0.0
        first = jnp.where(occupied, first, q_pos.astype(F32)).astype(jnp.int32)
        k_pos = (tile * STEP + lax.rem(row, STEP)) * peers + row // STEP
        bias[...] = jnp.where((k_pos <= q_pos) & (k_pos >= first), 0.0, NEG_FILL)
        if tile > 0:
            if tile < last:
                landed(tile, pair, row_wide - pair, tiles + heads + tile)
            own_block(tile - 1).wait()
            landed(tile - 1, 0, pair, tile - 1)
            halo_pos = (tile * STEP - halo + lax.rem(halo_row, halo)) * peers + halo_row // halo
            halo_bias[...] = jnp.where(halo_pos >= first, 0.0, NEG_FILL)
            kv_before = recv[tile - 1, :, :, : 2 * HEAD_DIM].reshape(tile_tok, 2 * HEAD_DIM)
            kv_cut = dot_nn(cut, kv_before)
            halo_kv[...] = kv_cut.astype(BF16)
            halo_turned[...] = kv_cut[:, :HEAD_DIM].T.astype(BF16)
            halo_acc[...] = jnp.zeros_like(halo_acc)

        k_turned[...] = (
            recv[tile, :, :, :HEAD_DIM].reshape(tile_tok, HEAD_DIM).astype(F32).T.astype(BF16)
        )

        @pl.loop(0, heads)
        def _(head):
            if tile == 0:
                landed(0, pair, pair, tiles + head)

            at = pl.multiple_of(head * HEAD_DIM, HEAD_DIM)
            q_at = pl.multiple_of((head + 1) * pair, HEAD_DIM)
            g_at = pl.multiple_of((head + 1) * pair + HEAD_DIM, HEAD_DIM)
            q_head = recv[tile, :, :, pl.ds(q_at, HEAD_DIM)].reshape(tile_tok, HEAD_DIM)
            g_head = recv[tile, :, :, pl.ds(g_at, HEAD_DIM)].reshape(tile_tok, HEAD_DIM)
            keys = [recv[tile, :, :, :HEAD_DIM].reshape(tile_tok, HEAD_DIM)]
            vals = [recv[tile, :, :, HEAD_DIM : 2 * HEAD_DIM].reshape(tile_tok, HEAD_DIM)]
            masks = [bias]
            turned = [k_turned]
            if tile > 0:
                keys.append(halo_kv[:, :HEAD_DIM])
                vals.append(halo_kv[:, HEAD_DIM:])
                masks.append(halo_bias)
                turned.append(halo_turned)
            logits = [dot_nt(key, q_head) * factor + mask[...] for key, mask in zip(keys, masks)]
            high = jnp.max(logits[0], axis=0, keepdims=True)
            for part in logits[1:]:
                high = jnp.maximum(high, jnp.max(part, axis=0, keepdims=True))
            probs = [jnp.exp(part - high) for part in logits]
            mass = sum(jnp.sum(part, axis=0, keepdims=True) for part in probs)
            scale = 1.0 / mass
            probs = [part * scale for part in probs]
            d_probs = [dot_nt(val, g_head) for val in vals]
            delta = sum(
                jnp.sum(part * d_part, axis=0, keepdims=True) for part, d_part in zip(probs, d_probs)
            )
            dq_turned = jnp.zeros((HEAD_DIM, tile_tok), F32)
            for n in range(len(keys)):
                d_logits = (probs[n] * (d_probs[n] - delta)).astype(BF16)
                d_key = dot_nn(d_logits, q_head)
                d_val = dot_nn(probs[n].astype(BF16), g_head)
                if n == 0:
                    d_acc[tile, :, :HEAD_DIM] += d_key
                    d_acc[tile, :, HEAD_DIM:] += d_val
                else:
                    halo_acc[:, :HEAD_DIM] += d_key
                    halo_acc[:, HEAD_DIM:] += d_val
                dq_turned += dot_nn(turned[n][...], d_logits)
            dq_head = dot_nt(order[...], (dq_turned * factor).astype(BF16)).astype(BF16)
            lanes = pl.ds(at, HEAD_DIM)
            home_q[tile, :, :, lanes] = dq_head.reshape(n_sp, out_rows, HEAD_DIM)
            if tile == 0:
                go_home(
                    home_q.at[0, :, :, lanes],
                    dq_ref,
                    0,
                    my_sp * q_wide + head * HEAD_DIM,
                    hq_send.at[last + head],
                    hq_recv.at[last + head],
                    hq_own.at[last + head],
                )

        if tile > 0:
            go_home(
                home_q.at[tile],
                dq_ref,
                tile,
                my_sp * q_wide,
                hq_send.at[tile - 1],
                hq_recv.at[tile - 1],
                hq_own.at[tile - 1],
            )
        kv_home(tile)
        if tile > 0:
            d_acc[tile - 1] += lax.dot_general(
                paste,
                halo_acc[...],
                (((1,), (0,)), ((), ())),
                precision=lax.Precision.HIGHEST,
                preferred_element_type=F32,
            )

    def settle(block, sem):
        pltpu.make_async_copy(block, block, sem).wait()

    def settle_home(here, sends, recvs, own):
        away = here.at[pl.ds(0, n_sp - 1)]
        settle(here.at[0], own)
        settle(away, sends)
        settle(away, recvs)

    def settle_sent(tile, lane, wide, count, sem):
        settle(send.at[tile, pl.ds(0, count), :, pl.ds(lane, wide)], send_sem.at[sem])

    for tile in range(tiles):
        settle_home(home_k.at[tile], hk_send.at[tile], hk_recv.at[tile], hk_own.at[tile])
        settle_home(home_v.at[tile], hv_send.at[tile], hv_recv.at[tile], hv_own.at[tile])
    for n in range(last):
        settle_home(home_q.at[n + 1], hq_send.at[n], hq_recv.at[n], hq_own.at[n])
    for head in range(heads):
        n = last + head
        settle_home(home_q.at[0, :, :, pl.ds(0, HEAD_DIM)], hq_send.at[n], hq_recv.at[n], hq_own.at[n])
        settle_sent(0, 0, pair, peers - 1, tiles + head)
    settle_sent(0, 0, pair, peers - 1, 0)
    for tile in range(1, last):
        settle_sent(tile, 0, pair, peers - 1, tile)
        settle_sent(tile, pair, row_wide - pair, peers - 1, tiles + heads + tile)

    @pl.when(takes_last)
    def _():
        settle_sent(last, 0, row_wide, len(full_grps) * n_sp - 1, last)

    if len(full_grps) < n_grp:

        @pl.when(jnp.logical_not(takes_last))
        def _():
            settle_sent(last, 0, row_wide, len(full_grps) * n_sp, last)


def result_kernel(*refs):
    sources, results, held = refs[:3], refs[3:6], refs[6:9]
    load_sem, store_sem = refs[9:]
    rows = held[0].shape[0]
    cuts = [(0, pl.ds(n * rows // 4, rows // 4)) for n in range(4)] + [(1, pl.ds(0, rows)), (2, pl.ds(0, rows))]
    loads = [
        pltpu.make_async_copy(sources[n].at[cut], held[n].at[cut], load_sem.at[i])
        for i, (n, cut) in enumerate(cuts)
    ]
    stores = [
        pltpu.make_async_copy(held[n].at[cut], results[n].at[cut], store_sem.at[i])
        for i, (n, cut) in enumerate(cuts)
    ]
    for load in loads:
        load.start()
    for load, store in zip(loads, stores):
        load.wait()
        store.start()
    for store in stores:
        store.wait()


def on_device_fused(q_src, k_src, v_src, grad_src, doc_lengths, doc_groups, doc_offsets):
    n_grp = lax.axis_size("grp")
    n_sp = lax.axis_size("sp")
    units = q_src.shape[0]
    slots = doc_lengths.shape[0]
    cap = slots // n_grp
    tiles = cap // STEP
    peers = n_grp * n_sp
    q_all = q_src.shape[-1]
    kv_all = k_src.shape[-1]
    q_wide = q_all // n_sp
    heads = q_wide // HEAD_DIM
    row_wide = 2 * HEAD_DIM * (heads + 1)
    tile_tok = peers * STEP
    halo_tok = peers * (MAXDOC - 1)
    out_rows = n_grp * STEP
    rows = cap * n_grp
    shapes = (
        jax.ShapeDtypeStruct((rows, q_all), BF16),
        jax.ShapeDtypeStruct((rows, kv_all), BF16),
        jax.ShapeDtypeStruct((rows, kv_all), BF16),
    )
    vmem = pl.BlockSpec(memory_space=pltpu.VMEM)
    hbm = pl.BlockSpec(memory_space=pl.ANY)
    dma = pltpu.SemaphoreType.DMA

    def run(full_grps, number):
        return pl.pallas_call(
            lambda *refs: fused_kernel(n_grp, n_sp, tiles, full_grps, *refs),
            out_shape=shapes,
            in_specs=[vmem] * 7,
            out_specs=(hbm,) * 3,
            scratch_shapes=[
                pltpu.VMEM((tiles, peers, STEP, row_wide), BF16),
                pltpu.VMEM((tiles, peers, STEP, row_wide), BF16),
                pltpu.VMEM((tiles, n_sp, out_rows, q_wide), BF16),
                pltpu.VMEM((tiles, n_sp, out_rows, HEAD_DIM), BF16),
                pltpu.VMEM((tiles, n_sp, out_rows, HEAD_DIM), BF16),
                pltpu.VMEM((tile_tok, tile_tok), BF16),
                pltpu.VMEM((tile_tok, tile_tok), F32),
                pltpu.VMEM((halo_tok, tile_tok), F32),
                pltpu.VMEM((halo_tok, 2 * HEAD_DIM), BF16),
                pltpu.VMEM((HEAD_DIM, tile_tok), BF16),
                pltpu.VMEM((HEAD_DIM, halo_tok), BF16),
                pltpu.VMEM((tiles, tile_tok, 2 * HEAD_DIM), F32),
                pltpu.VMEM((halo_tok, 2 * HEAD_DIM), F32),
                dma((2 * tiles + heads,)),
                dma((2 * tiles + heads,)),
                dma((tiles,)),
                dma((tiles - 1 + heads,)),
                dma((tiles - 1 + heads,)),
                dma((tiles - 1 + heads,)),
            ]
            + [dma((tiles,))] * 6,
            compiler_params=pltpu.CompilerParams(
                collective_id=number, has_side_effects=True, vmem_limit_bytes=56 * 1024 * 1024
            ),
        )(
            q_src.reshape(units, q_all),
            k_src.reshape(units, kv_all),
            v_src.reshape(units, kv_all),
            grad_src.reshape(units, q_all),
            doc_lengths.reshape(1, slots),
            doc_groups.reshape(1, slots),
            doc_offsets.reshape(1, slots),
        )

    passed = run(tuple(range(n_grp)), 0)
    dq, dk, dv = pl.pallas_call(
        result_kernel,
        out_shape=shapes,
        in_specs=[hbm] * 3,
        out_specs=(hbm,) * 3,
        scratch_shapes=[pltpu.VMEM(shape.shape, BF16) for shape in shapes] + [dma((6,)), dma((6,))],
        compiler_params=pltpu.CompilerParams(vmem_limit_bytes=56 * 1024 * 1024),
    )(*passed)
    return (
        dq.reshape(1, rows, 1, q_all),
        dk.reshape(1, rows, 1, kv_all),
        dv.reshape(1, rows, 1, kv_all),
    )


def on_device(q_src, k_src, v_src, grad_src, doc_lengths, doc_groups, doc_offsets):
    n_grp = lax.axis_size("grp")
    cap = doc_lengths.shape[0] // n_grp
    fits = lax.axis_size("sp") == KV_HEADS and cap % STEP == 0 and cap > STEP and n_grp % 2 == 0
    chosen = on_device_fused if fits else on_device_wide
    return chosen(q_src, k_src, v_src, grad_src, doc_lengths, doc_groups, doc_offsets)


def solution(mesh):
    placed = (
        P(None, "grp", "sp", None),
        P(None, "grp", "sp", None),
        P(None, "grp", "sp", None),
        P(None, "grp", "sp", None),
        P(),
        P(),
        P(),
    )
    return jax.shard_map(
        on_device,
        mesh=mesh,
        in_specs=placed,
        out_specs=(
            P("grp", None, "sp", None),
            P("grp", None, "sp", None),
            P("grp", None, "sp", None),
        ),
        check_vma=False,
    )
```
